256 devices in a mesh: section: 8 (over y, x_lo), expert: 32 (over x_hi, z, core).
Axes of the slice: x: 4 (x_hi: 2, x_lo: 2; x = x_hi * 2 + x_lo), y: 4, z: 8, core: 2. Of those that a mesh axis runs over, the one named last changes fastest.
Arguments:
- tokens: bfloat16 [8, 512, 7168], P('section', 'expert'), may hold values from -6 to 6
- expert_ids: int32 [8, 512, 2], P('section', 'expert'), may hold values from 0 to 3, all different within a row; in each aligned block of 16 rows (0 to 15, 16 to 31, ..., all dimensions but the last counted through in order) at most 12 rows name the same one
- gate_values: float32 [8, 512, 2], P('section', 'expert'), may hold values from 0.3 to 1.5
- w_gate: bfloat16 [8, 7168, 4096], P('section', None, 'expert'), may hold values from -0.0625 to 0.0625
- w_up: bfloat16 [8, 7168, 4096], P('section', None, 'expert'), may hold values from -0.0625 to 0.0625
- w_down: bfloat16 [8, 4096, 7168], P('section', 'expert'), may hold values from -0.1875 to 0.1875
- norm_gain: float32 [8, 7168], P('section'), may hold values from 0.1 to 1.9
- w_dq: bfloat16 [8, 7168, 1536], P('section', 'expert'), may hold values from -0.0625 to 0.0625
- w_dkv: bfloat16 [8, 7168, 576], P('section', 'expert'), may hold values from -0.0625 to 0.0625
- q_gain: float32 [8, 1536], P('section'), may hold values from 0.1 to 1.9
- kv_gain: float32 [8, 512], P('section'), may hold values from 0.1 to 1.9
- w_uq: bfloat16 [8, 1536, 12288], P('section', None, 'expert'), may hold values from -0.15625 to 0.15625
- w_uk: bfloat16 [8, 64, 128, 512], P('section', 'expert'), may hold values from -3 to 3
- w_uv: bfloat16 [8, 64, 512, 128], P('section', 'expert'), may hold values from -0.25 to 0.25
- prefix_cache: bfloat16 [8, 2048, 576], P('section', 'expert'), may hold values from -8 to 8
Outputs:
- attended: bfloat16 [8, 512, 8192], P('section', None, 'expert')
The draws below stay inside these ranges and needn't reach their ends.
Inputs may be any that keep to these rules, and one draw needn't show every extreme that they name: `expert_ids`: A token's 2 experts differ. Among the 16 tokens of one device (aligned blocks of rows) at most 12 entries name one expert, and in every draw some block reaches 12.
All inputs are finite; a program needn't handle non-finite values.
Results may differ from the reference program's by a relative error of at most 0.039.
Values may be sent and summed in bfloat16 or wider, within the bound.
A program may use at most 128 MiB of HBM per device.

```python
import math
import jax
import jax.numpy as jnp
import numpy as np
from jax import lax

D = 7168
FF = 1024
EXPERTS = 4
TOPK = 2
QR = 1536
KVR = 512
ROPE = 64
NOPE = 128
VDIM = 128
TOK_DEV = 16
SRC_CAP = 12
TOKENS = 512
CACHE = 2048
HEADS = 64
SECTIONS = 8
N_EXPERT = 32


def draw_w_uk(key, part):
    key = jax.random.fold_in(key, 11)
    shape = (SECTIONS, HEADS, NOPE, KVR)
    return (jnp.clip(jax.random.normal(key, shape, jnp.float32), -6.0, 6.0) * NOPE ** (-0.5)).astype(jnp.bfloat16)


def draw_prefix_cache(key, part):
    key = jax.random.fold_in(key, 7)
    shape = (SECTIONS, CACHE, KVR + ROPE)
    return jnp.clip(jax.random.normal(key, shape, jnp.float32), -6.0, 6.0).astype(jnp.bfloat16)


def levels(rng, extent, cuts, smallest, high):
    level, own = 1.0, jax.random.fold_in(rng, 6)
    for dim, shards_of in cuts:
        steps = jnp.exp(jax.random.uniform(jax.random.fold_in(own, dim), (shards_of,), jnp.float32, smallest / len(cuts), high / len(cuts)))
        level = level * jnp.repeat(steps, extent[dim] // shards_of).reshape([-1 if axis == dim else 1 for axis in range(len(extent))])
    return level


def routed_block(own_key, own, number, rows, number_of, top, reach, skew):
    ranking = jax.random.permutation(own_key, number_of)
    packed, ordinary = portions_of(number_of, rows * top, reach, skew, True), portions_of(number_of, rows * top, reach, skew, False)
    places = jnp.arange(number_of)

    def named(sizes, rotation):
        used = int((sizes > 0).sum())
        fixed = max(1, used // 4)
        shifted = fixed + (places - fixed + rotation * (used - fixed)) % max(1, number_of - fixed)
        return jnp.zeros((number_of,), jnp.int32).at[ranking[jnp.where(places < fixed, places, shifted)]].set(jnp.asarray(sizes, jnp.int32))

    sizes = jnp.where(number % 4 == 0, named(packed, number // 4), named(ordinary, number - number // 4 - 1))
    mixed = jax.random.permutation(jax.random.fold_in(own, 3), number_of)
    donor, taker = mixed[0:number_of // 2 * 2:2], mixed[1:number_of // 2 * 2:2]
    room = jnp.minimum(sizes[donor] - 1, reach - sizes[taker]) // 2
    room = jnp.where((donor == ranking[0]) | (taker == ranking[0]) | (sizes[taker] == 0), 0, jnp.maximum(room, 0))
    shifted = jax.random.randint(jax.random.fold_in(own, 4), (number_of // 2,), 0, 1 << 20) % (room + 1)
    sizes = sizes.at[donor].add(-shifted).at[taker].add(shifted)
    items = jnp.searchsorted(jnp.cumsum(sizes), jnp.arange(rows * top), side="right").astype(jnp.int32)
    grid = items.reshape(top, rows).T
    grid = grid[jax.random.permutation(jax.random.fold_in(own, 1), rows)]
    rotation = jax.random.randint(jax.random.fold_in(own, 2), (rows, 1), 0, top)
    return jnp.take_along_axis(grid, (jnp.arange(top)[None, :] + rotation) % top, axis=1)


def portions_of(count, total, most, lean, full):
    weights = [(1 << 20) // math.isqrt(rank ** lean) + 1 for rank in range(1, count + 1)]
    largest = most if full else min(most, max(-(-total // count), total * weights[0] // sum(weights)))
    least = 1 if total - largest >= count - 1 else 0
    counts, rest = [largest] + [least] * (count - 1), total - largest - least * (count - 1)
    while rest > 0:
        free = [i for i in range(1, count) if counts[i] < largest] or [i for i in range(1, count) if counts[i] < most]
        pool, left = sum([weights[i] for i in free]), rest
        for i in free:
            extra = min(most - counts[i], max(1, left * weights[i] // pool), rest)
            counts[i] = counts[i] + extra
            rest = rest - extra
    return np.array(counts)


def normal_values(rng, extent, spread, reach, pieces=(), held_as=jnp.bfloat16):
    drawn = spread * jax.random.normal(rng, extent, jnp.float32)
    if pieces:
        drawn = drawn * levels(rng, extent, pieces, -0.22, 0.18)
    return jnp.clip(drawn, -reach, reach).astype(held_as)


def setup_inputs(seed: int = 0) -> dict:
    key_list = jax.random.split(jax.random.key(seed), 16)
    tokens = normal_values(key_list[0], (SECTIONS, TOKENS, D), 1.0, 6.0, ((0, 8), (1, 32)))
    expert_ids_keys = jax.random.split(jax.random.fold_in(key_list[1], 1), SECTIONS * TOKENS // TOK_DEV)
    expert_ids_turns = jax.random.permutation(jax.random.fold_in(key_list[1], 3), SECTIONS * TOKENS // TOK_DEV)
    expert_ids = jax.vmap(lambda own, number: routed_block(jax.random.fold_in(key_list[1], 2), own, number, TOK_DEV, EXPERTS, TOPK, SRC_CAP, 1))(expert_ids_keys, expert_ids_turns).reshape((SECTIONS, TOKENS, TOPK))
    gate_values = jnp.clip(0.3 + 1.2 * jax.random.uniform(key_list[2], (SECTIONS, TOKENS, TOPK), jnp.float32) ** levels(key_list[2], (SECTIONS, TOKENS, TOPK), ((0, 8), (1, 32)), -0.2, 0.2), 0.3, 1.5)
    w_gate = normal_values(key_list[3], (SECTIONS, D, EXPERTS * FF), D ** -0.5, 0.0625, ((0, 8), (2, 32)))
    w_up = normal_values(key_list[4], (SECTIONS, D, EXPERTS * FF), D ** -0.5, 0.0625, ((0, 8), (2, 32)))
    w_down = normal_values(key_list[5], (SECTIONS, EXPERTS * FF, D), FF ** -0.5, 0.1875, ((0, 8), (1, 32)))
    norm_gain = jnp.clip(1.0 + 0.18 * jax.random.normal(key_list[6], (SECTIONS, D), jnp.float32), 0.1, 1.9)
    w_dq = normal_values(key_list[7], (SECTIONS, D, QR), D ** -0.5, 0.0625, ((0, 8), (1, 32)))
    w_dkv = normal_values(key_list[8], (SECTIONS, D, KVR + ROPE), D ** -0.5, 0.0625, ((0, 8), (1, 32)))
    q_gain = jnp.clip(1.0 + 0.18 * jax.random.normal(key_list[9], (SECTIONS, QR), jnp.float32), 0.1, 1.9)
    kv_gain = jnp.clip(1.0 + 0.18 * jax.random.normal(key_list[10], (SECTIONS, KVR), jnp.float32), 0.1, 1.9)
    w_uq = normal_values(key_list[11], (SECTIONS, QR, HEADS * (NOPE + ROPE)), QR ** -0.5, 0.15625, ((0, 8), (2, 32)))
    w_uk = draw_w_uk(jax.random.fold_in(key_list[15], 71), 0)
    w_uv = normal_values(key_list[13], (SECTIONS, HEADS, KVR, VDIM), KVR ** -0.5, 0.25, ((0, 8), (1, 32)))
    prefix_cache = draw_prefix_cache(jax.random.fold_in(key_list[15], 71), 0)
    return {"tokens": tokens, "expert_ids": expert_ids, "gate_values": gate_values, "w_gate": w_gate, "w_up": w_up, "w_down": w_down, "norm_gain": norm_gain, "w_dq": w_dq, "w_dkv": w_dkv, "q_gain": q_gain, "kv_gain": kv_gain, "w_uq": w_uq, "w_uk": w_uk, "w_uv": w_uv, "prefix_cache": prefix_cache}


EPSILON = 1e-06

def rms_apply(values, gain_row):
    mean_square = lax.optimization_barrier(jnp.mean(values * values, axis=-1, keepdims=True))
    return values * lax.rsqrt(mean_square + EPSILON) * gain_row

def rotate(values, positions):
    half_width = values.shape[-1] // 2
    frequency = 10000.0 ** (-jnp.arange(half_width).astype(jnp.float32) / half_width)
    angles = positions.astype(jnp.float32)[:, None] * frequency[None, :]
    angles = angles.reshape((angles.shape[0],) + (1,) * (values.ndim - 2) + (half_width,))
    cosine = jnp.cos(angles)
    sine_part = jnp.sin(angles)
    leading = values[..., :half_width]
    trailing = values[..., half_width:]
    return jnp.concatenate([leading * cosine - trailing * sine_part, leading * sine_part + trailing * cosine], axis=-1)

def finish_latent(latent, q_gain, kv_gain, positions):
    query_width = q_gain.shape[-1]
    key_width = kv_gain.shape[-1]
    query_part = rms_apply(latent[:, :query_width], q_gain)
    key_part = rms_apply(latent[:, query_width:query_width + key_width], kv_gain)
    rope_part = rotate(latent[:, query_width + key_width:], positions)
    return jnp.concatenate([query_part, key_part, rope_part], axis=1).astype(jnp.bfloat16)

def moe_section(section_tokens, routed_ids, gate_weights, w_gate, w_up, w_down):
    block_size = EXPERTS * FF // N_EXPERT
    block_count = FF // block_size
    total = section_tokens.astype(jnp.float32)
    for expert in range(EXPERTS):
        gate_part = jnp.dot(section_tokens, w_gate[:, expert * FF:(expert + 1) * FF], preferred_element_type=jnp.float32)
        up_part = jnp.dot(section_tokens, w_up[:, expert * FF:(expert + 1) * FF], preferred_element_type=jnp.float32)
        hidden = (jax.nn.silu(gate_part) * up_part).astype(jnp.bfloat16)
        output = jnp.zeros(section_tokens.shape, jnp.float32)
        for block_index in range(block_count):
            first_row = expert * FF + block_index * block_size
            partial_value = jnp.dot(hidden[:, block_index * block_size:(block_index + 1) * block_size], w_down[first_row:first_row + block_size], preferred_element_type=jnp.float32)
            rounded = lax.optimization_barrier(partial_value.astype(jnp.bfloat16))
            output = output + rounded.astype(jnp.float32)
        chosen = lax.optimization_barrier(jnp.sum(jnp.where(routed_ids == expert, gate_weights, 0.0), axis=-1, keepdims=True))
        total = total + chosen * output
    return total.astype(jnp.bfloat16)

def attend_section(arriving, norm_gain, w_dq, w_dkv, q_gain, kv_gain, w_uq, w_uk, w_uv, prefix):
    row_count = arriving.shape[0]
    cache_len = prefix.shape[0]
    positions = cache_len + jnp.arange(row_count).astype(jnp.int32)
    normed = rms_apply(arriving.astype(jnp.float32), norm_gain).astype(jnp.bfloat16)
    latent = jnp.concatenate([jnp.dot(normed, w_dq, preferred_element_type=jnp.float32), jnp.dot(normed, w_dkv, preferred_element_type=jnp.float32)], axis=1)
    finished = finish_latent(latent, q_gain, kv_gain, positions)
    query_width = q_gain.shape[-1]
    key_rows = jnp.concatenate([prefix, finished[:, query_width:]], axis=0)
    query_rows = jnp.dot(finished[:, :query_width], w_uq, preferred_element_type=jnp.float32)
    query_rows = query_rows.reshape(row_count, HEADS, NOPE + ROPE)
    heads_nope = query_rows[..., :NOPE].astype(jnp.bfloat16)
    heads_rope = rotate(query_rows[..., NOPE:], positions).astype(jnp.bfloat16)
    visible = jnp.arange(key_rows.shape[0]).astype(jnp.int32)[None, :] <= positions[:, None]

    def head_output(operands):
        nope_rows, rope_rows, key_weight, value_weight = operands
        absorbed = jnp.dot(nope_rows, key_weight, preferred_element_type=jnp.float32).astype(jnp.bfloat16)
        queries = jnp.concatenate([absorbed, rope_rows], axis=1)
        scores = jnp.dot(queries, key_rows.T, preferred_element_type=jnp.float32) * (NOPE + ROPE) ** (-0.5)
        scores = jnp.where(visible, scores, -jnp.inf)
        weights = jax.nn.softmax(scores, axis=-1).astype(jnp.bfloat16)
        mixed_latent = jnp.dot(weights, key_rows[:, :KVR], preferred_element_type=jnp.float32).astype(jnp.bfloat16)
        return jnp.dot(mixed_latent, value_weight, preferred_element_type=jnp.float32).astype(jnp.bfloat16)
    per_head = lax.map(head_output, (jnp.transpose(heads_nope, (1, 0, 2)), jnp.transpose(heads_rope, (1, 0, 2)), w_uk, w_uv))
    return jnp.transpose(per_head, (1, 0, 2)).reshape(row_count, HEADS * VDIM)

def reference(tokens, expert_ids, gate_values, w_gate, w_up, w_down, norm_gain, w_dq, w_dkv, q_gain, kv_gain, w_uq, w_uk, w_uv, prefix_cache):
    mixed = jnp.stack([moe_section(tokens[section_index], expert_ids[section_index], gate_values[section_index], w_gate[section_index], w_up[section_index], w_down[section_index]) for section_index in range(SECTIONS)])
    arriving = jnp.roll(mixed, 1, axis=0)
    outputs = [attend_section(arriving[section_index], norm_gain[section_index], w_dq[section_index], w_dkv[section_index], q_gain[section_index], kv_gain[section_index], w_uq[section_index], w_uk[section_index], w_uv[section_index], prefix_cache[section_index]) for section_index in range(SECTIONS)]
    return jnp.stack(outputs)
```

```python
import functools

import jax
import jax.numpy as jnp
import numpy as np
from jax import lax
from jax.experimental import pallas as pl
from jax.experimental.pallas import tpu as pltpu
from jax.sharding import PartitionSpec as P

MESH = pl.DeviceIdType.MESH
BF = jnp.bfloat16
F32 = jnp.float32
EPSILON = 1e-06
D = 7168
ROWS = 16
SIDE = 128
WIDE = D + SIDE
HID = 128
QR = 1536
KVR = 512
ROPE = 64
NOPE = 128
KEY = KVR + ROPE
LAT = QR + KEY
LATW = 2176
FB = 224
TOK = 512
CACHE = 2048
PRE = 64
KT = (((1,), (0,)), ((), ()))
NT = (((1,), (1,)), ((), ()))
TN = (((0,), (0,)), ((), ()))


def mm(a, b, dims=KT):
    return lax.dot_general(a, b, dims, preferred_element_type=F32)


class Net:
    def __init__(self, send_sems, recv_sems, places):
        self.send_sems, self.recv_sems, self.places = send_sems, recv_sems, places
        self.ids, self.pending = {}, []

    def copy(self, key, src, dst, place):
        index = self.ids.setdefault(key, len(self.ids))
        return pltpu.make_async_remote_copy(
            src_ref=src,
            dst_ref=dst,
            send_sem=self.send_sems.at[index],
            recv_sem=self.recv_sems.at[index],
            device_id=self.places[place],
            device_id_type=MESH,
        )

    def send(self, key, src, dst, place):
        c = self.copy(key, src, dst, place)
        c.start()
        self.pending.append(c)

    def wait(self, key, ref):
        self.copy(key, ref, ref, "sib").wait_recv()

    def drain(self):
        for c in self.pending:
            c.wait_send()
        self.pending = []


DIRS = (("R", -1), ("L", 1))


def all_gather(n, net, slot, part):
    def pass_on(key, s, what, place):
        net.send(key, part(s, what), part(s, what), place)

    me, mate = slot(0, 0, 0), slot(1, 0, 0)
    pass_on((n, "xA"), me, "A", "xp")
    for way, _ in DIRS:
        pass_on((n, "A", way, 1), me, "A", way)
    pass_on((n, "xB", "", 0), me, "B", "xp")
    for way, _ in DIRS:
        pass_on((n, "B", way, 1), me, "B", way)
    pass_on((n, "s0", "", 0), me, "F", "sib")
    net.wait((n, "xA"), part(mate, "A"))
    for way, _ in DIRS:
        pass_on((n, "A1", way, 1), mate, "A", way)
    net.wait((n, "xB", "", 0), part(mate, "B"))
    pass_on((n, "s1", "", 0), mate, "F", "sib")
    yield 0

    def finish(h):
        if h < 4:
            for way, sign in DIRS:
                s = slot(1, sign * h, 0)
                net.wait((n, "xB", way, h), part(s, "B"))
                pass_on((n, "s1", way, h), s, "F", "sib")
        else:
            s = slot(1, 4, 0)
            net.wait((n, "xB", "R", 4), part(s, "B1"))
            net.wait((n, "xB", "L", 4), part(s, "B2"))
            pass_on((n, "s1", "R", 4), s, "F", "sib")

    for h in range(1, 5):
        for way, sign in DIRS:
            if h < 4 or way == "R":
                s = slot(0, sign * h, 0)
                net.wait((n, "A", way, h), part(s, "A"))
                if h < 3 or (h == 3 and way == "R"):
                    pass_on((n, "A", way, h + 1), s, "A", way)
        for way, sign in DIRS:
            s = slot(0, sign * h, 0)
            half = "B1" if way == "R" else "B2"
            if h < 4:
                net.wait((n, "B", way, h), part(s, "B"))
                pass_on((n, "B", way, h + 1), s, "B" if h < 3 else half, way)
                pass_on((n, "xB", way, h), s, "B", "xp")
                pass_on((n, "s0", way, h), s, "F", "sib")
            else:
                net.wait((n, "B", way, 4), part(s, half))
                pass_on((n, "xB", way, 4), s, half, "xp")
        if h == 4:
            pass_on((n, "s0", "R", 4), slot(0, 4, 0), "F", "sib")
        for way, sign in DIRS:
            if h < 4 or way == "L":
                s = slot(1, sign * h, 0)
                net.wait((n, "A1", way, h), part(s, "A"))
                if h < 3 or (h == 3 and way == "L"):
                    pass_on((n, "A1", way, h + 1), s, "A", way)
        if h >= 2:
            finish(h - 1)
            yield h - 1
    finish(4)
    yield 4


def sib_rows(n, net, slot, part, h):
    slots = []
    for way, sign in DIRS if 0 < h < 4 else (("" if h == 0 else "R", 1),):
        for dx in (0, 1):
            net.wait((n, f"s{dx}", way, h), part(slot(dx, sign * h, 1), "F"))
            slots += [slot(dx, sign * h, 0), slot(dx, sign * h, 1)]
    return slots


def reduce_scatter(n, net, value, cut, ms, mr, xs, xr):
    order = [4, 3, -3, 2, -2, 1, -1, 0]

    def put(key, buf, there, what, val, place):
        cut(buf, what)[...] = val.astype(BF)
        net.send(key, cut(buf, what), cut(there, what), place)

    def got(key, buf, what):
        net.wait(key, cut(buf, what))
        return cut(buf, what)[...].astype(F32)

    def over_x(k):
        put((n, "x", k), xs.at[k], xr.at[k], "B", value(1, order[k], "B"), "xp")

    over_x(0)
    for way, d in (("R", 0), ("L", 1)):
        w = 0 if way == "R" else 1
        put((n, "A", way, 1, d), ms.at[w, 0, d], mr.at[w, 0, d], "A", value(d, 4, "A"), way)
    for k in range(1, 3):
        over_x(k)
    net.wait((n, "x", 0), cut(xr.at[0], "B"))
    for w, (way, half) in enumerate((("R", "B1"), ("L", "B2"))):
        val = value(0, 4, half) + cut(xr.at[0], half)[...].astype(F32)
        put((n, "B", way, 1), ms.at[w, 0, 0], mr.at[w, 0, 0], half, val, way)
    for k in range(3, 8):
        over_x(k)
    yield 1
    for h in range(2, 5):
        for d in (1, 0):
            for w, way in enumerate("RL"):
                dz = (5 - h) * (1 if way == "R" else -1)
                val = value(d, dz, "A")
                if h > 2 or w == d:
                    val = val + got((n, "A", way, h - 1, d), mr.at[w, h - 2, d], "A")
                put((n, "A", way, h, d), ms.at[w, h - 1, d], mr.at[w, h - 1, d], "A", val, way)
        for w, (way, half, rest) in enumerate((("R", "B1", "B2"), ("L", "B2", "B1"))):
            dz = (5 - h) * (1 if way == "R" else -1)
            k = order.index(dz)
            net.wait((n, "x", k), cut(xr.at[k], "B"))
            if h == 2:
                buf = ms.at[w, h - 1, 0]
                val = value(0, dz, rest) + cut(xr.at[k], rest)[...].astype(F32)
                cut(buf, rest)[...] = val.astype(BF)
                val = value(0, dz, half) + cut(xr.at[k], half)[...].astype(F32)
                val = val + got((n, "B", way, 1), mr.at[w, 0, 0], half)
                cut(buf, half)[...] = val.astype(BF)
                net.send((n, "B", way, h), cut(buf, "B"), cut(mr.at[w, h - 1, 0], "B"), way)
            else:
                val = value(0, dz, "B") + cut(xr.at[k], "B")[...].astype(F32)
                val = val + got((n, "B", way, h - 1), mr.at[w, h - 2, 0], "B")
                put((n, "B", way, h), ms.at[w, h - 1, 0], mr.at[w, h - 1, 0], "B", val, way)
        yield h
    val = value(1, 0, "A")
    for w, way in enumerate("RL"):
        val = val + got((n, "A", way, 4, 1), mr.at[w, 3, 1], "A")
    put((n, "xA"), xs.at[7], xr.at[7], "A", val, "xp")
    own = value(0, 0, "A")
    for w, way in enumerate("RL"):
        own = own + got((n, "A", way, 4, 0), mr.at[w, 3, 0], "A")
    val = value(0, 0, "B") + got((n, "x", 7), xr.at[7], "B")
    for w, way in enumerate("RL"):
        val = val + got((n, "B", way, 4), mr.at[w, 3, 0], "B")
    yield "B", val
    yield "A", own + got((n, "xA"), xr.at[7], "A")


def last_cut(ref, a, b):
    return ref.at[..., pl.ds(a, b - a)]


TOK_CUTS = {"A": (0, 3072), "B": (3072, WIDE), "B1": (3072, 5120), "B2": (5120, WIDE), "F": (0, WIDE)}
LAT_CUTS = {"A": (0, 896), "B": (896, LATW), "B1": (896, 1536), "B2": (1536, LATW), "F": (0, LATW)}
PRE_CUTS = {"A": (0, 32), "B": (32, 64), "B1": (32, 48), "B2": (48, 64), "F": (0, 64)}
MIX_CUTS = {"A": (0, 96), "B": (96, 224), "B1": (96, 160), "B2": (160, 224), "F": (0, 224)}


def relay_kernel(
    sections,
    tok_ref, ids_ref, gates_ref, wg_ref, wu_ref, wd_ref, gain_ref, wq_ref, wk_ref, qg_ref, kg_ref, trig_ref, pre_ref,
    lat_out, pre_out,
    buf, wgu, wdn, wt, wdt, hid, hidt, toks_t, ms, mr, xs, xr, arr, sib_arr, arr_s, wqs, wks, lat,
    ms2, mr2, xs2, xr2, send_sems, recv_sems, local_sems,
):
    sec, e = lax.axis_index("section"), lax.axis_index("expert")
    xh, z, c = e // 16, (e // 2) % 8, e % 2

    def at(dx, dz, dc):
        return (xh + dx) % 2 * 16 + (z + dz + 8) % 8 * 2 + (c + dc) % 2

    places = {
        "R": (sec, at(0, 1, 0)),
        "L": (sec, at(0, -1, 0)),
        "xp": (sec, at(1, 0, 0)),
        "sib": (sec, at(0, 0, 1)),
        "next": ((sec + 1) % sections, e),
        "prev": ((sec + sections - 1) % sections, e),
    }
    net = Net(send_sems, recv_sems, places)
    local = []

    def fetch(k, src, dst):
        cp = pltpu.make_async_copy(src, dst, local_sems.at[k])
        cp.start()
        local.append(cp)
        return cp

    def slot(dx, dz, dc):
        return (c + dc) % 2 * 16 + (xh + dx) % 2 * 8 + (z + dz + 8) % 8

    me = slot(0, 0, 0)
    own = fetch(0, tok_ref, buf.at[me, :, pl.ds(0, D)])
    load_g = fetch(1, wg_ref, wgu.at[:, pl.ds(0, HID)])
    load_u = fetch(2, wu_ref, wgu.at[:, pl.ds(HID, HID)])
    load_d = fetch(3, wd_ref, wdn)
    load_q = fetch(4, wq_ref, wqs.at[0])
    load_k = fetch(5, wk_ref, wks.at[0])
    load_p = fetch(6, pre_ref, pre_out.at[e])

    barrier = pltpu.get_barrier_semaphore()
    for there in places.values():
        pl.semaphore_signal(barrier, inc=1, device_id=there, device_id_type=MESH)

    lane = lax.broadcasted_iota(jnp.int32, (ROWS, SIDE), 1)
    g = jnp.zeros((ROWS, SIDE), F32)
    for k in range(2):
        g = g + jnp.where(ids_ref[:, k : k + 1] == lane % 4, gates_ref[:, k : k + 1], 0.0)
    high = g.astype(BF)
    low = (g - high.astype(F32)).astype(BF)
    side = jnp.where(lane < 4, high.astype(F32), jnp.where(lane < 8, low.astype(F32), 0.0)).astype(BF)
    buf[me, :, D:WIDE] = side
    pl.semaphore_wait(barrier, len(places))
    own.wait()

    def tok_part(s, what):
        return last_cut(buf.at[s], *TOK_CUTS[what])

    expert = e // 8
    gather = all_gather("t", net, slot, tok_part)
    next(gather)
    load_q.wait()
    net.send("wq", wqs.at[0], wqs.at[1], "sib")
    load_k.wait()
    net.send("wk", wks.at[0], wks.at[1], "sib")

    load_d.wait()
    for k in range(8):
        wt[4 * k : 4 * k + 4] = wdn[:, 896 * k : 896 * (k + 1)].T.reshape(4, FB, HID)
    half = pl.ds(pl.multiple_of(c * HID, HID), HID)
    pairs = wt.reshape(16, 2, FB, HID)
    net.send("wd", pairs.at[:, (c + 1) % 2], wdt.at[:, :, half], "sib")
    keep_d = fetch(7, pairs.at[:, c], wdt.at[:, :, half])

    load_g.wait()
    load_u.wait()

    def experts(h):
        slots = sib_rows("t", net, slot, tok_part, h)
        m = len(slots) * ROWS
        acc = jnp.zeros((m, 2 * HID), F32)
        for k in range(7):
            rows = jnp.concatenate([buf[s, :, 1024 * k : 1024 * (k + 1)] for s in slots], axis=0)
            acc = acc + mm(rows, wgu[1024 * k : 1024 * (k + 1), :])
        side = jnp.concatenate([buf[s, :, D:WIDE] for s in slots], axis=0).astype(F32)
        lane = lax.broadcasted_iota(jnp.int32, (m, SIDE), 1)
        gate = jnp.sum(jnp.where((lane % 4 == expert) & (lane < 8), side, 0.0), axis=1, keepdims=True)
        gp, up = acc[:, :HID], acc[:, HID:]
        val = (gp / (1.0 + jnp.exp(-gp)) * up * gate).astype(BF)
        for i, s in enumerate(slots):
            hid[pl.ds(pl.multiple_of(s * ROWS, ROWS), ROWS), half] = val[ROWS * i : ROWS * (i + 1)]

    experts(0)
    for h in gather:
        experts(h)
    net.send("hid", hid.at[:, half], hid.at[:, half], "sib")

    start = jnp.minimum(FB * e // 128 * 128, D - 384)
    window = buf[:, :, pl.ds(pl.multiple_of(start, 128), 384)].reshape(TOK, 384)
    toks_t[...] = window.T

    other = pl.ds(pl.multiple_of((c + 1) % 2 * HID, HID), HID)
    net.wait("hid", hid.at[:, other])
    net.wait("wd", wdt.at[:, :, other])
    keep_d.wait()
    hidt[...] = hid[...].T

    def mixed_term(dx, dz, what):
        a, b = MIX_CUTS[what]
        block = (xh + dx) % 2 * 8 + (z + dz + 8) % 8
        return mm(wdt[block, a:b, :], hidt[...])

    def mix_cut(ref, what):
        a, b = MIX_CUTS[what]
        return ref.at[pl.ds(a, b - a)]

    load_p.wait()
    off = FB * e - start
    for got in reduce_scatter("m", net, mixed_term, mix_cut, ms, mr, xs, xr):
        if not isinstance(got, tuple):
            continue
        what, val = got
        a, b = MIX_CUTS[what]
        rows = toks_t[pl.ds(pl.multiple_of(off + a, 32), b - a), :].astype(F32)
        arr_s[a:b] = (val + rows).astype(BF)
        net.send(("next", what), arr_s.at[pl.ds(a, b - a)], arr.at[pl.ds(a, b - a)], "next")

    def pre_part(s, what):
        a, b = PRE_CUTS[what]
        return pre_out.at[s, pl.ds(a, b - a)]

    prefix = all_gather("p", net, at, pre_part)
    next(prefix)

    for what in "BA":
        net.wait(("next", what), mix_cut(arr, what))
    mine = pl.ds(pl.multiple_of(c * 256, 256), 256)
    theirs = pl.ds(pl.multiple_of((c + 1) % 2 * 256, 256), 256)
    net.send("arr", arr.at[:, theirs], sib_arr, "sib")
    net.wait("wq", wqs.at[1])
    net.wait("wk", wks.at[1])
    squares = jnp.zeros((1, 256), F32)
    for i in range(2):
        if i == 1:
            net.wait("arr", sib_arr)
        x = (arr[:, mine] if i == 0 else sib_arr[...]).astype(F32)
        squares = squares + jnp.sum(x * x, axis=0, keepdims=True)
        scaled = (x * gain_ref[i, :, 0:1]).T.astype(BF)
        if i == 0:
            lat[:, 0:QR] = mm(scaled, wqs[0])
            lat[:, QR:LAT] = mm(scaled, wks[0])
        else:
            lat[:, 0:QR] += mm(scaled, wqs[1])
            lat[:, QR:LAT] += mm(scaled, wks[1])
    lat[:, LAT:LATW] = jnp.broadcast_to(squares, (128, 256)).T[:, 0 : LATW - LAT]

    def lat_term(dx, dz, what):
        a, b = LAT_CUTS[what]
        block = (xh + dx) % 2 * 8 + (z + dz + 8) % 8
        return lat[pl.ds(pl.multiple_of(block * ROWS, ROWS), ROWS), a:b]

    def lat_cut(ref, what):
        return last_cut(ref, *LAT_CUTS[what])

    sums = {}
    for got in reduce_scatter("l", net, lat_term, lat_cut, ms2, mr2, xs2, xr2):
        if isinstance(got, tuple):
            sums[got[0]] = got[1]
        else:
            next(prefix, None)
    total = jnp.concatenate([sums["A"], sums["B"]], axis=1)
    scale = lax.rsqrt(total[:, LAT : LAT + 1] * (1.0 / D) + EPSILON)

    def rms(v, gain):
        v = v * scale
        return (v * lax.rsqrt(jnp.mean(v * v, axis=1, keepdims=True) + EPSILON) * gain).astype(BF)

    lat_out[e, :, 0:QR] = rms(total[:, 0:QR], qg_ref[...])
    lat_out[e, :, QR : QR + KVR] = rms(total[:, QR : QR + KVR], kg_ref[...])
    tail = total[:, QR + KVR :] * scale
    first, second = tail[:, 0:32], tail[:, 32:64]
    cos, sin = trig_ref[e, :, 0:32], trig_ref[e, :, 32:64]
    turned = jnp.concatenate([first * cos - second * sin, first * sin + second * cos], axis=1)
    lat_out[e, :, QR + KVR : LAT] = turned.astype(BF)
    lat_out[e, :, LAT:LATW] = jnp.zeros((ROWS, LATW - LAT), BF)

    def lat_part(s, what):
        return last_cut(lat_out.at[s], *LAT_CUTS[what])

    for _ in prefix:
        pass
    for h in range(5):
        sib_rows("p", net, at, pre_part, h)
    for h in all_gather("o", net, at, lat_part):
        sib_rows("o", net, at, lat_part, h)
    net.drain()


def trig_table():
    half = ROPE // 2
    frequency = 10000.0 ** (-np.arange(half) / half)
    angles = (CACHE + np.arange(TOK))[:, None] * frequency[None, :].astype(np.float32)
    angles = angles.astype(np.float32).astype(np.float64)
    both = np.concatenate([np.cos(angles), np.sin(angles)], axis=1)
    return both.astype(np.float32)


def attend_kernel(lat_ref, pre_ref, trig_ref, wuq_ref, wuk_ref, wuv_ref, out_ref, kv, qs, acc_ref, m_ref, l_ref):
    scale = (NOPE + ROPE) ** (-0.5)
    trig = trig_ref[...]
    cos, sin = trig[:, 0:32], trig[:, 32:64]
    kv[:, 0:KEY] = lat_ref[:, QR:LAT]
    q = mm(lat_ref[:, 0:QR], wuq_ref[...])
    for h in range(2):
        base = h * (NOPE + ROPE)
        nope = q[:, base : base + NOPE].astype(BF)
        qs[h, :, 0:KVR] = mm(nope, wuk_ref[h]).astype(BF)
        first = q[:, base + NOPE : base + NOPE + 32]
        second = q[:, base + NOPE + 32 : base + NOPE + 64]
        turned = jnp.concatenate([first * cos - second * sin, first * sin + second * cos], axis=1)
        qs[h, :, KVR:KEY] = turned.astype(BF)
    for h in range(2):
        for i in range(2):
            rows = pl.ds(256 * i, 256)
            query = qs[h, rows, :]
            for b in range(5):
                if b < 4:
                    keys = pre_ref[512 * b : 512 * (b + 1), :]
                else:
                    keys = kv[...]
                s = mm(query, keys, NT) * scale
                if b == 4:
                    t = lax.broadcasted_iota(jnp.int32, s.shape, 0) + 256 * i
                    j = lax.broadcasted_iota(jnp.int32, s.shape, 1)
                    s = jnp.where(j <= t, s, -jnp.inf)
                top = jnp.max(s, axis=1, keepdims=True)
                if b == 0:
                    m = top
                    p = jnp.exp(s - m)
                    l = jnp.sum(p, axis=1, keepdims=True)
                    acc = mm(p.astype(BF), keys[:, 0:KVR])
                else:
                    new = jnp.maximum(m, top)
                    fade = jnp.exp(m - new)
                    p = jnp.exp(s - new)
                    l = l * fade + jnp.sum(p, axis=1, keepdims=True)
                    acc = acc * fade + mm(p.astype(BF), keys[:, 0:KVR])
                    m = new
            latent = (acc / l).astype(BF)
            out_ref[rows, 128 * h : 128 * (h + 1)] = mm(latent, wuv_ref[h]).astype(BF)


def per_device(
    sections, tokens, expert_ids, gate_values, w_gate, w_up, w_down, norm_gain, w_dq, w_dkv, q_gain, kv_gain, w_uq, w_uk,
    w_uv, prefix_cache,
):
    e = lax.axis_index("expert")
    gains = norm_gain[0].reshape(32, FB)
    pair = jnp.stack([lax.dynamic_index_in_dim(gains, k, 0, False) for k in (e, e // 2 * 2 + 1 - e % 2)])
    pair = jnp.broadcast_to(pair[:, :, None], (2, FB, 128))
    table = trig_table()
    vm = pl.BlockSpec(memory_space=pltpu.VMEM)
    anyw = pl.BlockSpec(memory_space=pl.ANY)
    V = pltpu.VMEM
    lat_rows, prefix = pl.pallas_call(
        functools.partial(relay_kernel, sections),
        name="relay",
        out_shape=(jax.ShapeDtypeStruct((32, ROWS, LATW), BF), jax.ShapeDtypeStruct((32, PRE, KEY), BF)),
        in_specs=[anyw, vm, vm, anyw, anyw, anyw, vm, anyw, anyw, vm, vm, vm, anyw],
        out_specs=(vm, vm),
        scratch_shapes=[
            V((32, ROWS, WIDE), BF),
            V((D, 2 * HID), BF),
            V((HID, D), BF),
            V((32, FB, HID), BF),
            V((16, FB, 2 * HID), BF),
            V((TOK, 2 * HID), BF),
            V((2 * HID, TOK), BF),
            V((384, TOK), BF),
            V((2, 4, 2, FB, TOK), BF),
            V((2, 4, 2, FB, TOK), BF),
            V((8, FB, TOK), BF),
            V((8, FB, TOK), BF),
            V((FB, TOK), BF),
            V((FB, TOK // 2), BF),
            V((FB, TOK), BF),
            V((2, FB, QR), BF),
            V((2, FB, KEY), BF),
            V((TOK // 2, LATW), F32),
            V((2, 4, 2, ROWS, LATW), BF),
            V((2, 4, 2, ROWS, LATW), BF),
            V((8, ROWS, LATW), BF),
            V((8, ROWS, LATW), BF),
            pltpu.SemaphoreType.DMA((256,)),
            pltpu.SemaphoreType.DMA((256,)),
            pltpu.SemaphoreType.DMA((8,)),
        ],
        compiler_params=pltpu.CompilerParams(collective_id=0, has_side_effects=True, vmem_limit_bytes=58 << 20),
        cost_estimate=pl.CostEstimate(flops=4 * 10**9, bytes_accessed=12 * 10**6, transcendentals=10**6),
    )(
        tokens[0], expert_ids[0], gate_values[0], w_gate[0], w_up[0], w_down[0], pair, w_dq[0], w_dkv[0], q_gain,
        kv_gain, jnp.asarray(table.reshape(32, ROWS, ROPE)), prefix_cache[0],
    )
    out = pl.pallas_call(
        attend_kernel,
        name="attend",
        out_shape=jax.ShapeDtypeStruct((TOK, 256), BF),
        in_specs=[vm] * 6,
        out_specs=vm,
        scratch_shapes=[
            V((TOK, KEY), BF),
            V((2, TOK, KEY), BF),
            V((8, 128), F32),
            V((8, 128), F32),
            V((8, 128), F32),
        ],
        compiler_params=pltpu.CompilerParams(vmem_limit_bytes=58 << 20),
        cost_estimate=pl.CostEstimate(flops=9 * 10**9, bytes_accessed=8 * 10**6, transcendentals=3 * 10**6),
    )(
        lat_rows.reshape(TOK, LATW), prefix.reshape(CACHE, KEY), jnp.asarray(table), w_uq[0], w_uk[0], w_uv[0]
    )
    return out[None]


def solution(mesh):
    placed = (
        P("section", "expert", None),
        P("section", "expert", None),
        P("section", "expert", None),
        P("section", None, "expert"),
        P("section", None, "expert"),
        P("section", "expert", None),
        P("section", None),
        P("section", "expert", None),
        P("section", "expert", None),
        P("section", None),
        P("section", None),
        P("section", None, "expert"),
        P("section", "expert", None, None),
        P("section", "expert", None, None),
        P("section", "expert", None),
    )
    return jax.shard_map(
        functools.partial(per_device, mesh.shape["section"]),
        mesh=mesh,
        in_specs=placed,
        out_specs=P("section", None, "expert"),
        check_vma=False,
    )
```

```python
import functools

import jax
import jax.numpy as jnp
import numpy as np
from jax import lax
from jax.experimental import pallas as pl
from jax.experimental.pallas import tpu as pltpu
from jax.sharding import PartitionSpec as P

MESH = pl.DeviceIdType.MESH
BF = jnp.bfloat16
F32 = jnp.float32
EPSILON = 1e-06
D = 7168
ROWS = 16
SIDE = 128
WIDE = D + SIDE
HID = 128
QR = 1536
KVR = 512
ROPE = 64
NOPE = 128
KEY = KVR + ROPE
LAT = QR + KEY
LATW = 2176
FB = 224
TOK = 512
CACHE = 2048
PRE = 64
KT = (((1,), (0,)), ((), ()))
NT = (((1,), (1,)), ((), ()))
TN = (((0,), (0,)), ((), ()))


def mm(a, b, dims=KT):
    return lax.dot_general(a, b, dims, preferred_element_type=F32)


class Net:
    def __init__(self, send_sems, recv_sems, places):
        self.send_sems, self.recv_sems, self.places = send_sems, recv_sems, places
        self.ids, self.pending = {}, []

    def copy(self, key, src, dst, place):
        index = self.ids.setdefault(key, len(self.ids))
        return pltpu.make_async_remote_copy(
            src_ref=src,
            dst_ref=dst,
            send_sem=self.send_sems.at[index],
            recv_sem=self.recv_sems.at[index],
            device_id=self.places[place],
            device_id_type=MESH,
        )

    def send(self, key, src, dst, place):
        c = self.copy(key, src, dst, place)
        c.start()
        self.pending.append(c)

    def wait(self, key, ref):
        self.copy(key, ref, ref, "sib").wait_recv()

    def drain(self):
        for c in self.pending:
            c.wait_send()
        self.pending = []


DIRS = (("R", -1), ("L", 1))


def all_gather(n, net, slot, part):
    def pass_on(key, s, what, place):
        net.send(key, part(s, what), part(s, what), place)

    me, mate = slot(0, 0, 0), slot(1, 0, 0)
    pass_on((n, "xA"), me, "A", "xp")
    for way, _ in DIRS:
        pass_on((n, "A", way, 1), me, "A", way)
    pass_on((n, "xB", "", 0), me, "B", "xp")
    for way, _ in DIRS:
        pass_on((n, "B", way, 1), me, "B", way)
    pass_on((n, "s0", "", 0), me, "F", "sib")
    yield None
    net.wait((n, "xA"), part(mate, "A"))
    for way, _ in DIRS:
        pass_on((n, "A1", way, 1), mate, "A", way)
    yield None
    net.wait((n, "xB", "", 0), part(mate, "B"))
    pass_on((n, "s1", "", 0), mate, "F", "sib")

    def finish(h):
        if h < 4:
            for way, sign in DIRS:
                s = slot(1, sign * h, 0)
                net.wait((n, "xB", way, h), part(s, "B"))
                pass_on((n, "s1", way, h), s, "F", "sib")
        else:
            s = slot(1, 4, 0)
            net.wait((n, "xB", "R", 4), part(s, "B1"))
            net.wait((n, "xB", "L", 4), part(s, "B2"))
            pass_on((n, "s1", "R", 4), s, "F", "sib")

    for h in range(1, 5):
        for way, sign in DIRS:
            if h < 4 or way == "R":
                s = slot(0, sign * h, 0)
                net.wait((n, "A", way, h), part(s, "A"))
                if h < 3 or (h == 3 and way == "R"):
                    pass_on((n, "A", way, h + 1), s, "A", way)
        yield None
        if h >= 2:
            finish(h - 1)
        for way, sign in DIRS:
            s = slot(0, sign * h, 0)
            half = "B1" if way == "R" else "B2"
            if h < 4:
                net.wait((n, "B", way, h), part(s, "B"))
                pass_on((n, "B", way, h + 1), s, "B" if h < 3 else half, way)
                pass_on((n, "xB", way, h), s, "B", "xp")
                pass_on((n, "s0", way, h), s, "F", "sib")
            else:
                net.wait((n, "B", way, 4), part(s, half))
                pass_on((n, "xB", way, 4), s, half, "xp")
        if h == 4:
            pass_on((n, "s0", "R", 4), slot(0, 4, 0), "F", "sib")
        yield h - 1
        for way, sign in DIRS:
            if h < 4 or way == "L":
                s = slot(1, sign * h, 0)
                net.wait((n, "A1", way, h), part(s, "A"))
                if h < 3 or (h == 3 and way == "L"):
                    pass_on((n, "A1", way, h + 1), s, "A", way)
        yield None
    finish(4)
    yield 4


def sib_rows(n, net, slot, part, h):
    slots = []
    for way, sign in DIRS if 0 < h < 4 else (("" if h == 0 else "R", 1),):
        for dx in (0, 1):
            net.wait((n, f"s{dx}", way, h), part(slot(dx, sign * h, 1), "F"))
            slots += [slot(dx, sign * h, 0), slot(dx, sign * h, 1)]
    return slots


def reduce_scatter(n, net, value, cut, ms, mr, xs, xr):
    order = [4, 3, -3, 2, -2, 1, -1, 0]

    def put(key, buf, there, what, val, place):
        cut(buf, what)[...] = val.astype(BF)
        net.send(key, cut(buf, what), cut(there, what), place)

    def got(key, buf, what):
        net.wait(key, cut(buf, what))
        return cut(buf, what)[...].astype(F32)

    def over_x(k):
        if k < 8:
            put((n, "x", k), xs.at[k], xr.at[k], "B", value(1, order[k], "B"), "xp")

    def from_x(k):
        net.wait((n, "x", k), cut(xr.at[k], "B"))
        over_x(k + 3)

    def hop_a(h):
        for d in (1, 0):
            for w, way in enumerate("RL"):
                if h == 1 and w != d:
                    continue
                val = value(d, (5 - h) * (1 if way == "R" else -1), "A")
                if h > 2 or (h == 2 and w == d):
                    val = val + got((n, "A", way, h - 1, d), mr.at[w, h - 2, d], "A")
                put((n, "A", way, h, d), ms.at[w, h - 1, d], mr.at[w, h - 1, d], "A", val, way)

    def hop_b(h):
        for w, (way, half, rest) in enumerate((("R", "B1", "B2"), ("L", "B2", "B1"))):
            dz = (5 - h) * (1 if way == "R" else -1)
            k = order.index(dz if h > 1 else 4)
            if h > 1 or w == 0:
                from_x(k)
            buf, there = ms.at[w, h - 1, 0], mr.at[w, h - 1, 0]
            if h == 1:
                val = value(0, 4, half) + cut(xr.at[k], half)[...].astype(F32)
                put((n, "B", way, 1), buf, there, half, val, way)
            elif h == 2:
                val = value(0, dz, rest) + cut(xr.at[k], rest)[...].astype(F32)
                cut(buf, rest)[...] = val.astype(BF)
                val = value(0, dz, half) + cut(xr.at[k], half)[...].astype(F32)
                val = val + got((n, "B", way, 1), mr.at[w, 0, 0], half)
                cut(buf, half)[...] = val.astype(BF)
                net.send((n, "B", way, h), cut(buf, "B"), cut(there, "B"), way)
            else:
                val = value(0, dz, "B") + cut(xr.at[k], "B")[...].astype(F32)
                val = val + got((n, "B", way, h - 1), mr.at[w, h - 2, 0], "B")
                put((n, "B", way, h), buf, there, "B", val, way)

    over_x(0)
    hop_a(1)
    over_x(1)
    over_x(2)
    yield 1
    for h in range(2, 5):
        hop_a(h)
        hop_b(h - 1)
        yield h
    val = value(1, 0, "A")
    for w, way in enumerate("RL"):
        val = val + got((n, "A", way, 4, 1), mr.at[w, 3, 1], "A")
    put((n, "xA"), xs.at[7], xr.at[7], "A", val, "xp")
    hop_b(4)
    yield 5
    own = value(0, 0, "A")
    for w, way in enumerate("RL"):
        own = own + got((n, "A", way, 4, 0), mr.at[w, 3, 0], "A")
    yield "A", own + got((n, "xA"), xr.at[7], "A")
    val = value(0, 0, "B")
    from_x(7)
    val = val + cut(xr.at[7], "B")[...].astype(F32)
    for w, way in enumerate("RL"):
        val = val + got((n, "B", way, 4), mr.at[w, 3, 0], "B")
    yield "B", val


def last_cut(ref, a, b):
    return ref.at[..., pl.ds(a, b - a)]


TOK_CUTS = {"A": (0, 3072), "B": (3072, WIDE), "B1": (3072, 5120), "B2": (5120, WIDE), "F": (0, WIDE)}
LAT_CUTS = {"A": (0, 896), "B": (896, LATW), "B1": (896, 1536), "B2": (1536, LATW), "F": (0, LATW)}
PRE_CUTS = {"A": (0, 32), "B": (32, 64), "B1": (32, 48), "B2": (48, 64), "F": (0, 64)}
MIX_CUTS = {"A": (0, 112), "B": (112, 224), "B1": (112, 176), "B2": (176, 224), "F": (0, 224)}


def relay_kernel(
    sections,
    tok_ref, ids_ref, gates_ref, wg_ref, wu_ref, wd_ref, gain_ref, wq_ref, wk_ref, qg_ref, kg_ref, trig_ref, pre_ref,
    wuq_ref, wuk_ref, wuv_ref,
    out_ref,
    buf, wgu, wdn, wt, wdt, hid, hidt, toks_t, ms, mr, xs, xr, arr, sib_arr, arr_s, wqs, wks, lat,
    ms2, mr2, xs2, xr2, lat_out, pre_out, gcol, wuq, wuk, wuv, qs, acc_s, max_s, sum_s, send_sems, recv_sems, local_sems,
):
    sec, e = lax.axis_index("section"), lax.axis_index("expert")
    xh, z, c = e // 16, (e // 2) % 8, e % 2

    def at(dx, dz, dc):
        return (xh + dx) % 2 * 16 + (z + dz + 8) % 8 * 2 + (c + dc) % 2

    places = {
        "R": (sec, at(0, 1, 0)),
        "L": (sec, at(0, -1, 0)),
        "xp": (sec, at(1, 0, 0)),
        "sib": (sec, at(0, 0, 1)),
        "next": ((sec + 1) % sections, e),
        "prev": ((sec + sections - 1) % sections, e),
    }
    net = Net(send_sems, recv_sems, places)
    local = []

    def fetch(k, src, dst):
        cp = pltpu.make_async_copy(src, dst, local_sems.at[k])
        cp.start()
        local.append(cp)
        return cp

    def slot(dx, dz, dc):
        return (c + dc) % 2 * 16 + (xh + dx) % 2 * 8 + (z + dz + 8) % 8

    me = slot(0, 0, 0)
    own = fetch(0, tok_ref, buf.at[me, :, pl.ds(0, D)])
    load_g = fetch(1, wg_ref, wgu.at[:, pl.ds(0, HID)])
    load_u = fetch(2, wu_ref, wgu.at[:, pl.ds(HID, HID)])
    load_d = fetch(3, wd_ref, wdn)
    load_q = fetch(4, wq_ref, wqs.at[0])
    load_k = fetch(5, wk_ref, wks.at[0])
    load_p = fetch(6, pre_ref, pre_out.at[e])
    load_uq = fetch(8, wuq_ref, wuq)
    load_uk = fetch(9, wuk_ref, wuk)
    load_uv = fetch(10, wuv_ref, wuv)

    barrier = pltpu.get_barrier_semaphore()
    for there in places.values():
        pl.semaphore_signal(barrier, inc=1, device_id=there, device_id_type=MESH)

    lane = lax.broadcasted_iota(jnp.int32, (ROWS, SIDE), 1)
    diag = lax.broadcasted_iota(jnp.int32, (ROWS, ROWS), 0) == lax.broadcasted_iota(jnp.int32, (ROWS, ROWS), 1)
    g = jnp.zeros((ROWS, SIDE), F32)
    for k in range(2):
        chosen = jnp.sum(jnp.where(diag, ids_ref[k : k + 1, :], 0), axis=1, keepdims=True)
        weight = jnp.sum(jnp.where(diag, gates_ref[k : k + 1, :], 0.0), axis=1, keepdims=True)
        g = g + jnp.where(chosen == lane % 4, weight, 0.0)
    high = g.astype(BF)
    low = (g - high.astype(F32)).astype(BF)
    side = jnp.where(lane < 4, high.astype(F32), jnp.where(lane < 8, low.astype(F32), 0.0)).astype(BF)
    buf[me, :, D:WIDE] = side

    load_d.wait()
    for k in range(8):
        wt[4 * k : 4 * k + 4] = wdn[:, 896 * k : 896 * (k + 1)].T.reshape(4, FB, HID)

    def window(owner):
        return jnp.minimum(FB * owner // 128 * 128, D - 384)

    for i in range(2):
        first = window(at(0, 0, i))
        piece = gain_ref[0:1, pl.ds(pl.multiple_of(first, 128), 384)]
        gcol[i] = jnp.broadcast_to(piece, (128, 384)).T
    pl.semaphore_wait(barrier, len(places))
    own.wait()

    def tok_part(s, what):
        return last_cut(buf.at[s], *TOK_CUTS[what])

    expert = e // 8
    gather = all_gather("t", net, slot, tok_part)
    next(gather)
    load_q.wait()
    net.send("wq", wqs.at[0], wqs.at[1], "sib")
    load_k.wait()
    net.send("wk", wks.at[0], wks.at[1], "sib")

    half = pl.ds(pl.multiple_of(c * HID, HID), HID)
    pairs = wt.reshape(16, 2, FB, HID)
    net.send("wd", pairs.at[:, (c + 1) % 2], wdt.at[:, :, half], "sib")
    keep_d = fetch(7, pairs.at[:, c], wdt.at[:, :, half])

    load_g.wait()
    load_u.wait()

    def experts(h):
        slots = sib_rows("t", net, slot, tok_part, h)
        m = len(slots) * ROWS
        acc = jnp.zeros((m, 2 * HID), F32)
        for k in range(7):
            rows = jnp.concatenate([buf[s, :, 1024 * k : 1024 * (k + 1)] for s in slots], axis=0)
            acc = acc + mm(rows, wgu[1024 * k : 1024 * (k + 1), :])
        side = jnp.concatenate([buf[s, :, D:WIDE] for s in slots], axis=0).astype(F32)
        lane = lax.broadcasted_iota(jnp.int32, (m, SIDE), 1)
        gate = jnp.sum(jnp.where((lane % 4 == expert) & (lane < 8), side, 0.0), axis=1, keepdims=True)
        gp, up = acc[:, :HID], acc[:, HID:]
        val = (gp / (1.0 + jnp.exp(-gp)) * up * gate).astype(BF)
        for i, s in enumerate(slots):
            hid[pl.ds(pl.multiple_of(s * ROWS, ROWS), ROWS), half] = val[ROWS * i : ROWS * (i + 1)]

    def pre_part(s, what):
        a, b = PRE_CUTS[what]
        return pre_out.at[s, pl.ds(a, b - a)]

    prefix = all_gather("p", net, at, pre_part)

    def ticks(count):
        for _ in range(count):
            next(prefix, None)

    for h in gather:
        if h is not None:
            if h == 4:
                load_p.wait()
                ticks(1)
            experts(h)
    net.send("hid", hid.at[:, half], hid.at[:, half], "sib")

    start = window(e)
    toks_t[...] = buf[:, :, pl.ds(pl.multiple_of(start, 128), 384)].reshape(TOK, 384).T

    other = pl.ds(pl.multiple_of((c + 1) % 2 * HID, HID), HID)
    net.wait("hid", hid.at[:, other])
    net.wait("wd", wdt.at[:, :, other])
    keep_d.wait()
    hidt[...] = hid[...].T

    def mixed_term(dx, dz, what):
        a, b = MIX_CUTS[what]
        block = (xh + dx) % 2 * 8 + (z + dz + 8) % 8
        return mm(wdt[block, a:b, :], hidt[...])

    def mix_cut(ref, what):
        a, b = MIX_CUTS[what]
        return ref.at[pl.ds(a, b - a)]

    off = FB * e - start
    for got in reduce_scatter("m", net, mixed_term, mix_cut, ms, mr, xs, xr):
        if not isinstance(got, tuple):
            ticks({1: 1, 5: 2}.get(got, 0))
            continue
        what, val = got
        a, b = MIX_CUTS[what]
        rows = toks_t[pl.ds(pl.multiple_of(off + a, 16), b - a), :].astype(F32)
        arr_s[a:b] = (val + rows).astype(BF)
        net.send(("next", what), arr_s.at[pl.ds(a, b - a)], arr.at[pl.ds(a, b - a)], "next")
    ticks(4)

    for what in "AB":
        net.wait(("next", what), mix_cut(arr, what))
    mine = pl.ds(pl.multiple_of(c * 256, 256), 256)
    theirs = pl.ds(pl.multiple_of((c + 1) % 2 * 256, 256), 256)
    net.send("arr", arr.at[:, theirs], sib_arr, "sib")
    net.wait("wq", wqs.at[1])
    net.wait("wk", wks.at[1])
    squares = jnp.zeros((1, 256), F32)
    for i in range(2):
        if i == 1:
            net.wait("arr", sib_arr)
        x = (arr[:, mine] if i == 0 else sib_arr[...]).astype(F32)
        squares = squares + jnp.sum(x * x, axis=0, keepdims=True)
        shift = FB * at(0, 0, i) - window(at(0, 0, i))
        scaled = (x * gcol[i, pl.ds(pl.multiple_of(shift, 32), FB), 0:1]).T.astype(BF)
        if i == 0:
            lat[:, 0:QR] = mm(scaled, wqs[0])
            lat[:, QR:LAT] = mm(scaled, wks[0])
        else:
            lat[:, 0:QR] += mm(scaled, wqs[1])
            lat[:, QR:LAT] += mm(scaled, wks[1])
    lat[:, LAT:LATW] = jnp.broadcast_to(squares, (128, 256)).T[:, 0 : LATW - LAT]

    def lat_term(dx, dz, what):
        a, b = LAT_CUTS[what]
        block = (xh + dx) % 2 * 8 + (z + dz + 8) % 8
        return lat[pl.ds(pl.multiple_of(block * ROWS, ROWS), ROWS), a:b]

    def lat_cut(ref, what):
        return last_cut(ref, *LAT_CUTS[what])

    sums = {}
    for got in reduce_scatter("l", net, lat_term, lat_cut, ms2, mr2, xs2, xr2):
        if isinstance(got, tuple):
            sums[got[0]] = got[1]
        else:
            ticks(2)
    total = jnp.concatenate([sums["A"], sums["B"]], axis=1)
    scale = lax.rsqrt(total[:, LAT : LAT + 1] * (1.0 / D) + EPSILON)

    def rms(v, gain):
        v = v * scale
        return (v * lax.rsqrt(jnp.mean(v * v, axis=1, keepdims=True) + EPSILON) * gain).astype(BF)

    lat_out[e, :, 0:QR] = rms(total[:, 0:QR], qg_ref[...])
    lat_out[e, :, QR : QR + KVR] = rms(total[:, QR : QR + KVR], kg_ref[...])
    tail = total[:, QR + KVR :] * scale
    first, second = tail[:, 0:32], tail[:, 32:64]
    cos, sin = trig_ref[e, :, 0:32], trig_ref[e, :, 32:64]
    turned = jnp.concatenate([first * cos - second * sin, first * sin + second * cos], axis=1)
    lat_out[e, :, QR + KVR : LAT] = turned.astype(BF)
    lat_out[e, :, LAT:LATW] = jnp.zeros((ROWS, LATW - LAT), BF)

    def lat_part(s, what):
        return last_cut(lat_out.at[s], *LAT_CUTS[what])

    for cp in (load_uq, load_uk, load_uv):
        cp.wait()
    groups = {}

    def queries(h):
        slots = sib_rows("o", net, at, lat_part, h)
        m = len(slots) * ROWS
        base = {0: 0, 1: 128, 2: 384, 3: 640, 4: 896}[h]
        rows = jnp.concatenate([lat_out[s, :, 0:QR] for s in slots], axis=0)
        turn = jnp.concatenate([trig_ref[s] for s in slots], axis=0)
        cos, sin = turn[:, 0:32], turn[:, 32:64]
        q = mm(rows, wuq[...])
        for k in range(2):
            a, own_rows = k * (NOPE + ROPE), slice(base + k * m, base + (k + 1) * m)
            qs[own_rows, 0:KVR] = mm(q[:, a : a + NOPE].astype(BF), wuk[k]).astype(BF)
            first, second = q[:, a + NOPE : a + NOPE + 32], q[:, a + NOPE + 32 : a + NOPE + 64]
            turned = jnp.concatenate([first * cos - second * sin, first * sin + second * cos], axis=1)
            qs[own_rows, KVR:KEY] = turned.astype(BF)
        query = qs[base : base + 2 * m, :]
        score, top = [], None
        for b in range(4):
            keys = pre_out[8 * b : 8 * b + 8].reshape(512, KEY)
            score.append(mm(query, keys, NT))
            high = jnp.max(score[-1], axis=1, keepdims=True)
            top = high if top is None else jnp.maximum(top, high)
        total, mixed = 0.0, 0.0
        for b in range(4):
            keys = pre_out[8 * b : 8 * b + 8, :, 0:KVR].reshape(512, KVR)
            p = jnp.exp2(score[b] * SHARP - top * SHARP)
            total = total + jnp.sum(p, axis=1, keepdims=True)
            mixed = mixed + mm(p.astype(BF), keys)
        acc_s[base : base + 2 * m, :] = mixed
        max_s[base : base + 2 * m, :] = jnp.broadcast_to(top, (2 * m, 128))
        sum_s[base : base + 2 * m, :] = jnp.broadcast_to(total, (2 * m, 128))
        groups[h] = (base, m, slots)

    def new_keys(h):
        base, m, slots = groups[h]
        both = slice(base, base + 2 * m)
        keys = lat_out[:, :, QR:LAT].reshape(TOK, KEY)
        row = lax.broadcasted_iota(jnp.int32, (ROWS, 1), 0)
        when = jnp.concatenate([row + s * ROWS for s in slots] * 2, axis=0)
        score = mm(qs[both, :], keys, NT)
        score = jnp.where(lax.broadcasted_iota(jnp.int32, score.shape, 1) <= when, score, -jnp.inf)
        top = max_s[both, 0:1]
        new = jnp.maximum(top, jnp.max(score, axis=1, keepdims=True))
        fade = jnp.exp2(top * SHARP - new * SHARP)
        p = jnp.exp2(score * SHARP - new * SHARP)
        total = sum_s[both, 0:1] * fade + jnp.sum(p, axis=1, keepdims=True)
        mixed = acc_s[both, :] * fade + mm(p.astype(BF), keys[:, 0:KVR])
        mixed = (mixed / total).astype(BF)
        for k in range(2):
            val = mm(mixed[k * m : (k + 1) * m], wuv[k]).astype(BF)
            for i, s in enumerate(slots):
                there = pl.ds(pl.multiple_of(s * ROWS, ROWS), ROWS)
                out_ref[there, 128 * k : 128 * (k + 1)] = val[ROWS * i : ROWS * (i + 1)]

    finish_gather = all_gather("o", net, at, lat_part)
    next(finish_gather)
    for _ in prefix:
        pass
    for h in range(5):
        sib_rows("p", net, at, pre_part, h)
    for h in finish_gather:
        if h is not None:
            queries(h)
    for h in range(5):
        new_keys(h)
    net.drain()


SHARP = float((NOPE + ROPE) ** (-0.5) * np.log2(np.e))


def trig_table():
    half = ROPE // 2
    frequency = 10000.0 ** (-np.arange(half) / half)
    angles = (CACHE + np.arange(TOK))[:, None] * frequency[None, :].astype(np.float32)
    angles = angles.astype(np.float32).astype(np.float64)
    both = np.concatenate([np.cos(angles), np.sin(angles)], axis=1)
    return both.astype(np.float32)


def per_device(
    sections, tokens, expert_ids, gate_values, w_gate, w_up, w_down, norm_gain, w_dq, w_dkv, q_gain, kv_gain, w_uq, w_uk,
    w_uv, prefix_cache,
):
    vm = pl.BlockSpec(memory_space=pltpu.VMEM)
    anyw = pl.BlockSpec(memory_space=pl.ANY)
    V = pltpu.VMEM
    out = pl.pallas_call(
        functools.partial(relay_kernel, sections),
        name="relay",
        out_shape=jax.ShapeDtypeStruct((TOK, 256), BF),
        in_specs=[anyw, vm, vm, anyw, anyw, anyw, vm, anyw, anyw, vm, vm, vm, anyw, anyw, anyw, anyw],
        out_specs=vm,
        scratch_shapes=[
            V((32, ROWS, WIDE), BF),
            V((D, 2 * HID), BF),
            V((HID, D), BF),
            V((32, FB, HID), BF),
            V((16, FB, 2 * HID), BF),
            V((TOK, 2 * HID), BF),
            V((2 * HID, TOK), BF),
            V((384, TOK), BF),
            V((2, 4, 2, FB, TOK), BF),
            V((2, 4, 2, FB, TOK), BF),
            V((8, FB, TOK), BF),
            V((8, FB, TOK), BF),
            V((FB, TOK), BF),
            V((FB, TOK // 2), BF),
            V((FB, TOK), BF),
            V((2, FB, QR), BF),
            V((2, FB, KEY), BF),
            V((TOK // 2, LATW), F32),
            V((2, 4, 2, ROWS, LATW), BF),
            V((2, 4, 2, ROWS, LATW), BF),
            V((8, ROWS, LATW), BF),
            V((8, ROWS, LATW), BF),
            V((32, ROWS, LATW), BF),
            V((32, PRE, KEY), BF),
            V((2, 384, 128), F32),
            V((QR, 384), BF),
            V((2, NOPE, KVR), BF),
            V((2, KVR, 128), BF),
            V((2 * TOK, KEY), BF),
            V((2 * TOK, KVR), F32),
            V((2 * TOK, 128), F32),
            V((2 * TOK, 128), F32),
            pltpu.SemaphoreType.DMA((256,)),
            pltpu.SemaphoreType.DMA((256,)),
            pltpu.SemaphoreType.DMA((16,)),
        ],
        compiler_params=pltpu.CompilerParams(collective_id=0, has_side_effects=True, vmem_limit_bytes=60 << 20),
        cost_estimate=pl.CostEstimate(flops=12 * 10**9, bytes_accessed=12 * 10**6, transcendentals=4 * 10**6),
    )(
        tokens[0], expert_ids[0].T, gate_values[0].T, w_gate[0], w_up[0], w_down[0], norm_gain, w_dq[0], w_dkv[0],
        q_gain, kv_gain, jnp.asarray(trig_table().reshape(32, ROWS, ROPE)), prefix_cache[0], w_uq[0], w_uk[0], w_uv[0],
    )
    return out[None]


def solution(mesh):
    placed = (
        P("section", "expert", None),
        P("section", "expert", None),
        P("section", "expert", None),
        P("section", None, "expert"),
        P("section", None, "expert"),
        P("section", "expert", None),
        P("section", None),
        P("section", "expert", None),
        P("section", "expert", None),
        P("section", None),
        P("section", None),
        P("section", None, "expert"),
        P("section", "expert", None, None),
        P("section", "expert", None, None),
        P("section", "expert", None),
    )
    return jax.shard_map(
        functools.partial(per_device, mesh.shape["section"]),
        mesh=mesh,
        in_specs=placed,
        out_specs=P("section", None, "expert"),
        check_vma=False,
    )
```

```python
import functools

import jax
import jax.numpy as jnp
import numpy as np
from jax import lax
from jax.experimental import pallas as pl
from jax.experimental.pallas import tpu as pltpu
from jax.sharding import PartitionSpec as P

MESH = pl.DeviceIdType.MESH
COPIES = 107
SENDS = 11
REUSED = {"o": "t", "l": "m"}
BF = jnp.bfloat16
F32 = jnp.float32
EPSILON = 1e-06
D = 7168
ROWS = 16
SIDE = 128
WIDE = D + SIDE
HID = 128
QR = 1536
KVR = 512
ROPE = 64
NOPE = 128
KEY = KVR + ROPE
LAT = QR + KEY
LATW = 2176
FB = 224
TOK = 512
CACHE = 2048
PRE = 64
KT = (((1,), (0,)), ((), ()))
NT = (((1,), (1,)), ((), ()))
TN = (((0,), (0,)), ((), ()))


def mm(a, b, dims=KT):
    return lax.dot_general(a, b, dims, preferred_element_type=F32)


class Net:
    def __init__(self, send_sems, recv_sems, places):
        self.send_sems, self.recv_sems, self.places = send_sems, recv_sems, places
        self.ids, self.groups = {}, {}

    def copy(self, key, src, dst, place, group="t"):
        same = (REUSED.get(key[0], key[0]),) + key[1:]
        index = self.ids.setdefault(same, len(self.ids))
        return pltpu.make_async_remote_copy(
            src_ref=src,
            dst_ref=dst,
            send_sem=self.send_sems.at[self.groups.setdefault(group, len(self.groups))],
            recv_sem=self.recv_sems.at[index],
            device_id=self.places[place],
            device_id_type=MESH,
        )

    def send(self, key, src, dst, place):
        self.copy(key, src, dst, place, key[0]).start()

    def wait(self, key, ref):
        self.copy(key, ref, ref, "sib").wait_recv()

    def sent(self, group, ref):
        self.copy(("t", "xA"), ref, ref, "sib", group).wait_send()


class Hops:
    def __init__(self, ref):
        self.ref, self.at = ref, self

    def __getitem__(self, index):
        first = index[0] * 8 + index[1] * 2
        return self.ref.at[first + index[2]] if len(index) == 3 else self.ref.at[pl.ds(first, 2)]


DIRS = (("R", -1), ("L", 1))


def all_gather(n, net, slot, part):
    def pass_on(key, s, what, place):
        net.send(key, part(s, what), part(s, what), place)

    me, mate = slot(0, 0, 0), slot(1, 0, 0)
    pass_on((n, "xA"), me, "A", "xp")
    for what in "BA":
        for way, _ in DIRS:
            pass_on((n, what, way, 1), me, what, way)
    pass_on((n, "xB", "", 0), me, "B", "xp")
    pass_on((n, "s0", "", 0), me, "F", "sib")
    yield []
    net.wait((n, "xA"), part(mate, "A"))
    for way, _ in DIRS:
        pass_on((n, "A1", way, 1), mate, "A", way)
    net.wait((n, "xB", "", 0), part(mate, "B"))
    pass_on((n, "s1", "", 0), mate, "F", "sib")

    def finish(h):
        if h < 4:
            for way, sign in DIRS:
                s = slot(1, sign * h, 0)
                net.wait((n, "xB", way, h), part(s, "B"))
                pass_on((n, "s1", way, h), s, "F", "sib")
        else:
            s = slot(1, 4, 0)
            net.wait((n, "xB", "R", 4), part(s, "B1"))
            net.wait((n, "xB", "L", 4), part(s, "B2"))
            pass_on((n, "s1", "R", 4), s, "F", "sib")

    for h in range(1, 5):
        for way, sign in DIRS:
            s = slot(0, sign * h, 0)
            half = "B1" if way == "R" else "B2"
            if h < 4:
                net.wait((n, "B", way, h), part(s, "B"))
                pass_on((n, "B", way, h + 1), s, "B" if h < 3 else half, way)
                pass_on((n, "xB", way, h), s, "B", "xp")
            else:
                net.wait((n, "B", way, 4), part(s, half))
                pass_on((n, "xB", way, 4), s, half, "xp")
        if h >= 2:
            finish(h - 1)
        for way, sign in DIRS:
            if h < 4 or way == "R":
                s = slot(0, sign * h, 0)
                net.wait((n, "A", way, h), part(s, "A"))
                if h < 3 or (h == 3 and way == "R"):
                    pass_on((n, "A", way, h + 1), s, "A", way)
                pass_on((n, "s0", way, h), s, "F", "sib")
        yield [(0, h - 1)] + ([(1, h - 2)] if h > 1 else [])
        for way, sign in DIRS:
            if h < 4 or way == "L":
                s = slot(1, sign * h, 0)
                net.wait((n, "A1", way, h), part(s, "A"))
                if h < 3 or (h == 3 and way == "L"):
                    pass_on((n, "A1", way, h + 1), s, "A", way)
    yield [(0, 4), (1, 3)]
    finish(4)
    yield [(1, 4)]


def sib_rows(n, net, slot, part, group):
    slots = []
    for dx, h in group:
        for way, sign in DIRS if 0 < h < 4 else (("" if h == 0 else "R", 1),):
            net.wait((n, f"s{dx}", way, h), part(slot(dx, sign * h, 1), "F"))
            slots += [slot(dx, sign * h, 0), slot(dx, sign * h, 1)]
    return slots


def reduce_scatter(n, net, value, cut, ms, mr, xs, xr, joined=False):
    order = [4, 3, -3, 2, -2, 1, -1, 0]

    def put(key, buf, there, what, val, place):
        cut(buf, what)[...] = val.astype(BF)
        net.send(key, cut(buf, what), cut(there, what), place)

    def got(key, buf, what):
        net.wait(key, cut(buf, what))
        return cut(buf, what)[...].astype(F32)

    last = ("B",) if joined else ("B1", "B2")
    trips = [(0, 1), (1, 2), (3, 2), (5, 2), (7, 1)] if joined else [(k, 1) for k in range(8)]

    def over_x(j):
        if j < len(trips):
            k, count = trips[j]
            for i in range(k, k + count):
                cut(xs.at[i], "B")[...] = value(1, order[i], "B").astype(BF)
            there = pl.ds(k, count)
            if count == 1:
                there = k
            net.send((n, "x", k), cut(xs.at[there], "B"), cut(xr.at[there], "B"), "xp")

    def from_x(i):
        for j, (k, count) in enumerate(trips):
            if k == i:
                net.wait((n, "x", k), cut(xr.at[pl.ds(k, count) if count > 1 else k], "B"))
                over_x(j + 3)

    def hop_a(h):
        for d in (1, 0):
            for w, way in enumerate("RL"):
                if h == 1 and w != d:
                    continue
                val = value(d, (5 - h) * (1 if way == "R" else -1), "A")
                if h > 2 or (h == 2 and w == d):
                    val = val + got((n, "A", way, h - 1, d), mr.at[w, h - 2, d], "A")
                put((n, "A", way, h, d), ms.at[w, h - 1, d], mr.at[w, h - 1, d], "A", val, way)

    def hop_b(h):
        for w, (way, half, rest) in enumerate((("R", "B1", "B2"), ("L", "B2", "B1"))):
            dz = (5 - h) * (1 if way == "R" else -1)
            k = order.index(dz if h > 1 else 4)
            if h > 1 or w == 0:
                from_x(k)
            buf, there = ms.at[w, h - 1, 0], mr.at[w, h - 1, 0]
            if h == 1:
                val = value(0, 4, half) + cut(xr.at[k], half)[...].astype(F32)
                put((n, "B", way, 1), buf, there, half, val, way)
            elif h == 2:
                val = value(0, dz, rest) + cut(xr.at[k], rest)[...].astype(F32)
                cut(buf, rest)[...] = val.astype(BF)
                val = value(0, dz, half) + cut(xr.at[k], half)[...].astype(F32)
                val = val + got((n, "B", way, 1), mr.at[w, 0, 0], half)
                cut(buf, half)[...] = val.astype(BF)
                net.send((n, "B", way, h), cut(buf, "B"), cut(there, "B"), way)
            else:
                net.wait((n, "B", way, h - 1), cut(mr.at[w, h - 2, 0], "B"))
                for what in last if h == 4 else ("B",):
                    val = value(0, dz, what) + cut(xr.at[k], what)[...].astype(F32)
                    val = val + cut(mr.at[w, h - 2, 0], what)[...].astype(F32)
                    put((n, "B2" if what == "B2" else "B", way, h), buf, there, what, val, way)

    over_x(0)
    hop_a(1)
    over_x(1)
    over_x(2)
    yield 1
    for h in range(2, 5):
        hop_a(h)
        hop_b(h - 1)
        yield h
    val = value(1, 0, "A")
    for w, way in enumerate("RL"):
        val = val + got((n, "A", way, 4, 1), mr.at[w, 3, 1], "A")
    put((n, "xA"), xs.at[7], xr.at[7], "A", val, "xp")
    hop_b(4)
    yield 5
    own = value(0, 0, "A")
    for w, way in enumerate("RL"):
        own = own + got((n, "A", way, 4, 0), mr.at[w, 3, 0], "A")
    yield "A", own + got((n, "xA"), xr.at[7], "A")
    from_x(7)
    for what in last:
        val = value(0, 0, what) + cut(xr.at[7], what)[...].astype(F32)
        for w, way in enumerate("RL"):
            val = val + got((n, "B2" if what == "B2" else "B", way, 4), mr.at[w, 3, 0], what)
        yield what, val


def last_cut(ref, a, b):
    return ref.at[..., pl.ds(a, b - a)]


TOK_CUTS = {"A": (0, 3456), "B": (3456, WIDE), "B1": (3456, 5376), "B2": (5376, WIDE), "F": (0, WIDE)}
LAT_CUTS = {"A": (0, 1024), "B": (1024, LATW), "B1": (1024, 1664), "B2": (1664, LATW), "F": (0, LATW)}
MIX_CUTS = {"A": (0, 96), "B": (96, 224), "B1": (96, 160), "B2": (160, 224), "F": (0, 224)}


def relay_kernel(
    sections,
    tok_ref, ids_ref, gates_ref, wg_ref, wu_ref, wd_ref, gain_ref, wq_ref, wk_ref, qg_ref, kg_ref, trig_ref, pre_ref,
    wuq_ref, wuk_ref, wuv_ref,
    out_ref,
    buf, wgu, wdn, wt, wdt, hid, hidt, toks_t, ms, mr, xs, xr, arr, arr_s, wqs, wks, lat,
    ms2, mr2, xs2, xr2, lat_out, pre_out, gcol, wuq, wuk, wuv, wx, kx, vx, qs, acc_s, max_s, sum_s, send_sems, recv_sems, local_sems,
):
    sec, e = lax.axis_index("section"), lax.axis_index("expert")
    xh, z, c = e // 16, (e // 2) % 8, e % 2

    turn = 1 - 2 * c

    def column(dz, dc=0):
        return (z + turn * (-dz if dc else dz) + 8) % 8

    def at(dx, dz, dc):
        return (xh + dx) % 2 * 16 + column(dz, dc) * 2 + (c + dc) % 2

    places = {
        "R": (sec, at(0, 1, 0)),
        "L": (sec, at(0, -1, 0)),
        "xp": (sec, at(1, 0, 0)),
        "sib": (sec, at(0, 0, 1)),
        "next": ((sec + 1) % sections, e),
        "next sib": ((sec + 1) % sections, at(0, 0, 1)),
        "prev": ((sec + sections - 1) % sections, e),
        "prev sib": ((sec + sections - 1) % sections, at(0, 0, 1)),
    }
    net = Net(send_sems, recv_sems, places)
    all_blocks, all_rows = ms.at[pl.ds(0, 15)], ms2.at[pl.ds(0, 15)]
    ms, mr, ms2, mr2 = (Hops(r) for r in (ms, mr, ms2, mr2))
    local = []

    def fetch(k, src, dst):
        cp = pltpu.make_async_copy(src, dst, local_sems.at[k])
        cp.start()
        local.append(cp)
        return cp

    def slot(dx, dz, dc):
        return (c + dc) % 2 * 16 + (xh + dx) % 2 * 8 + column(dz, dc)

    me = slot(0, 0, 0)
    own = fetch(0, tok_ref, buf.at[me, :, pl.ds(0, D)])
    load_g = fetch(1, wg_ref, wgu.at[:, pl.ds(0, HID)])
    load_u = fetch(2, wu_ref, wgu.at[:, pl.ds(HID, HID)])
    load_d = fetch(3, wd_ref, wdn)
    load_q = fetch(4, wq_ref, wqs.at[0])
    load_k = fetch(5, wk_ref, wks.at[0])
    load_p = fetch(6, pre_ref, pre_out.at[c, xh * 8 + z])
    load_uq = fetch(8, wuq_ref, wuq)
    load_uk = fetch(9, wuk_ref, wuk)
    load_uv = fetch(10, wuv_ref, wuv)

    barrier = pltpu.get_barrier_semaphore()
    for there in places.values():
        pl.semaphore_signal(barrier, inc=1, device_id=there, device_id_type=MESH)

    lane = lax.broadcasted_iota(jnp.int32, (ROWS, SIDE), 1)
    diag = lax.broadcasted_iota(jnp.int32, (ROWS, ROWS), 0) == lax.broadcasted_iota(jnp.int32, (ROWS, ROWS), 1)
    g = jnp.zeros((ROWS, SIDE), F32)
    for k in range(2):
        chosen = jnp.sum(jnp.where(diag, ids_ref[k : k + 1, :], 0), axis=1, keepdims=True)
        weight = jnp.sum(jnp.where(diag, gates_ref[k : k + 1, :], 0.0), axis=1, keepdims=True)
        g = g + jnp.where(chosen == lane % 4, weight, 0.0)
    high = g.astype(BF)
    low = (g - high.astype(F32)).astype(BF)
    side = jnp.where(lane < 4, high.astype(F32), jnp.where(lane < 8, low.astype(F32), 0.0)).astype(BF)
    buf[me, :, D:WIDE] = side

    pl.semaphore_wait(barrier, len(places))
    own.wait()

    def tok_part(s, what):
        return last_cut(buf.at[s], *TOK_CUTS[what])

    expert = e // 8
    gather = all_gather("t", net, slot, tok_part)
    next(gather)
    load_q.wait()
    net.send(("wq",), wqs.at[0], wqs.at[1], "sib")
    load_k.wait()
    net.send(("wk",), wks.at[0], wks.at[1], "sib")

    def window(owner):
        return jnp.minimum(FB * owner // 128 * 128, D - 384)

    for i in range(2):
        first = window(at(0, 0, i))
        piece = gain_ref[0:1, pl.ds(pl.multiple_of(first, 128), 384)]
        gcol[i] = jnp.broadcast_to(piece, (128, 384)).T
    load_d.wait()
    for k in range(8):
        wt[4 * k : 4 * k + 4] = wdn[:, 896 * k : 896 * (k + 1)].T.reshape(4, FB, HID)

    half = pl.ds(pl.multiple_of(c * HID, HID), HID)
    pairs = wt.reshape(16, 2, FB, HID)
    net.send(("wd",), pairs.at[:, (c + 1) % 2], wdt.at[:, :, half], "sib")
    keep_d = fetch(7, pairs.at[:, c], wdt.at[:, :, half])

    load_g.wait()
    load_u.wait()

    def experts(group):
        slots = sib_rows("t", net, slot, tok_part, group)
        m = len(slots) * ROWS
        acc = jnp.zeros((m, 2 * HID), F32)
        for k in range(7):
            rows = jnp.concatenate([buf[s, :, 1024 * k : 1024 * (k + 1)] for s in slots], axis=0)
            acc = acc + mm(rows, wgu[1024 * k : 1024 * (k + 1), :])
        side = jnp.concatenate([buf[s, :, D:WIDE] for s in slots], axis=0).astype(F32)
        lane = lax.broadcasted_iota(jnp.int32, (m, SIDE), 1)
        gate = jnp.sum(jnp.where((lane % 4 == expert) & (lane < 8), side, 0.0), axis=1, keepdims=True)
        gp, up = acc[:, :HID], acc[:, HID:]
        val = (gp / (1.0 + jnp.exp(-gp)) * up * gate).astype(BF)
        for i, s in enumerate(slots):
            hid[pl.ds(pl.multiple_of(s * ROWS, ROWS), ROWS), half] = val[ROWS * i : ROWS * (i + 1)]

    def gather_prefix():
        def chunk(dx, dz):
            return pre_out.at[c, (xh + dx) % 2 * 8 + column(dz)]

        def pass_on(key, ref, place):
            net.send(key, ref, ref, place)

        def hop(d, h):
            for way, sign in DIRS:
                if h < 4 or (way == "R") == (d == 0):
                    if h > 0:
                        net.wait(("p", d, way, h), chunk(d, sign * h))
                    if h < 3 or (h == 3 and (way == "R") == (d == 0)):
                        pass_on(("p", d, way, h + 1), chunk(d, sign * h), way)

        hop(0, 0)
        pass_on(("p", "x"), chunk(0, 0), "xp")
        yield
        hop(0, 1)
        yield
        net.wait(("p", "x"), chunk(1, 0))
        hop(1, 0)
        yield
        for d, h in ((0, 2), (0, 3), (1, 1), (0, 4), (1, 2), (1, 3), (1, 4)):
            hop(d, h)
            yield
        pass_on(("all", "sib"), pre_out.at[c], "sib")
        yield
        net.wait(("all", "sib"), pre_out.at[(c + 1) % 2])

    prefix = gather_prefix()

    def ticks(count):
        for _ in range(count):
            next(prefix, None)

    for group in gather:
        if group == [(0, 3), (1, 2)]:
            load_p.wait()
            ticks(1)
        if group == [(1, 4)]:
            ticks(1)
        experts(group)
    net.send(("hid",), hid.at[:, half], hid.at[:, half], "sib")
    ticks(1)

    start = window(e)
    toks_t[...] = buf[:, :, pl.ds(pl.multiple_of(start, 128), 384)].reshape(TOK, 384).T

    load_uk.wait()
    load_uv.wait()
    for k in range(2):
        wx[:, 128 * k : 128 * (k + 1)] = wuv[k]

    other = pl.ds(pl.multiple_of((c + 1) % 2 * HID, HID), HID)
    net.wait(("hid",), hid.at[:, other])
    net.wait(("wd",), wdt.at[:, :, other])
    keep_d.wait()
    hidt[...] = hid[...].T

    def mixed_term(dx, dz, what):
        a, b = MIX_CUTS[what]
        block = (xh + dx) % 2 * 8 + column(dz)
        return mm(wdt[block, a:b, :], hidt[...])

    def mix_cut(ref, what):
        a, b = MIX_CUTS[what]
        return ref.at[pl.ds(a, b - a)]

    off = FB * e - start
    for got in reduce_scatter("m", net, mixed_term, mix_cut, ms, mr, xs, xr):
        if not isinstance(got, tuple):
            ticks({1: 1, 5: 2}.get(got, 0))
            continue
        what, val = got
        a, b = MIX_CUTS[what]
        rows = toks_t[pl.ds(pl.multiple_of(off + a, 16), b - a), :].astype(F32)
        arr_s[a:b] = (val + rows).astype(BF)
        for i, place in enumerate(("next", "next sib")):
            tokens_of = pl.ds(pl.multiple_of((c + i) % 2 * 256, 256), 256)
            block = arr_s.at[pl.ds(a, b - a), tokens_of]
            net.send(("next", i, what), block, arr.at[i, pl.ds(a, b - a)], place)

    ticks(2)
    net.wait(("wq",), wqs.at[1])
    net.wait(("wk",), wks.at[1])
    squares = jnp.zeros((1, 256), F32)
    for i in range(2):
        for what in ("A", "B1", "B2"):
            net.wait(("next", i, what), mix_cut(arr.at[i], what))
        x = arr[i].astype(F32)
        squares = squares + jnp.sum(x * x, axis=0, keepdims=True)
        shift = FB * at(0, 0, i) - window(at(0, 0, i))
        scaled = (x * gcol[i, pl.ds(pl.multiple_of(shift, 32), FB), 0:1]).T.astype(BF)
        if i == 0:
            lat[:, 0:QR] = mm(scaled, wqs[0])
            lat[:, QR:LAT] = mm(scaled, wks[0])
        else:
            lat[:, 0:QR] += mm(scaled, wqs[1])
            lat[:, QR:LAT] += mm(scaled, wks[1])
    lat[:, LAT:LATW] = jnp.broadcast_to(squares, (128, 256)).T[:, 0 : LATW - LAT]

    def lat_term(dx, dz, what):
        a, b = LAT_CUTS[what]
        block = (xh + dx) % 2 * 8 + column(dz)
        return lat[pl.ds(pl.multiple_of(block * ROWS, ROWS), ROWS), a:b]

    def lat_cut(ref, what):
        return last_cut(ref, *LAT_CUTS[what])

    ticks(1)
    sums = {}
    for got in reduce_scatter("l", net, lat_term, lat_cut, ms2, mr2, xs2, xr2, True):
        if isinstance(got, tuple):
            sums[got[0]] = got[1]
        elif got == 3:
            ticks(2)
    total = jnp.concatenate([sums["A"], sums["B"]], axis=1)
    scale = lax.rsqrt(total[:, LAT : LAT + 1] * (1.0 / D) + EPSILON)

    def rms(v, gain):
        v = v * scale
        return (v * lax.rsqrt(jnp.mean(v * v, axis=1, keepdims=True) + EPSILON) * gain).astype(BF)

    lat_out[e, :, 0:QR] = rms(total[:, 0:QR], qg_ref[...])
    lat_out[e, :, QR : QR + KVR] = rms(total[:, QR : QR + KVR], kg_ref[...])
    tail = total[:, QR + KVR :] * scale
    first, second = tail[:, 0:32], tail[:, 32:64]
    cos, sin = trig_ref[e, :, 0:32], trig_ref[e, :, 32:64]
    turned = jnp.concatenate([first * cos - second * sin, first * sin + second * cos], axis=1)
    lat_out[e, :, QR + KVR : LAT] = turned.astype(BF)
    lat_out[e, :, LAT:LATW] = jnp.zeros((ROWS, LATW - LAT), BF)

    def lat_part(s, what):
        return last_cut(lat_out.at[s], *LAT_CUTS[what])

    load_uq.wait()
    order = []

    def expand(first, rows):
        there = slice(first, first + 512)
        values = mm(rows[:, 0:KVR], wx[...]).astype(BF)
        for k in range(2):
            kx[k, 0:NOPE, there] = mm(wuk[k], rows[:, 0:KVR], NT).astype(BF)
            kx[k, NOPE:, there] = rows[:, KVR:KEY].T
            vx[k, there, :] = values[:, 128 * k : 128 * (k + 1)]

    def queries(group):
        slots = sib_rows("o", net, at, lat_part, group)
        m = len(slots) * ROWS
        base = len(order) * ROWS
        order.extend(slots)
        mine = slice(base, base + m)
        angle = jnp.concatenate([trig_ref[s] for s in slots], axis=0)
        cos, sin = angle[:, 0:32], angle[:, 32:64]
        q = mm(jnp.concatenate([lat_out[s, :, 0:QR] for s in slots], axis=0), wuq[...]) * SHARP
        for k in range(2):
            a = k * (NOPE + ROPE)
            first, second = q[:, a + NOPE : a + NOPE + 32], q[:, a + NOPE + 32 : a + NOPE + 64]
            turned = jnp.concatenate([first * cos - second * sin, first * sin + second * cos], axis=1)
            qs[k, mine, 0:NOPE] = q[:, a : a + NOPE].astype(BF)
            qs[k, mine, NOPE:] = turned.astype(BF)
        both = range(2)
        score = [[mm(qs[k, mine, :], kx[k, :, 512 * b : 512 * (b + 1)]) for b in range(4)] for k in both]
        top = [functools.reduce(jnp.maximum, [jnp.max(x, axis=1, keepdims=True) for x in score[k]]) for k in both]
        for k in both:
            total, mixed = 0.0, 0.0
            for b in range(4):
                p = jnp.exp2(score[k][b] - top[k])
                total = total + jnp.sum(p, axis=1, keepdims=True)
                mixed = mixed + mm(p.astype(BF), vx[k, 512 * b : 512 * (b + 1), :])
            acc_s[k, mine, :] = mixed
            max_s[k, mine, :] = jnp.broadcast_to(top[k], (m, 128))
            sum_s[k, mine, :] = jnp.broadcast_to(total, (m, 128))

    def new_keys():
        row = lax.broadcasted_iota(jnp.int32, (ROWS, 1), 0)
        when = jnp.concatenate([row + s * ROWS for s in order], axis=0)
        key_when = lax.broadcasted_iota(jnp.int32, (1, TOK), 1)
        pieces = [(k, slice(256 * i, 256 * (i + 1))) for i in range(2) for k in range(2)]
        score = [mm(qs[k, mine, :], kx[k, :, CACHE:]) for k, mine in pieces]
        score = [jnp.where(key_when <= when[mine], x, -jnp.inf) for x, (k, mine) in zip(score, pieces)]
        new = [jnp.maximum(max_s[k, mine, 0:1], jnp.max(x, axis=1, keepdims=True)) for x, (k, mine) in zip(score, pieces)]
        for (k, mine), x, top in zip(pieces, score, new):
            fade = jnp.exp2(max_s[k, mine, 0:1] - top)
            p = jnp.exp2(x - top)
            total = sum_s[k, mine, 0:1] * fade + jnp.sum(p, axis=1, keepdims=True)
            mixed = acc_s[k, mine, :] * fade + mm(p.astype(BF), vx[k, CACHE:, :])
            val = (mixed * (1.0 / total)).astype(BF)
            for j, s in enumerate(order[mine.start // ROWS : mine.stop // ROWS]):
                there = pl.ds(pl.multiple_of(s * ROWS, ROWS), ROWS)
                out_ref[there, 128 * k : 128 * (k + 1)] = val[ROWS * j : ROWS * (j + 1)]

    finish_gather = all_gather("o", net, at, lat_part)
    next(finish_gather)
    ticks(1)
    for b in range(4):
        expand(512 * b, pre_out[b // 2, b % 2 * 8 : b % 2 * 8 + 8].reshape(512, KEY))
    for group in finish_gather:
        queries(group)
    expand(CACHE, lat_out[:, :, QR:LAT].reshape(TOK, KEY))
    new_keys()
    for group, ref in (
        ("t", buf.at[pl.ds(0, 31)]),
        ("o", lat_out.at[pl.ds(0, 31)]),
        ("m", all_blocks),
        ("l", all_rows),
        ("p", pre_out.at[0, pl.ds(0, 15)]),
        ("all", pre_out.at[0]),
        ("next", arr_s),
        ("wq", wqs.at[0]),
        ("wk", wks.at[0]),
        ("wd", wdt.at[:, :, half]),
        ("hid", hid.at[:, half]),
    ):
        net.sent(group, ref)
    assert (len(net.ids), len(net.groups)) == (COPIES, SENDS)


SHARP = float((NOPE + ROPE) ** (-0.5) * np.log2(np.e))


def trig_table():
    half = ROPE // 2
    frequency = 10000.0 ** (-np.arange(half) / half)
    angles = (CACHE + np.arange(TOK))[:, None] * frequency[None, :].astype(np.float32)
    angles = angles.astype(np.float32).astype(np.float64)
    both = np.concatenate([np.cos(angles), np.sin(angles)], axis=1)
    return both.astype(np.float32)


def per_device(
    sections, tokens, expert_ids, gate_values, w_gate, w_up, w_down, norm_gain, w_dq, w_dkv, q_gain, kv_gain, w_uq, w_uk,
    w_uv, prefix_cache,
):
    vm = pl.BlockSpec(memory_space=pltpu.VMEM)
    anyw = pl.BlockSpec(memory_space=pl.ANY)
    V = pltpu.VMEM
    out = pl.pallas_call(
        functools.partial(relay_kernel, sections),
        name="relay",
        out_shape=jax.ShapeDtypeStruct((TOK, 256), BF),
        in_specs=[anyw, vm, vm, anyw, anyw, anyw, vm, anyw, anyw, vm, vm, vm, anyw, anyw, anyw, anyw],
        out_specs=vm,
        scratch_shapes=[
            V((32, ROWS, WIDE), BF),
            V((D, 2 * HID), BF),
            V((HID, D), BF),
            V((32, FB, HID), BF),
            V((16, FB, 2 * HID), BF),
            V((TOK, 2 * HID), BF),
            V((2 * HID, TOK), BF),
            V((384, TOK), BF),
            V((16, FB, TOK), BF),
            V((16, FB, TOK), BF),
            V((8, FB, TOK), BF),
            V((8, FB, TOK), BF),
            V((2, FB, TOK // 2), BF),
            V((FB, TOK), BF),
            V((2, FB, QR), BF),
            V((2, FB, KEY), BF),
            V((TOK // 2, LATW), F32),
            V((16, ROWS, LATW), BF),
            V((16, ROWS, LATW), BF),
            V((8, ROWS, LATW), BF),
            V((8, ROWS, LATW), BF),
            V((32, ROWS, LATW), BF),
            V((2, 16, PRE, KEY), BF),
            V((2, 384, 128), F32),
            V((QR, 384), BF),
            V((2, NOPE, KVR), BF),
            V((2, KVR, 128), BF),
            V((KVR, 256), BF),
            V((2, NOPE + ROPE, CACHE + TOK), BF),
            V((2, CACHE + TOK, 128), BF),
            V((2, TOK, NOPE + ROPE), BF),
            V((2, TOK, 128), F32),
            V((2, TOK, 128), F32),
            V((2, TOK, 128), F32),
            pltpu.SemaphoreType.DMA((SENDS,)),
            pltpu.SemaphoreType.DMA((COPIES,)),
            pltpu.SemaphoreType.DMA((11,)),
        ],
        compiler_params=pltpu.CompilerParams(collective_id=0, has_side_effects=True, vmem_limit_bytes=60 << 20),
        cost_estimate=pl.CostEstimate(flops=12 * 10**9, bytes_accessed=12 * 10**6, transcendentals=4 * 10**6),
    )(
        tokens[0], expert_ids[0].T, gate_values[0].T, w_gate[0], w_up[0], w_down[0], norm_gain, w_dq[0], w_dkv[0],
        q_gain, kv_gain, jnp.asarray(trig_table().reshape(32, ROWS, ROPE)), prefix_cache[0], w_uq[0], w_uk[0], w_uv[0],
    )
    return out[None]


def solution(mesh):
    placed = (
        P("section", "expert", None),
        P("section", "expert", None),
        P("section", "expert", None),
        P("section", None, "expert"),
        P("section", None, "expert"),
        P("section", "expert", None),
        P("section", None),
        P("section", "expert", None),
        P("section", "expert", None),
        P("section", None),
        P("section", None),
        P("section", None, "expert"),
        P("section", "expert", None, None),
        P("section", "expert", None, None),
        P("section", "expert", None),
    )
    return jax.shard_map(
        functools.partial(per_device, mesh.shape["section"]),
        mesh=mesh,
        in_specs=placed,
        out_specs=P("section", None, "expert"),
        check_vma=False,
    )
```

```python
import functools

import jax
import jax.numpy as jnp
import numpy as np
from jax import lax
from jax.experimental import pallas as pl
from jax.experimental.pallas import tpu as pltpu
from jax.sharding import PartitionSpec as P

MESH = pl.DeviceIdType.MESH
COPIES = 107
SENDS = 11
REUSED = {"o": "t", "l": "m"}
BF = jnp.bfloat16
F32 = jnp.float32
EPSILON = 1e-06
D = 7168
ROWS = 16
SIDE = 128
WIDE = D + SIDE
HID = 128
QR = 1536
KVR = 512
ROPE = 64
NOPE = 128
KEY = KVR + ROPE
LAT = QR + KEY
LATW = 2176
FB = 224
TOK = 512
CACHE = 2048
PRE = 64
KT = (((1,), (0,)), ((), ()))
NT = (((1,), (1,)), ((), ()))
TN = (((0,), (0,)), ((), ()))


def mm(a, b, dims=KT):
    return lax.dot_general(a, b, dims, preferred_element_type=F32)


class Net:
    def __init__(self, send_sems, recv_sems, places):
        self.send_sems, self.recv_sems, self.places = send_sems, recv_sems, places
        self.ids, self.groups = {}, {}

    def copy(self, key, src, dst, place, group="t"):
        same = (REUSED.get(key[0], key[0]),) + key[1:]
        index = self.ids.setdefault(same, len(self.ids))
        return pltpu.make_async_remote_copy(
            src_ref=src,
            dst_ref=dst,
            send_sem=self.send_sems.at[self.groups.setdefault(group, len(self.groups))],
            recv_sem=self.recv_sems.at[index],
            device_id=self.places[place],
            device_id_type=MESH,
        )

    def send(self, key, src, dst, place):
        self.copy(key, src, dst, place, key[0]).start()

    def wait(self, key, ref):
        self.copy(key, ref, ref, "sib").wait_recv()

    def sent(self, group, ref):
        self.copy(("t", "xA"), ref, ref, "sib", group).wait_send()


class Hops:
    def __init__(self, ref):
        self.ref, self.at = ref, self

    def __getitem__(self, index):
        first = index[0] * 8 + index[1] * 2
        return self.ref.at[first + index[2]] if len(index) == 3 else self.ref.at[pl.ds(first, 2)]


DIRS = (("R", -1), ("L", 1))


def all_gather(n, net, slot, part):
    def pass_on(key, s, what, place):
        net.send(key, part(s, what), part(s, what), place)

    me, mate = slot(0, 0, 0), slot(1, 0, 0)
    pass_on((n, "xA"), me, "A", "xp")
    for what in "BA":
        for way, _ in DIRS:
            pass_on((n, what, way, 1), me, what, way)
    pass_on((n, "xB", "", 0), me, "B", "xp")
    pass_on((n, "s0", "", 0), me, "F", "sib")
    yield []

    net.wait((n, "xA"), part(mate, "A"))
    for way, _ in DIRS:
        pass_on((n, "A1", way, 1), mate, "A", way)
    net.wait((n, "xB", "", 0), part(mate, "B"))
    pass_on((n, "s1", "", 0), mate, "F", "sib")

    def finish(h):
        if h < 4:
            for way, sign in DIRS:
                s = slot(1, sign * h, 0)
                net.wait((n, "xB", way, h), part(s, "B"))
                pass_on((n, "s1", way, h), s, "F", "sib")
        else:
            s = slot(1, 4, 0)
            net.wait((n, "xB", "R", 4), part(s, "B1"))
            net.wait((n, "xB", "L", 4), part(s, "B2"))
            pass_on((n, "s1", "R", 4), s, "F", "sib")

    def second(h):
        for way, sign in DIRS:
            if h < 4 or way == "L":
                s = slot(1, sign * h, 0)
                net.wait((n, "A1", way, h), part(s, "A"))
                if h < 3 or (h == 3 and way == "L"):
                    pass_on((n, "A1", way, h + 1), s, "A", way)

    for h in range(1, 5):
        for way, sign in DIRS:
            s = slot(0, sign * h, 0)
            half = "B1" if way == "R" else "B2"
            if h < 4:
                net.wait((n, "B", way, h), part(s, "B"))
                pass_on((n, "B", way, h + 1), s, "B" if h < 3 else half, way)
                pass_on((n, "xB", way, h), s, "B", "xp")
            else:
                net.wait((n, "B", way, 4), part(s, half))
                pass_on((n, "xB", way, 4), s, half, "xp")
        if h > 1:
            finish(h - 1)
        for way, sign in DIRS:
            if h < 4 or way == "R":
                s = slot(0, sign * h, 0)
                net.wait((n, "A", way, h), part(s, "A"))
                if h < 3 or (h == 3 and way == "R"):
                    pass_on((n, "A", way, h + 1), s, "A", way)
                pass_on((n, "s0", way, h), s, "F", "sib")
        yield [(0, h - 1)] + ([(1, h - 2)] if h > 1 else [])
        if h < 4:
            second(h)
    second(4)
    yield [(0, 4), (1, 3)]
    finish(4)
    yield [(1, 4)]


def gather_far(n, net, slot, part):
    def pass_on(key, s, what, place):
        net.send(key, part(s, what), part(s, what), place)

    def both_ways(name, h, s, what):
        for way, _ in DIRS:
            pass_on((n, name, way, h), s, what, way + "2" if h == 2 else way)

    me, mate = slot(0, 0, 0), slot(1, 0, 0)
    pass_on((n, "xA"), me, "A", "xp")
    for what in "BA":
        both_ways(what, 2, me, what)
        both_ways(what, 1, me, what)
    pass_on((n, "xB", "", 0), me, "B", "xp")
    pass_on((n, "s0", "", 0), me, "F", "sib")
    yield []
    net.wait((n, "xA"), part(mate, "A"))
    both_ways("A1", 2, mate, "A")
    both_ways("A1", 1, mate, "A")
    net.wait((n, "xB", "", 0), part(mate, "B"))
    pass_on((n, "s1", "", 0), mate, "F", "sib")

    def ring_b(h):
        for way, sign in DIRS:
            s = slot(0, sign * h, 0)
            half = "B1" if way == "R" else "B2"
            what = "B" if h < 4 else half
            net.wait((n, "B", way, h), part(s, what))
            if h == 2:
                pass_on((n, "B", way, 3), s, "B", way)
                pass_on((n, "B", way, 4), s, half, way + "2")
            pass_on((n, "xB", way, h), s, what, "xp")

    def ring_a(name, h, d):
        for way, sign in DIRS:
            last = (way == "R") == (d == 0)
            if h < 4 or last:
                s = slot(d, sign * h, 0)
                net.wait((n, name, way, h), part(s, "A"))
                if h == 2:
                    pass_on((n, name, way, 3), s, "A", way)
                    if last:
                        pass_on((n, name, way, 4), s, "A", way + "2")
                if d == 0:
                    pass_on((n, "s0", way, h), s, "F", "sib")

    def finish(h):
        if h < 4:
            for way, sign in DIRS:
                s = slot(1, sign * h, 0)
                net.wait((n, "xB", way, h), part(s, "B"))
                pass_on((n, "s1", way, h), s, "F", "sib")
        else:
            s = slot(1, 4, 0)
            net.wait((n, "xB", "R", 4), part(s, "B1"))
            net.wait((n, "xB", "L", 4), part(s, "B2"))
            pass_on((n, "s1", "R", 4), s, "F", "sib")

    ring_b(1)
    ring_b(2)
    ring_a("A", 1, 0)
    ring_a("A", 2, 0)
    yield [(0, 0)]
    ring_a("A1", 1, 1)
    ring_a("A1", 2, 1)
    finish(1)
    finish(2)
    yield [(1, 0), (0, 1), (0, 2)]
    ring_b(3)
    ring_b(4)
    ring_a("A", 3, 0)
    ring_a("A", 4, 0)
    yield [(1, 1), (1, 2)]
    ring_a("A1", 3, 1)
    ring_a("A1", 4, 1)
    finish(3)
    yield [(0, 3), (0, 4)]
    finish(4)
    yield [(1, 3), (1, 4)]


def sib_rows(n, net, slot, part, group):
    slots = []
    for dx, h in group:
        for way, sign in DIRS if 0 < h < 4 else (("" if h == 0 else "R", 1),):
            net.wait((n, f"s{dx}", way, h), part(slot(dx, sign * h, 1), "F"))
            slots += [slot(dx, sign * h, 0), slot(dx, sign * h, 1)]
    return slots


def reduce_scatter(n, net, value, cut, ms, mr, xs, xr):
    order = [4, 3, -3, 2, -2, 1, -1, 0]

    def put(key, buf, there, what, val, place):
        cut(buf, what)[...] = val.astype(BF)
        net.send(key, cut(buf, what), cut(there, what), place)

    def got(key, buf, what):
        net.wait(key, cut(buf, what))
        return cut(buf, what)[...].astype(F32)

    last = ("B1", "B2")
    trips = [(k, 1) for k in range(8)]

    def over_x(j):
        if j < len(trips):
            k, count = trips[j]
            for i in range(k, k + count):
                cut(xs.at[i], "B")[...] = value(1, order[i], "B").astype(BF)
            there = pl.ds(k, count)
            if count == 1:
                there = k
            net.send((n, "x", k), cut(xs.at[there], "B"), cut(xr.at[there], "B"), "xp")

    def from_x(i):
        for j, (k, count) in enumerate(trips):
            if k == i:
                net.wait((n, "x", k), cut(xr.at[pl.ds(k, count) if count > 1 else k], "B"))
                over_x(j + 3)

    def hop_a(h):
        for d in (1, 0):
            for w, way in enumerate("RL"):
                if h == 1 and w != d:
                    continue
                val = value(d, (5 - h) * (1 if way == "R" else -1), "A")
                if h > 2 or (h == 2 and w == d):
                    val = val + got((n, "A", way, h - 1, d), mr.at[w, h - 2, d], "A")
                put((n, "A", way, h, d), ms.at[w, h - 1, d], mr.at[w, h - 1, d], "A", val, way)

    def hop_b(h):
        for w, (way, half, rest) in enumerate((("R", "B1", "B2"), ("L", "B2", "B1"))):
            dz = (5 - h) * (1 if way == "R" else -1)
            k = order.index(dz if h > 1 else 4)
            if h > 1 or w == 0:
                from_x(k)
            buf, there = ms.at[w, h - 1, 0], mr.at[w, h - 1, 0]
            if h == 1:
                val = value(0, 4, half) + cut(xr.at[k], half)[...].astype(F32)
                put((n, "B", way, 1), buf, there, half, val, way)
            elif h == 2:
                val = value(0, dz, rest) + cut(xr.at[k], rest)[...].astype(F32)
                cut(buf, rest)[...] = val.astype(BF)
                val = value(0, dz, half) + cut(xr.at[k], half)[...].astype(F32)
                val = val + got((n, "B", way, 1), mr.at[w, 0, 0], half)
                cut(buf, half)[...] = val.astype(BF)
                net.send((n, "B", way, h), cut(buf, "B"), cut(there, "B"), way)
            else:
                net.wait((n, "B", way, h - 1), cut(mr.at[w, h - 2, 0], "B"))
                for what in last if h == 4 else ("B",):
                    val = value(0, dz, what) + cut(xr.at[k], what)[...].astype(F32)
                    val = val + cut(mr.at[w, h - 2, 0], what)[...].astype(F32)
                    put((n, "B2" if what == "B2" else "B", way, h), buf, there, what, val, way)

    over_x(0)
    hop_a(1)
    over_x(1)
    over_x(2)
    yield 1
    for h in range(2, 5):
        hop_a(h)
        hop_b(h - 1)
        yield h
    val = value(1, 0, "A")
    for w, way in enumerate("RL"):
        val = val + got((n, "A", way, 4, 1), mr.at[w, 3, 1], "A")
    put((n, "xA"), xs.at[7], xr.at[7], "A", val, "xp")
    hop_b(4)
    yield 5
    own = value(0, 0, "A")
    for w, way in enumerate("RL"):
        own = own + got((n, "A", way, 4, 0), mr.at[w, 3, 0], "A")
    yield "A", own + got((n, "xA"), xr.at[7], "A")
    from_x(7)
    for what in last:
        val = value(0, 0, what) + cut(xr.at[7], what)[...].astype(F32)
        for w, way in enumerate("RL"):
            val = val + got((n, "B2" if what == "B2" else "B", way, 4), mr.at[w, 3, 0], what)
        yield what, val


def scatter_far(n, net, value, cut, ms, mr, xs, xr):
    order = [4, 3, -3, 2, -2, 1, -1, 0]
    trips = [(0, 1), (1, 2), (3, 2), (5, 2), (7, 1)]

    def put(key, buf, there, what, val, place):
        cut(buf, what)[...] = val.astype(BF)
        net.send(key, cut(buf, what), cut(there, what), place)

    def got(key, buf, what):
        net.wait(key, cut(buf, what))
        return cut(buf, what)[...].astype(F32)

    def over_x(j):
        if j < len(trips):
            k, count = trips[j]
            for i in range(k, k + count):
                cut(xs.at[i], "B")[...] = value(1, order[i], "B").astype(BF)
            there = pl.ds(k, count) if count > 1 else k
            net.send((n, "x", k), cut(xs.at[there], "B"), cut(xr.at[there], "B"), "xp")

    def from_x(j):
        k, count = trips[j]
        net.wait((n, "x", k), cut(xr.at[pl.ds(k, count) if count > 1 else k], "B"))
        over_x(j + 3)

    def place(way, h):
        return way + "2" if h in (1, 3) else way

    def send_a(h):
        for d in (1, 0):
            for w, way in enumerate("RL"):
                if h == 1 and w != d:
                    continue
                val = value(d, (5 - h) * (1 if way == "R" else -1), "A")
                if h == 3:
                    val = val + got((n, "A", way, 2, d), mr.at[w, 1, d], "A")
                    if w == d:
                        val = val + got((n, "A", way, 1, d), mr.at[w, 0, d], "A")
                put((n, "A", way, h, d), ms.at[w, h - 1, d], mr.at[w, h - 1, d], "A", val, place(way, h))

    def send_b(h):
        for w, (way, half, rest) in enumerate((("R", "B1", "B2"), ("L", "B2", "B1"))):
            dz = (5 - h) * (1 if way == "R" else -1)
            k = order.index(dz if h > 1 else 4)
            buf, there = ms.at[w, h - 1, 0], mr.at[w, h - 1, 0]

            def mine(what):
                return value(0, dz, what) + cut(xr.at[k], what)[...].astype(F32)

            if h == 3:
                net.wait((n, "B", way, 2), cut(mr.at[w, 1, 0], "B"))
                val = mine(rest) + cut(mr.at[w, 1, 0], rest)[...].astype(F32)
                cut(buf, rest)[...] = val.astype(BF)
                val = mine(half) + cut(mr.at[w, 1, 0], half)[...].astype(F32)
                val = val + got((n, "B", way, 1), mr.at[w, 0, 0], half)
                cut(buf, half)[...] = val.astype(BF)
                net.send((n, "B", way, h), cut(buf, "B"), cut(there, "B"), place(way, h))
            else:
                what = half if h == 1 else "B"
                put((n, "B", way, h), buf, there, what, mine(what), place(way, h))

    over_x(0)
    send_a(1)
    send_a(2)
    over_x(1)
    over_x(2)
    yield 1
    from_x(0)
    send_b(1)
    from_x(1)
    send_b(2)
    send_a(4)
    yield 2
    send_a(3)
    yield 3
    from_x(2)
    send_b(3)
    from_x(3)
    send_b(4)
    yield 4
    val = value(1, 0, "A")
    for w, way in enumerate("RL"):
        for h in (4, 3):
            val = val + got((n, "A", way, h, 1), mr.at[w, h - 1, 1], "A")
    put((n, "xA"), xs.at[7], xr.at[7], "A", val, "xp")
    yield 5
    own = value(0, 0, "A")
    for w, way in enumerate("RL"):
        for h in (4, 3):
            own = own + got((n, "A", way, h, 0), mr.at[w, h - 1, 0], "A")
    from_x(4)
    val = value(0, 0, "B") + cut(xr.at[7], "B")[...].astype(F32)
    for w, way in enumerate("RL"):
        for h in (4, 3):
            val = val + got((n, "B", way, h), mr.at[w, h - 1, 0], "B")
    yield "B", val
    yield "A", own + got((n, "xA"), xr.at[7], "A")


def last_cut(ref, a, b):
    return ref.at[..., pl.ds(a, b - a)]


TOK_CUTS = {"A": (0, 3456), "B": (3456, WIDE), "B1": (3456, 5376), "B2": (5376, WIDE), "F": (0, WIDE)}
LAT_CUTS = {"A": (0, 1024), "B": (1024, LATW), "B1": (1024, 1664), "B2": (1664, LATW), "F": (0, LATW)}
MIX_CUTS = {"A": (0, 96), "B": (96, 224), "B1": (96, 160), "B2": (160, 224), "F": (0, 224)}


def relay_kernel(
    sections,
    tok_ref, ids_ref, gates_ref, wg_ref, wu_ref, wd_ref, gain_ref, wq_ref, wk_ref, qg_ref, kg_ref, trig_ref, pre_ref,
    wuq_ref, wuk_ref, wuv_ref,
    out_ref,
    buf, wgu, wdn, wt, wdt, hid, hidt, toks_t, ms, mr, xs, xr, arr, arr_s, wqs, wks, lat,
    ms2, mr2, xs2, xr2, lat_out, pre_out, gcol, wuq, wuk, wuv, wx, kx, vx, qs, acc_s, max_s, sum_s, send_sems, recv_sems, local_sems,
):
    sec, e = lax.axis_index("section"), lax.axis_index("expert")
    xh, z, c = e // 16, (e // 2) % 8, e % 2

    turn = 1 - 2 * c

    def column(dz, dc=0):
        return (z + turn * (-dz if dc else dz) + 8) % 8

    def at(dx, dz, dc):
        return (xh + dx) % 2 * 16 + column(dz, dc) * 2 + (c + dc) % 2

    places = {
        "R": (sec, at(0, 1, 0)),
        "L": (sec, at(0, -1, 0)),
        "R2": (sec, at(0, 2, 0)),
        "L2": (sec, at(0, -2, 0)),
        "xp": (sec, at(1, 0, 0)),
        "sib": (sec, at(0, 0, 1)),
        "next": ((sec + 1) % sections, e),
        "next sib": ((sec + 1) % sections, at(0, 0, 1)),
        "prev": ((sec + sections - 1) % sections, e),
        "prev sib": ((sec + sections - 1) % sections, at(0, 0, 1)),
    }
    net = Net(send_sems, recv_sems, places)
    all_blocks, all_rows = ms.at[pl.ds(0, 15)], ms2.at[pl.ds(0, 15)]
    ms, mr, ms2, mr2 = (Hops(r) for r in (ms, mr, ms2, mr2))
    local = []

    def fetch(k, src, dst):
        cp = pltpu.make_async_copy(src, dst, local_sems.at[k])
        cp.start()
        local.append(cp)
        return cp

    def slot(dx, dz, dc):
        return (c + dc) % 2 * 16 + (xh + dx) % 2 * 8 + column(dz, dc)

    me = slot(0, 0, 0)
    own = fetch(0, tok_ref, buf.at[me, :, pl.ds(0, D)])
    load_g = fetch(1, wg_ref, wgu.at[:, pl.ds(0, HID)])
    load_u = fetch(2, wu_ref, wgu.at[:, pl.ds(HID, HID)])
    load_d = fetch(3, wd_ref, wdn)
    load_q = fetch(4, wq_ref, wqs.at[0])
    load_k = fetch(5, wk_ref, wks.at[0])
    load_p = fetch(6, pre_ref, pre_out.at[c, xh * 8 + z])
    load_uq = fetch(8, wuq_ref, wuq)
    load_uk = fetch(9, wuk_ref, wuk)
    load_uv = fetch(10, wuv_ref, wuv)

    barrier = pltpu.get_barrier_semaphore()
    for there in places.values():
        pl.semaphore_signal(barrier, inc=1, device_id=there, device_id_type=MESH)

    lane = lax.broadcasted_iota(jnp.int32, (ROWS, SIDE), 1)
    diag = lax.broadcasted_iota(jnp.int32, (ROWS, ROWS), 0) == lax.broadcasted_iota(jnp.int32, (ROWS, ROWS), 1)
    g = jnp.zeros((ROWS, SIDE), F32)
    for k in range(2):
        chosen = jnp.sum(jnp.where(diag, ids_ref[k : k + 1, :], 0), axis=1, keepdims=True)
        weight = jnp.sum(jnp.where(diag, gates_ref[k : k + 1, :], 0.0), axis=1, keepdims=True)
        g = g + jnp.where(chosen == lane % 4, weight, 0.0)
    high = g.astype(BF)
    low = (g - high.astype(F32)).astype(BF)
    side = jnp.where(lane < 4, high.astype(F32), jnp.where(lane < 8, low.astype(F32), 0.0)).astype(BF)
    buf[me, :, D:WIDE] = side

    pl.semaphore_wait(barrier, len(places))
    own.wait()

    def tok_part(s, what):
        return last_cut(buf.at[s], *TOK_CUTS[what])

    expert = e // 8
    gather = all_gather("t", net, slot, tok_part)
    next(gather)
    load_q.wait()
    net.send(("wq",), wqs.at[0], wqs.at[1], "sib")
    load_k.wait()
    net.send(("wk",), wks.at[0], wks.at[1], "sib")

    def window(owner):
        return jnp.minimum(FB * owner // 128 * 128, D - 384)

    for i in range(2):
        first = window(at(0, 0, i))
        piece = gain_ref[0:1, pl.ds(pl.multiple_of(first, 128), 384)]
        gcol[i] = jnp.broadcast_to(piece, (128, 384)).T
    load_d.wait()
    for k in range(8):
        wt[4 * k : 4 * k + 4] = wdn[:, 896 * k : 896 * (k + 1)].T.reshape(4, FB, HID)

    half = pl.ds(pl.multiple_of(c * HID, HID), HID)
    pairs = wt.reshape(16, 2, FB, HID)
    net.send(("wd",), pairs.at[:, (c + 1) % 2], wdt.at[:, :, half], "sib")
    keep_d = fetch(7, pairs.at[:, c], wdt.at[:, :, half])

    load_g.wait()
    load_u.wait()

    def experts(group):
        slots = sib_rows("t", net, slot, tok_part, group)
        m = len(slots) * ROWS
        acc = jnp.zeros((m, 2 * HID), F32)
        for k in range(7):
            rows = jnp.concatenate([buf[s, :, 1024 * k : 1024 * (k + 1)] for s in slots], axis=0)
            acc = acc + mm(rows, wgu[1024 * k : 1024 * (k + 1), :])
        side = jnp.concatenate([buf[s, :, D:WIDE] for s in slots], axis=0).astype(F32)
        lane = lax.broadcasted_iota(jnp.int32, (m, SIDE), 1)
        gate = jnp.sum(jnp.where((lane % 4 == expert) & (lane < 8), side, 0.0), axis=1, keepdims=True)
        gp, up = acc[:, :HID], acc[:, HID:]
        val = (gp / (1.0 + jnp.exp(-gp)) * up * gate).astype(BF)
        for i, s in enumerate(slots):
            hid[pl.ds(pl.multiple_of(s * ROWS, ROWS), ROWS), half] = val[ROWS * i : ROWS * (i + 1)]

    def gather_prefix():
        def chunk(dx, dz):
            return pre_out.at[c, (xh + dx) % 2 * 8 + column(dz)]

        def pass_on(key, ref, place):
            net.send(key, ref, ref, place)

        def hop(d, h):
            for way, sign in DIRS:
                if h < 4 or (way == "R") == (d == 0):
                    if h > 0:
                        net.wait(("p", d, way, h), chunk(d, sign * h))
                    if h < 3 or (h == 3 and (way == "R") == (d == 0)):
                        pass_on(("p", d, way, h + 1), chunk(d, sign * h), way)

        hop(0, 0)
        pass_on(("p", "x"), chunk(0, 0), "xp")
        yield
        hop(0, 1)
        yield
        net.wait(("p", "x"), chunk(1, 0))
        hop(1, 0)
        yield
        for d, h in ((0, 2), (0, 3), (1, 1), (0, 4), (1, 2), (1, 3), (1, 4)):
            hop(d, h)
            yield
        pass_on(("all", "sib"), pre_out.at[c], "sib")
        yield
        net.wait(("all", "sib"), pre_out.at[(c + 1) % 2])

    prefix = gather_prefix()

    def ticks(count):
        for _ in range(count):
            next(prefix, None)

    for group in gather:
        if group == [(0, 3), (1, 2)]:
            load_p.wait()
            ticks(1)
        if group == [(1, 4)]:
            ticks(1)
        experts(group)
        if group == [(0, 4), (1, 3)]:
            ticks(1)
    net.send(("hid",), hid.at[:, half], hid.at[:, half], "sib")

    start = window(e)
    toks_t[...] = buf[:, :, pl.ds(pl.multiple_of(start, 128), 384)].reshape(TOK, 384).T

    load_uk.wait()
    load_uv.wait()
    for k in range(2):
        wx[:, 128 * k : 128 * (k + 1)] = wuv[k]

    other = pl.ds(pl.multiple_of((c + 1) % 2 * HID, HID), HID)
    net.wait(("hid",), hid.at[:, other])
    net.wait(("wd",), wdt.at[:, :, other])
    keep_d.wait()
    hidt[...] = hid[...].T

    def mixed_term(dx, dz, what):
        a, b = MIX_CUTS[what]
        block = (xh + dx) % 2 * 8 + column(dz)
        return mm(wdt[block, a:b, :], hidt[...])

    def mix_cut(ref, what):
        a, b = MIX_CUTS[what]
        return ref.at[pl.ds(a, b - a)]

    off = FB * e - start
    for got in reduce_scatter("m", net, mixed_term, mix_cut, ms, mr, xs, xr):
        if not isinstance(got, tuple):
            ticks({1: 1, 5: 2}.get(got, 0))
            continue
        what, val = got
        a, b = MIX_CUTS[what]
        rows = toks_t[pl.ds(pl.multiple_of(off + a, 16), b - a), :].astype(F32)
        arr_s[a:b] = (val + rows).astype(BF)
        for i, place in enumerate(("next", "next sib")):
            tokens_of = pl.ds(pl.multiple_of((c + i) % 2 * 256, 256), 256)
            block = arr_s.at[pl.ds(a, b - a), tokens_of]
            net.send(("next", i, what), block, arr.at[i, pl.ds(a, b - a)], place)

    ticks(2)
    net.wait(("wq",), wqs.at[1])
    net.wait(("wk",), wks.at[1])
    squares = jnp.zeros((1, 256), F32)
    for i in range(2):
        for what in ("A", "B1", "B2"):
            net.wait(("next", i, what), mix_cut(arr.at[i], what))
        x = arr[i].astype(F32)
        squares = squares + jnp.sum(x * x, axis=0, keepdims=True)
        shift = FB * at(0, 0, i) - window(at(0, 0, i))
        scaled = (x * gcol[i, pl.ds(pl.multiple_of(shift, 32), FB), 0:1]).T.astype(BF)
        if i == 0:
            lat[:, 0:QR] = mm(scaled, wqs[0])
            lat[:, QR:LAT] = mm(scaled, wks[0])
        else:
            lat[:, 0:QR] += mm(scaled, wqs[1])
            lat[:, QR:LAT] += mm(scaled, wks[1])
    lat[:, LAT:LATW] = jnp.broadcast_to(squares, (128, 256)).T[:, 0 : LATW - LAT]

    def lat_term(dx, dz, what):
        a, b = LAT_CUTS[what]
        block = (xh + dx) % 2 * 8 + column(dz)
        return lat[pl.ds(pl.multiple_of(block * ROWS, ROWS), ROWS), a:b]

    def lat_cut(ref, what):
        return last_cut(ref, *LAT_CUTS[what])

    load_uq.wait()
    order = []

    def expand(first, rows):
        there = slice(first, first + 512)
        values = mm(rows[:, 0:KVR], wx[...]).astype(BF)
        for k in range(2):
            kx[k, 0:NOPE, there] = mm(wuk[k], rows[:, 0:KVR], NT).astype(BF)
            kx[k, NOPE:, there] = rows[:, KVR:KEY].T
            vx[k, there, :] = values[:, 128 * k : 128 * (k + 1)]

    def expand_prefix(i):
        expand(512 * i, pre_out[(c + i // 2) % 2, i % 2 * 8 : i % 2 * 8 + 8].reshape(512, KEY))

    sums = {}
    for got in scatter_far("l", net, lat_term, lat_cut, ms2, mr2, xs2, xr2):
        if isinstance(got, tuple):
            sums[got[0]] = got[1]
        elif got == 1:
            ticks(1)
        elif got == 3:
            ticks(2)
            expand_prefix(0)
        elif got == 4:
            expand_prefix(1)
        elif got == 5:
            ticks(1)
            expand_prefix(2)
            expand_prefix(3)
    total = jnp.concatenate([sums["A"], sums["B"]], axis=1)
    scale = lax.rsqrt(total[:, LAT : LAT + 1] * (1.0 / D) + EPSILON)

    def rms(v, gain):
        v = v * scale
        return (v * lax.rsqrt(jnp.mean(v * v, axis=1, keepdims=True) + EPSILON) * gain).astype(BF)

    lat_out[e, :, 0:QR] = rms(total[:, 0:QR], qg_ref[...])
    lat_out[e, :, QR : QR + KVR] = rms(total[:, QR : QR + KVR], kg_ref[...])
    tail = total[:, QR + KVR :] * scale
    first, second = tail[:, 0:32], tail[:, 32:64]
    cos, sin = trig_ref[e, :, 0:32], trig_ref[e, :, 32:64]
    turned = jnp.concatenate([first * cos - second * sin, first * sin + second * cos], axis=1)
    lat_out[e, :, QR + KVR : LAT] = turned.astype(BF)
    lat_out[e, :, LAT:LATW] = jnp.zeros((ROWS, LATW - LAT), BF)

    def lat_part(s, what):
        return last_cut(lat_out.at[s], *LAT_CUTS[what])

    def queries(group):
        slots = sib_rows("o", net, at, lat_part, group)
        m = len(slots) * ROWS
        base = len(order) * ROWS
        order.extend(slots)
        mine = slice(base, base + m)
        angle = jnp.concatenate([trig_ref[s] for s in slots], axis=0)
        cos, sin = angle[:, 0:32], angle[:, 32:64]
        q = mm(jnp.concatenate([lat_out[s, :, 0:QR] for s in slots], axis=0), wuq[...]) * SHARP
        for k in range(2):
            a = k * (NOPE + ROPE)
            first, second = q[:, a + NOPE : a + NOPE + 32], q[:, a + NOPE + 32 : a + NOPE + 64]
            turned = jnp.concatenate([first * cos - second * sin, first * sin + second * cos], axis=1)
            qs[k, mine, 0:NOPE] = q[:, a : a + NOPE].astype(BF)
            qs[k, mine, NOPE:] = turned.astype(BF)
        both = range(2)
        score = [[mm(qs[k, mine, :], kx[k, :, 512 * b : 512 * (b + 1)]) for b in range(4)] for k in both]
        top = [functools.reduce(jnp.maximum, [jnp.max(x, axis=1, keepdims=True) for x in score[k]]) for k in both]
        for k in both:
            total, mixed = 0.0, 0.0
            for b in range(4):
                p = jnp.exp2(score[k][b] - top[k])
                total = total + jnp.sum(p, axis=1, keepdims=True)
                mixed = mixed + mm(p.astype(BF), vx[k, 512 * b : 512 * (b + 1), :])
            acc_s[k, mine, :] = mixed
            max_s[k, mine, :] = jnp.broadcast_to(top[k], (m, 128))
            sum_s[k, mine, :] = jnp.broadcast_to(total, (m, 128))

    def new_keys():
        row = lax.broadcasted_iota(jnp.int32, (ROWS, 1), 0)
        when = jnp.concatenate([row + s * ROWS for s in order], axis=0)
        key_when = lax.broadcasted_iota(jnp.int32, (1, TOK), 1)
        pieces = [(k, slice(256 * i, 256 * (i + 1))) for i in range(2) for k in range(2)]
        score = [mm(qs[k, mine, :], kx[k, :, CACHE:]) for k, mine in pieces]
        score = [jnp.where(key_when <= when[mine], x, -jnp.inf) for x, (k, mine) in zip(score, pieces)]
        new = [jnp.maximum(max_s[k, mine, 0:1], jnp.max(x, axis=1, keepdims=True)) for x, (k, mine) in zip(score, pieces)]
        for (k, mine), x, top in zip(pieces, score, new):
            fade = jnp.exp2(max_s[k, mine, 0:1] - top)
            p = jnp.exp2(x - top)
            total = sum_s[k, mine, 0:1] * fade + jnp.sum(p, axis=1, keepdims=True)
            mixed = acc_s[k, mine, :] * fade + mm(p.astype(BF), vx[k, CACHE:, :])
            val = (mixed * (1.0 / total)).astype(BF)
            for j, s in enumerate(order[mine.start // ROWS : mine.stop // ROWS]):
                there = pl.ds(pl.multiple_of(s * ROWS, ROWS), ROWS)
                out_ref[there, 128 * k : 128 * (k + 1)] = val[ROWS * j : ROWS * (j + 1)]

    finish_gather = gather_far("o", net, at, lat_part)
    next(finish_gather)
    for group in finish_gather:
        queries(group)
    expand(CACHE, lat_out[:, :, QR:LAT].reshape(TOK, KEY))
    new_keys()
    for group, ref in (
        ("t", buf.at[pl.ds(0, 31)]),
        ("o", lat_out.at[pl.ds(0, 31)]),
        ("m", all_blocks),
        ("l", all_rows),
        ("p", pre_out.at[0, pl.ds(0, 15)]),
        ("all", pre_out.at[0]),
        ("next", arr_s),
        ("wq", wqs.at[0]),
        ("wk", wks.at[0]),
        ("wd", wdt.at[:, :, half]),
        ("hid", hid.at[:, half]),
    ):
        net.sent(group, ref)
    assert (len(net.ids), len(net.groups)) == (COPIES, SENDS)


SHARP = float((NOPE + ROPE) ** (-0.5) * np.log2(np.e))


def trig_table():
    half = ROPE // 2
    frequency = 10000.0 ** (-np.arange(half) / half)
    angles = (CACHE + np.arange(TOK))[:, None] * frequency[None, :].astype(np.float32)
    angles = angles.astype(np.float32).astype(np.float64)
    both = np.concatenate([np.cos(angles), np.sin(angles)], axis=1)
    return both.astype(np.float32)


def per_device(
    sections, tokens, expert_ids, gate_values, w_gate, w_up, w_down, norm_gain, w_dq, w_dkv, q_gain, kv_gain, w_uq, w_uk,
    w_uv, prefix_cache,
):
    vm = pl.BlockSpec(memory_space=pltpu.VMEM)
    anyw = pl.BlockSpec(memory_space=pl.ANY)
    V = pltpu.VMEM
    out = pl.pallas_call(
        functools.partial(relay_kernel, sections),
        name="relay",
        out_shape=jax.ShapeDtypeStruct((TOK, 256), BF),
        in_specs=[anyw, vm, vm, anyw, anyw, anyw, vm, anyw, anyw, vm, vm, vm, anyw, anyw, anyw, anyw],
        out_specs=vm,
        scratch_shapes=[
            V((32, ROWS, WIDE), BF),
            V((D, 2 * HID), BF),
            V((HID, D), BF),
            V((32, FB, HID), BF),
            V((16, FB, 2 * HID), BF),
            V((TOK, 2 * HID), BF),
            V((2 * HID, TOK), BF),
            V((384, TOK), BF),
            V((16, FB, TOK), BF),
            V((16, FB, TOK), BF),
            V((8, FB, TOK), BF),
            V((8, FB, TOK), BF),
            V((2, FB, TOK // 2), BF),
            V((FB, TOK), BF),
            V((2, FB, QR), BF),
            V((2, FB, KEY), BF),
            V((TOK // 2, LATW), F32),
            V((16, ROWS, LATW), BF),
            V((16, ROWS, LATW), BF),
            V((8, ROWS, LATW), BF),
            V((8, ROWS, LATW), BF),
            V((32, ROWS, LATW), BF),
            V((2, 16, PRE, KEY), BF),
            V((2, 384, 128), F32),
            V((QR, 384), BF),
            V((2, NOPE, KVR), BF),
            V((2, KVR, 128), BF),
            V((KVR, 256), BF),
            V((2, NOPE + ROPE, CACHE + TOK), BF),
            V((2, CACHE + TOK, 128), BF),
            V((2, TOK, NOPE + ROPE), BF),
            V((2, TOK, 128), F32),
            V((2, TOK, 128), F32),
            V((2, TOK, 128), F32),
            pltpu.SemaphoreType.DMA((SENDS,)),
            pltpu.SemaphoreType.DMA((COPIES,)),
            pltpu.SemaphoreType.DMA((11,)),
        ],
        compiler_params=pltpu.CompilerParams(collective_id=0, has_side_effects=True, vmem_limit_bytes=60 << 20),
        cost_estimate=pl.CostEstimate(flops=12 * 10**9, bytes_accessed=12 * 10**6, transcendentals=4 * 10**6),
    )(
        tokens[0], expert_ids[0].T, gate_values[0].T, w_gate[0], w_up[0], w_down[0], norm_gain, w_dq[0], w_dkv[0],
        q_gain, kv_gain, jnp.asarray(trig_table().reshape(32, ROWS, ROPE)), prefix_cache[0], w_uq[0], w_uk[0], w_uv[0],
    )
    return out[None]


def solution(mesh):
    placed = (
        P("section", "expert", None),
        P("section", "expert", None),
        P("section", "expert", None),
        P("section", None, "expert"),
        P("section", None, "expert"),
        P("section", "expert", None),
        P("section", None),
        P("section", "expert", None),
        P("section", "expert", None),
        P("section", None),
        P("section", None),
        P("section", None, "expert"),
        P("section", "expert", None, None),
        P("section", "expert", None, None),
        P("section", "expert", None),
    )
    return jax.shard_map(
        functools.partial(per_device, mesh.shape["section"]),
        mesh=mesh,
        in_specs=placed,
        out_specs=P("section", None, "expert"),
        check_vma=False,
    )
```

```python
import functools

import jax
import jax.numpy as jnp
import numpy as np
from jax import lax
from jax.experimental import pallas as pl
from jax.experimental.pallas import tpu as pltpu
from jax.sharding import PartitionSpec as P

MESH = pl.DeviceIdType.MESH
COPIES = 107
SENDS = 11
REUSED = {"o": "t", "l": "m"}
BF = jnp.bfloat16
F32 = jnp.float32
EPSILON = 1e-06
D = 7168
ROWS = 16
SIDE = 128
WIDE = D + SIDE
HID = 128
QR = 1536
KVR = 512
ROPE = 64
NOPE = 128
KEY = KVR + ROPE
LAT = QR + KEY
LATW = 2176
FB = 224
TOK = 512
CACHE = 2048
PRE = 64
KT = (((1,), (0,)), ((), ()))
NT = (((1,), (1,)), ((), ()))
TN = (((0,), (0,)), ((), ()))


def mm(a, b, dims=KT):
    return lax.dot_general(a, b, dims, preferred_element_type=F32)


class Net:
    def __init__(self, send_sems, recv_sems, places):
        self.send_sems, self.recv_sems, self.places = send_sems, recv_sems, places
        self.ids, self.groups = {}, {}

    def copy(self, key, src, dst, place, group="t"):
        same = (REUSED.get(key[0], key[0]),) + key[1:]
        index = self.ids.setdefault(same, len(self.ids))
        return pltpu.make_async_remote_copy(
            src_ref=src,
            dst_ref=dst,
            send_sem=self.send_sems.at[self.groups.setdefault(group, len(self.groups))],
            recv_sem=self.recv_sems.at[index],
            device_id=self.places[place],
            device_id_type=MESH,
        )

    def send(self, key, src, dst, place):
        self.copy(key, src, dst, place, key[0]).start()

    def wait(self, key, ref):
        self.copy(key, ref, ref, "sib").wait_recv()

    def sent(self, group, ref):
        self.copy(("t", "xA"), ref, ref, "sib", group).wait_send()


class Hops:
    def __init__(self, ref):
        self.ref, self.at = ref, self

    def __getitem__(self, index):
        first = index[0] * 8 + index[1] * 2
        return self.ref.at[first + index[2]] if len(index) == 3 else self.ref.at[pl.ds(first, 2)]


DIRS = (("R", -1), ("L", 1))


def all_gather(n, net, slot, part):
    def pass_on(key, s, what, place):
        net.send(key, part(s, what), part(s, what), place)

    me, mate = slot(0, 0, 0), slot(1, 0, 0)
    pass_on((n, "xA"), me, "A", "xp")
    for what in "BA":
        for way, _ in DIRS:
            pass_on((n, what, way, 1), me, what, way)
    pass_on((n, "xB", "", 0), me, "B", "xp")
    pass_on((n, "s0", "", 0), me, "F", "sib")
    yield []

    net.wait((n, "xA"), part(mate, "A"))
    for way, _ in DIRS:
        pass_on((n, "A1", way, 1), mate, "A", way)
    net.wait((n, "xB", "", 0), part(mate, "B"))
    pass_on((n, "s1", "", 0), mate, "F", "sib")

    def finish(h):
        if h < 4:
            for way, sign in DIRS:
                s = slot(1, sign * h, 0)
                net.wait((n, "xB", way, h), part(s, "B"))
                pass_on((n, "s1", way, h), s, "F", "sib")
        else:
            s = slot(1, 4, 0)
            net.wait((n, "xB", "R", 4), part(s, "B1"))
            net.wait((n, "xB", "L", 4), part(s, "B2"))
            pass_on((n, "s1", "R", 4), s, "F", "sib")

    def second(h):
        for way, sign in DIRS:
            if h < 4 or way == "L":
                s = slot(1, sign * h, 0)
                net.wait((n, "A1", way, h), part(s, "A"))
                if h < 3 or (h == 3 and way == "L"):
                    pass_on((n, "A1", way, h + 1), s, "A", way)

    for h in range(1, 5):
        for way, sign in DIRS:
            s = slot(0, sign * h, 0)
            half = "B1" if way == "R" else "B2"
            if h < 4:
                net.wait((n, "B", way, h), part(s, "B"))
                pass_on((n, "B", way, h + 1), s, "B" if h < 3 else half, way)
                pass_on((n, "xB", way, h), s, "B", "xp")
            else:
                net.wait((n, "B", way, 4), part(s, half))
                pass_on((n, "xB", way, 4), s, half, "xp")
        if h > 1:
            finish(h - 1)
        for way, sign in DIRS:
            if h < 4 or way == "R":
                s = slot(0, sign * h, 0)
                net.wait((n, "A", way, h), part(s, "A"))
                if h < 3 or (h == 3 and way == "R"):
                    pass_on((n, "A", way, h + 1), s, "A", way)
                pass_on((n, "s0", way, h), s, "F", "sib")
        yield [(0, h - 1)] + ([(1, h - 2)] if h > 1 else [])
        if h < 4:
            second(h)
    second(4)
    yield [(0, 4), (1, 3)]
    finish(4)
    yield [(1, 4)]


def gather_far(n, net, slot, part):
    def pass_on(key, s, what, place):
        net.send(key, part(s, what), part(s, what), place)

    def both_ways(name, h, s, what):
        for way, _ in DIRS:
            pass_on((n, name, way, h), s, what, way + "2" if h == 2 else way)

    me, mate = slot(0, 0, 0), slot(1, 0, 0)
    pass_on((n, "xA"), me, "A", "xp")
    for what in "BA":
        both_ways(what, 2, me, what)
        both_ways(what, 1, me, what)
    pass_on((n, "xB", "", 0), me, "B", "xp")
    pass_on((n, "s0", "", 0), me, "F", "sib")
    yield []
    net.wait((n, "xA"), part(mate, "A"))
    both_ways("A1", 2, mate, "A")
    both_ways("A1", 1, mate, "A")
    net.wait((n, "xB", "", 0), part(mate, "B"))
    pass_on((n, "s1", "", 0), mate, "F", "sib")

    def ring_b(h):
        for way, sign in DIRS:
            s = slot(0, sign * h, 0)
            half = "B1" if way == "R" else "B2"
            what = "B" if h < 4 else half
            net.wait((n, "B", way, h), part(s, what))
            if h == 2:
                pass_on((n, "B", way, 3), s, "B", way)
                pass_on((n, "B", way, 4), s, half, way + "2")
            pass_on((n, "xB", way, h), s, what, "xp")

    def ring_a(name, h, d):
        for way, sign in DIRS:
            last = (way == "R") == (d == 0)
            if h < 4 or last:
                s = slot(d, sign * h, 0)
                net.wait((n, name, way, h), part(s, "A"))
                if h == 2:
                    pass_on((n, name, way, 3), s, "A", way)
                    if last:
                        pass_on((n, name, way, 4), s, "A", way + "2")
                if d == 0:
                    pass_on((n, "s0", way, h), s, "F", "sib")

    def finish(h):
        if h < 4:
            for way, sign in DIRS:
                s = slot(1, sign * h, 0)
                net.wait((n, "xB", way, h), part(s, "B"))
                pass_on((n, "s1", way, h), s, "F", "sib")
        else:
            s = slot(1, 4, 0)
            net.wait((n, "xB", "R", 4), part(s, "B1"))
            net.wait((n, "xB", "L", 4), part(s, "B2"))
            pass_on((n, "s1", "R", 4), s, "F", "sib")

    ring_b(1)
    ring_b(2)
    ring_a("A", 1, 0)
    ring_a("A", 2, 0)
    yield [(0, 0)]
    ring_a("A1", 1, 1)
    ring_a("A1", 2, 1)
    finish(1)
    finish(2)
    yield [(1, 0), (0, 1), (0, 2)]
    ring_b(3)
    ring_b(4)
    ring_a("A", 3, 0)
    ring_a("A", 4, 0)
    yield [(1, 1), (1, 2)]
    yield [(0, 3), (0, 4)]
    ring_a("A1", 3, 1)
    ring_a("A1", 4, 1)
    finish(3)
    finish(4)
    yield [(1, 3), (1, 4)]


def sib_rows(n, net, slot, part, group):
    slots = []
    for dx, h in group:
        for way, sign in DIRS if 0 < h < 4 else (("" if h == 0 else "R", 1),):
            net.wait((n, f"s{dx}", way, h), part(slot(dx, sign * h, 1), "F"))
            slots += [slot(dx, sign * h, 0), slot(dx, sign * h, 1)]
    return slots


def reduce_scatter(n, net, value, cut, ms, mr, xs, xr):
    order = [4, 3, -3, 2, -2, 1, -1, 0]

    def put(key, buf, there, what, val, place):
        cut(buf, what)[...] = val.astype(BF)
        net.send(key, cut(buf, what), cut(there, what), place)

    def got(key, buf, what):
        net.wait(key, cut(buf, what))
        return cut(buf, what)[...].astype(F32)

    last = ("B1", "B2")
    trips = [(k, 1) for k in range(8)]

    def over_x(j):
        if j < len(trips):
            k, count = trips[j]
            for i in range(k, k + count):
                cut(xs.at[i], "B")[...] = value(1, order[i], "B").astype(BF)
            there = pl.ds(k, count)
            if count == 1:
                there = k
            net.send((n, "x", k), cut(xs.at[there], "B"), cut(xr.at[there], "B"), "xp")

    def from_x(i):
        for j, (k, count) in enumerate(trips):
            if k == i:
                net.wait((n, "x", k), cut(xr.at[pl.ds(k, count) if count > 1 else k], "B"))
                over_x(j + 3)

    def hop_a(h, apart=False):
        for d in (1, 0):
            for w, way in enumerate("RL"):
                if (h == 1 and w != d) or (h == 2 and (w != d) != apart):
                    continue
                val = value(d, (5 - h) * (1 if way == "R" else -1), "A")
                if h > 2 or (h == 2 and w == d):
                    val = val + got((n, "A", way, h - 1, d), mr.at[w, h - 2, d], "A")
                put((n, "A", way, h, d), ms.at[w, h - 1, d], mr.at[w, h - 1, d], "A", val, way)

    def hop_b(h):
        for w, (way, half, rest) in enumerate((("R", "B1", "B2"), ("L", "B2", "B1"))):
            dz = (5 - h) * (1 if way == "R" else -1)
            k = order.index(dz if h > 1 else 4)
            if h > 1 or w == 0:
                from_x(k)
            buf, there = ms.at[w, h - 1, 0], mr.at[w, h - 1, 0]
            if h == 1:
                val = value(0, 4, half) + cut(xr.at[k], half)[...].astype(F32)
                put((n, "B", way, 1), buf, there, half, val, way)
            elif h == 2:
                val = value(0, dz, rest) + cut(xr.at[k], rest)[...].astype(F32)
                cut(buf, rest)[...] = val.astype(BF)
                val = value(0, dz, half) + cut(xr.at[k], half)[...].astype(F32)
                val = val + got((n, "B", way, 1), mr.at[w, 0, 0], half)
                cut(buf, half)[...] = val.astype(BF)
                net.send((n, "B", way, h), cut(buf, "B"), cut(there, "B"), way)
            else:
                net.wait((n, "B", way, h - 1), cut(mr.at[w, h - 2, 0], "B"))
                for what in last if h == 4 else ("B",):
                    val = value(0, dz, what) + cut(xr.at[k], what)[...].astype(F32)
                    val = val + cut(mr.at[w, h - 2, 0], what)[...].astype(F32)
                    put((n, "B2" if what == "B2" else "B", way, h), buf, there, what, val, way)

    over_x(0)
    hop_a(1)
    hop_a(2, True)
    over_x(1)
    over_x(2)
    yield 1
    for h in range(2, 5):
        hop_a(h)
        hop_b(h - 1)
        yield h
    val = value(1, 0, "A")
    for w, way in enumerate("RL"):
        val = val + got((n, "A", way, 4, 1), mr.at[w, 3, 1], "A")
    put((n, "xA"), xs.at[7], xr.at[7], "A", val, "xp")
    hop_b(4)
    yield 5
    own = value(0, 0, "A")
    for w, way in enumerate("RL"):
        own = own + got((n, "A", way, 4, 0), mr.at[w, 3, 0], "A")
    yield "A", own + got((n, "xA"), xr.at[7], "A")
    from_x(7)
    for what in last:
        val = value(0, 0, what) + cut(xr.at[7], what)[...].astype(F32)
        for w, way in enumerate("RL"):
            val = val + got((n, "B2" if what == "B2" else "B", way, 4), mr.at[w, 3, 0], what)
        yield what, val


def scatter_far(n, net, value, cut, ms, mr, xs, xr):
    order = [4, 3, -3, 2, -2, 1, -1, 0]
    trips = [(0, 1), (1, 2), (3, 2), (5, 2), (7, 1)]

    def put(key, buf, there, what, val, place):
        cut(buf, what)[...] = val.astype(BF)
        net.send(key, cut(buf, what), cut(there, what), place)

    def got(key, buf, what):
        net.wait(key, cut(buf, what))
        return cut(buf, what)[...].astype(F32)

    def over_x(j):
        if j < len(trips):
            k, count = trips[j]
            for i in range(k, k + count):
                cut(xs.at[i], "B")[...] = value(1, order[i], "B").astype(BF)
            there = pl.ds(k, count) if count > 1 else k
            net.send((n, "x", k), cut(xs.at[there], "B"), cut(xr.at[there], "B"), "xp")

    def from_x(j):
        k, count = trips[j]
        net.wait((n, "x", k), cut(xr.at[pl.ds(k, count) if count > 1 else k], "B"))
        over_x(j + 3)

    def place(way, h):
        return way + "2" if h in (1, 3) else way

    def send_a(h):
        for d in (1, 0):
            for w, way in enumerate("RL"):
                if h == 1 and w != d:
                    continue
                val = value(d, (5 - h) * (1 if way == "R" else -1), "A")
                if h == 3:
                    val = val + got((n, "A", way, 2, d), mr.at[w, 1, d], "A")
                    if w == d:
                        val = val + got((n, "A", way, 1, d), mr.at[w, 0, d], "A")
                put((n, "A", way, h, d), ms.at[w, h - 1, d], mr.at[w, h - 1, d], "A", val, place(way, h))

    def send_b(h):
        for w, (way, half, rest) in enumerate((("R", "B1", "B2"), ("L", "B2", "B1"))):
            dz = (5 - h) * (1 if way == "R" else -1)
            k = order.index(dz if h > 1 else 4)
            buf, there = ms.at[w, h - 1, 0], mr.at[w, h - 1, 0]

            def mine(what):
                return value(0, dz, what) + cut(xr.at[k], what)[...].astype(F32)

            if h == 3:
                net.wait((n, "B", way, 2), cut(mr.at[w, 1, 0], "B"))
                val = mine(rest) + cut(mr.at[w, 1, 0], rest)[...].astype(F32)
                cut(buf, rest)[...] = val.astype(BF)
                val = mine(half) + cut(mr.at[w, 1, 0], half)[...].astype(F32)
                val = val + got((n, "B", way, 1), mr.at[w, 0, 0], half)
                cut(buf, half)[...] = val.astype(BF)
                net.send((n, "B", way, h), cut(buf, "B"), cut(there, "B"), place(way, h))
            else:
                what = half if h == 1 else "B"
                put((n, "B", way, h), buf, there, what, mine(what), place(way, h))

    over_x(0)
    send_a(1)
    send_a(2)
    over_x(1)
    over_x(2)
    yield 1
    from_x(0)
    send_b(1)
    from_x(1)
    send_b(2)
    send_a(4)
    yield 2
    send_a(3)
    yield 3
    from_x(2)
    send_b(3)
    from_x(3)
    send_b(4)
    yield 4
    val = value(1, 0, "A")
    for w, way in enumerate("RL"):
        for h in (4, 3):
            val = val + got((n, "A", way, h, 1), mr.at[w, h - 1, 1], "A")
    put((n, "xA"), xs.at[7], xr.at[7], "A", val, "xp")
    yield 5
    own = value(0, 0, "A")
    for w, way in enumerate("RL"):
        for h in (4, 3):
            own = own + got((n, "A", way, h, 0), mr.at[w, h - 1, 0], "A")
    from_x(4)
    val = value(0, 0, "B") + cut(xr.at[7], "B")[...].astype(F32)
    for w, way in enumerate("RL"):
        for h in (4, 3):
            val = val + got((n, "B", way, h), mr.at[w, h - 1, 0], "B")
    yield "B", val
    yield "A", own + got((n, "xA"), xr.at[7], "A")


def last_cut(ref, a, b):
    return ref.at[..., pl.ds(a, b - a)]


TOK_CUTS = {"A": (0, 3456), "B": (3456, WIDE), "B1": (3456, 5376), "B2": (5376, WIDE), "F": (0, WIDE)}
LAT_CUTS = {"A": (0, 1024), "B": (1024, LATW), "B1": (1024, 1664), "B2": (1664, LATW), "F": (0, LATW)}
MIX_CUTS = {"A": (0, 96), "B": (96, 224), "B1": (96, 160), "B2": (160, 224), "F": (0, 224)}


def relay_kernel(
    sections,
    tok_ref, ids_ref, gates_ref, wg_ref, wu_ref, wd_ref, gain_ref, wq_ref, wk_ref, qg_ref, kg_ref, trig_ref, pre_ref,
    wuq_ref, wuk_ref, wuv_ref,
    out_ref,
    buf, wgu, wdn, wt, wdt, hid, hidt, toks_t, ms, mr, xs, xr, arr, arr_s, wqs, wks, lat,
    ms2, mr2, xs2, xr2, lat_out, pre_out, gcol, wuq, wuk, wuv, wx, kx, vx, qs, acc_s, max_s, sum_s, send_sems, recv_sems, local_sems,
):
    sec, e = lax.axis_index("section"), lax.axis_index("expert")
    xh, z, c = e // 16, (e // 2) % 8, e % 2

    turn = 1 - 2 * c

    def column(dz, dc=0):
        return (z + turn * (-dz if dc else dz) + 8) % 8

    def at(dx, dz, dc):
        return (xh + dx) % 2 * 16 + column(dz, dc) * 2 + (c + dc) % 2

    places = {
        "R": (sec, at(0, 1, 0)),
        "L": (sec, at(0, -1, 0)),
        "R2": (sec, at(0, 2, 0)),
        "L2": (sec, at(0, -2, 0)),
        "xp": (sec, at(1, 0, 0)),
        "sib": (sec, at(0, 0, 1)),
        "next": ((sec + 1) % sections, e),
        "next sib": ((sec + 1) % sections, at(0, 0, 1)),
        "prev": ((sec + sections - 1) % sections, e),
        "prev sib": ((sec + sections - 1) % sections, at(0, 0, 1)),
    }
    net = Net(send_sems, recv_sems, places)
    all_blocks, all_rows = ms.at[pl.ds(0, 15)], ms2.at[pl.ds(0, 15)]
    ms, mr, ms2, mr2 = (Hops(r) for r in (ms, mr, ms2, mr2))
    local = []

    def fetch(k, src, dst):
        cp = pltpu.make_async_copy(src, dst, local_sems.at[k])
        cp.start()
        local.append(cp)
        return cp

    def slot(dx, dz, dc):
        return (c + dc) % 2 * 16 + (xh + dx) % 2 * 8 + column(dz, dc)

    me = slot(0, 0, 0)
    own = fetch(0, tok_ref, buf.at[me, :, pl.ds(0, D)])
    load_g = fetch(1, wg_ref, wgu.at[:, pl.ds(0, HID)])
    load_u = fetch(2, wu_ref, wgu.at[:, pl.ds(HID, HID)])
    load_d = fetch(3, wd_ref, wdn)
    load_q = fetch(4, wq_ref, wqs.at[0])
    load_k = fetch(5, wk_ref, wks.at[0])
    load_p = fetch(6, pre_ref, pre_out.at[c, xh * 8 + z])
    load_uq = fetch(8, wuq_ref, wuq)
    load_uk = fetch(9, wuk_ref, wuk)
    load_uv = fetch(10, wuv_ref, wuv)

    barrier = pltpu.get_barrier_semaphore()
    for there in places.values():
        pl.semaphore_signal(barrier, inc=1, device_id=there, device_id_type=MESH)

    lane = lax.broadcasted_iota(jnp.int32, (ROWS, SIDE), 1)
    diag = lax.broadcasted_iota(jnp.int32, (ROWS, ROWS), 0) == lax.broadcasted_iota(jnp.int32, (ROWS, ROWS), 1)
    g = jnp.zeros((ROWS, SIDE), F32)
    for k in range(2):
        chosen = jnp.sum(jnp.where(diag, ids_ref[k : k + 1, :], 0), axis=1, keepdims=True)
        weight = jnp.sum(jnp.where(diag, gates_ref[k : k + 1, :], 0.0), axis=1, keepdims=True)
        g = g + jnp.where(chosen == lane % 4, weight, 0.0)
    high = g.astype(BF)
    low = (g - high.astype(F32)).astype(BF)
    side = jnp.where(lane < 4, high.astype(F32), jnp.where(lane < 8, low.astype(F32), 0.0)).astype(BF)
    buf[me, :, D:WIDE] = side

    pl.semaphore_wait(barrier, len(places))
    own.wait()

    def tok_part(s, what):
        return last_cut(buf.at[s], *TOK_CUTS[what])

    expert = e // 8
    gather = all_gather("t", net, slot, tok_part)
    next(gather)
    load_q.wait()
    net.send(("wq",), wqs.at[0], wqs.at[1], "sib")
    load_k.wait()
    net.send(("wk",), wks.at[0], wks.at[1], "sib")

    def window(owner):
        return jnp.minimum(FB * owner // 128 * 128, D - 384)

    for i in range(2):
        first = window(at(0, 0, i))
        piece = gain_ref[0:1, pl.ds(pl.multiple_of(first, 128), 384)]
        gcol[i] = jnp.broadcast_to(piece, (128, 384)).T
    load_d.wait()
    for k in range(8):
        wt[4 * k : 4 * k + 4] = wdn[:, 896 * k : 896 * (k + 1)].T.reshape(4, FB, HID)

    half = pl.ds(pl.multiple_of(c * HID, HID), HID)
    pairs = wt.reshape(16, 2, FB, HID)
    net.send(("wd",), pairs.at[:, (c + 1) % 2], wdt.at[:, :, half], "sib")
    keep_d = fetch(7, pairs.at[:, c], wdt.at[:, :, half])

    load_g.wait()
    load_u.wait()

    def experts(group):
        slots = sib_rows("t", net, slot, tok_part, group)
        m = len(slots) * ROWS
        acc = jnp.zeros((m, 2 * HID), F32)
        for k in range(7):
            rows = jnp.concatenate([buf[s, :, 1024 * k : 1024 * (k + 1)] for s in slots], axis=0)
            acc = acc + mm(rows, wgu[1024 * k : 1024 * (k + 1), :])
        side = jnp.concatenate([buf[s, :, D:WIDE] for s in slots], axis=0).astype(F32)
        lane = lax.broadcasted_iota(jnp.int32, (m, SIDE), 1)
        gate = jnp.sum(jnp.where((lane % 4 == expert) & (lane < 8), side, 0.0), axis=1, keepdims=True)
        gp, up = acc[:, :HID], acc[:, HID:]
        val = (gp / (1.0 + jnp.exp(-gp)) * up * gate).astype(BF)
        for i, s in enumerate(slots):
            hid[pl.ds(pl.multiple_of(s * ROWS, ROWS), ROWS), half] = val[ROWS * i : ROWS * (i + 1)]

    def gather_prefix():
        def chunk(dx, dz):
            return pre_out.at[c, (xh + dx) % 2 * 8 + column(dz)]

        def pass_on(key, ref, place):
            net.send(key, ref, ref, place)

        def hop(d, h):
            for way, sign in DIRS:
                if h < 4 or (way == "R") == (d == 0):
                    if h > 0:
                        net.wait(("p", d, way, h), chunk(d, sign * h))
                    if h < 3 or (h == 3 and (way == "R") == (d == 0)):
                        pass_on(("p", d, way, h + 1), chunk(d, sign * h), way)

        hop(0, 0)
        pass_on(("p", "x"), chunk(0, 0), "xp")
        yield
        hop(0, 1)
        yield
        net.wait(("p", "x"), chunk(1, 0))
        hop(1, 0)
        yield
        for d, h in ((0, 2), (1, 1), (0, 3), (1, 2), (0, 4), (1, 3), (1, 4)):
            hop(d, h)
            yield
        pass_on(("all", "sib"), pre_out.at[c], "sib")
        yield
        net.wait(("all", "sib"), pre_out.at[(c + 1) % 2])

    prefix = gather_prefix()

    def ticks(count):
        for _ in range(count):
            next(prefix, None)

    for group in gather:
        if group == [(0, 3), (1, 2)]:
            load_p.wait()
            ticks(1)
        if group == [(1, 4)]:
            ticks(1)
        experts(group)
        if group == [(0, 4), (1, 3)]:
            ticks(1)
    net.send(("hid",), hid.at[:, half], hid.at[:, half], "sib")

    start = window(e)
    toks_t[...] = buf[:, :, pl.ds(pl.multiple_of(start, 128), 384)].reshape(TOK, 384).T

    load_uk.wait()
    load_uv.wait()
    for k in range(2):
        wx[:, 128 * k : 128 * (k + 1)] = wuv[k]

    other = pl.ds(pl.multiple_of((c + 1) % 2 * HID, HID), HID)
    net.wait(("hid",), hid.at[:, other])
    net.wait(("wd",), wdt.at[:, :, other])
    keep_d.wait()
    hidt[...] = hid[...].T

    def mixed_term(dx, dz, what):
        a, b = MIX_CUTS[what]
        block = (xh + dx) % 2 * 8 + column(dz)
        return mm(wdt[block, a:b, :], hidt[...])

    def mix_cut(ref, what):
        a, b = MIX_CUTS[what]
        return ref.at[pl.ds(a, b - a)]

    off = FB * e - start
    for got in reduce_scatter("m", net, mixed_term, mix_cut, ms, mr, xs, xr):
        if not isinstance(got, tuple):
            ticks({5: 2}.get(got, 0))
            continue
        what, val = got
        a, b = MIX_CUTS[what]
        rows = toks_t[pl.ds(pl.multiple_of(off + a, 16), b - a), :].astype(F32)
        arr_s[a:b] = (val + rows).astype(BF)
        for i, place in enumerate(("next", "next sib")):
            tokens_of = pl.ds(pl.multiple_of((c + i) % 2 * 256, 256), 256)
            block = arr_s.at[pl.ds(a, b - a), tokens_of]
            net.send(("next", i, what), block, arr.at[i, pl.ds(a, b - a)], place)

    net.wait(("wq",), wqs.at[1])
    net.wait(("wk",), wks.at[1])
    squares = jnp.zeros((1, 256), F32)
    for i in range(2):
        if i == 1:
            ticks(2)
        for what in ("A", "B1", "B2"):
            net.wait(("next", i, what), mix_cut(arr.at[i], what))
        x = arr[i].astype(F32)
        squares = squares + jnp.sum(x * x, axis=0, keepdims=True)
        shift = FB * at(0, 0, i) - window(at(0, 0, i))
        scaled = (x * gcol[i, pl.ds(pl.multiple_of(shift, 32), FB), 0:1]).T.astype(BF)
        if i == 0:
            lat[:, 0:QR] = mm(scaled, wqs[0])
            lat[:, QR:LAT] = mm(scaled, wks[0])
        else:
            lat[:, 0:QR] += mm(scaled, wqs[1])
            lat[:, QR:LAT] += mm(scaled, wks[1])
    lat[:, LAT:LATW] = jnp.broadcast_to(squares, (128, 256)).T[:, 0 : LATW - LAT]

    def lat_term(dx, dz, what):
        a, b = LAT_CUTS[what]
        block = (xh + dx) % 2 * 8 + column(dz)
        return lat[pl.ds(pl.multiple_of(block * ROWS, ROWS), ROWS), a:b]

    def lat_cut(ref, what):
        return last_cut(ref, *LAT_CUTS[what])

    load_uq.wait()
    order = []

    def expand(first, rows):
        there = slice(first, first + 512)
        values = mm(rows[:, 0:KVR], wx[...]).astype(BF)
        for k in range(2):
            kx[k, 0:NOPE, there] = mm(wuk[k], rows[:, 0:KVR], NT).astype(BF)
            kx[k, NOPE:, there] = rows[:, KVR:KEY].T
            vx[k, there, :] = values[:, 128 * k : 128 * (k + 1)]

    def expand_prefix(i):
        expand(512 * i, pre_out[(c + i // 2) % 2, i % 2 * 8 : i % 2 * 8 + 8].reshape(512, KEY))

    sums = {}
    for got in scatter_far("l", net, lat_term, lat_cut, ms2, mr2, xs2, xr2):
        if isinstance(got, tuple):
            sums[got[0]] = got[1]
        elif got == 1:
            ticks(2)
        elif got == 3:
            ticks(2)
            expand_prefix(0)
        elif got == 4:
            expand_prefix(1)
        elif got == 5:
            ticks(1)
            expand_prefix(2)
            expand_prefix(3)
    total = jnp.concatenate([sums["A"], sums["B"]], axis=1)
    scale = lax.rsqrt(total[:, LAT : LAT + 1] * (1.0 / D) + EPSILON)

    def rms(v, gain):
        v = v * scale
        return (v * lax.rsqrt(jnp.mean(v * v, axis=1, keepdims=True) + EPSILON) * gain).astype(BF)

    lat_out[e, :, 0:QR] = rms(total[:, 0:QR], qg_ref[...])
    lat_out[e, :, QR : QR + KVR] = rms(total[:, QR : QR + KVR], kg_ref[...])
    tail = total[:, QR + KVR :] * scale
    first, second = tail[:, 0:32], tail[:, 32:64]
    cos, sin = trig_ref[e, :, 0:32], trig_ref[e, :, 32:64]
    turned = jnp.concatenate([first * cos - second * sin, first * sin + second * cos], axis=1)
    lat_out[e, :, QR + KVR : LAT] = turned.astype(BF)
    lat_out[e, :, LAT:LATW] = jnp.zeros((ROWS, LATW - LAT), BF)

    def lat_part(s, what):
        return last_cut(lat_out.at[s], *LAT_CUTS[what])

    def queries(group):
        slots = sib_rows("o", net, at, lat_part, group)
        m = len(slots) * ROWS
        base = len(order) * ROWS
        order.extend(slots)
        mine = slice(base, base + m)
        angle = jnp.concatenate([trig_ref[s] for s in slots], axis=0)
        cos, sin = angle[:, 0:32], angle[:, 32:64]
        q = mm(jnp.concatenate([lat_out[s, :, 0:QR] for s in slots], axis=0), wuq[...]) * SHARP
        for k in range(2):
            a = k * (NOPE + ROPE)
            first, second = q[:, a + NOPE : a + NOPE + 32], q[:, a + NOPE + 32 : a + NOPE + 64]
            turned = jnp.concatenate([first * cos - second * sin, first * sin + second * cos], axis=1)
            qs[k, mine, 0:NOPE] = q[:, a : a + NOPE].astype(BF)
            qs[k, mine, NOPE:] = turned.astype(BF)
        both = range(2)
        score = [[mm(qs[k, mine, :], kx[k, :, 512 * b : 512 * (b + 1)]) for b in range(4)] for k in both]
        top = [functools.reduce(jnp.maximum, [jnp.max(x, axis=1, keepdims=True) for x in score[k]]) for k in both]
        for k in both:
            total, mixed = 0.0, 0.0
            for b in range(4):
                p = jnp.exp2(score[k][b] - top[k])
                total = total + jnp.sum(p, axis=1, keepdims=True)
                mixed = mixed + mm(p.astype(BF), vx[k, 512 * b : 512 * (b + 1), :])
            acc_s[k, mine, :] = mixed
            max_s[k, mine, :] = jnp.broadcast_to(top[k], (m, 128))
            sum_s[k, mine, :] = jnp.broadcast_to(total, (m, 128))

    def new_keys():
        row = lax.broadcasted_iota(jnp.int32, (ROWS, 1), 0)
        when = jnp.concatenate([row + s * ROWS for s in order], axis=0)
        key_when = lax.broadcasted_iota(jnp.int32, (1, TOK), 1)
        pieces = [(k, slice(256 * i, 256 * (i + 1))) for i in range(2) for k in range(2)]
        score = [mm(qs[k, mine, :], kx[k, :, CACHE:]) for k, mine in pieces]
        score = [jnp.where(key_when <= when[mine], x, -jnp.inf) for x, (k, mine) in zip(score, pieces)]
        new = [jnp.maximum(max_s[k, mine, 0:1], jnp.max(x, axis=1, keepdims=True)) for x, (k, mine) in zip(score, pieces)]
        for (k, mine), x, top in zip(pieces, score, new):
            fade = jnp.exp2(max_s[k, mine, 0:1] - top)
            p = jnp.exp2(x - top)
            total = sum_s[k, mine, 0:1] * fade + jnp.sum(p, axis=1, keepdims=True)
            mixed = acc_s[k, mine, :] * fade + mm(p.astype(BF), vx[k, CACHE:, :])
            val = (mixed * (1.0 / total)).astype(BF)
            for j, s in enumerate(order[mine.start // ROWS : mine.stop // ROWS]):
                there = pl.ds(pl.multiple_of(s * ROWS, ROWS), ROWS)
                out_ref[there, 128 * k : 128 * (k + 1)] = val[ROWS * j : ROWS * (j + 1)]

    finish_gather = gather_far("o", net, at, lat_part)
    next(finish_gather)
    for group in finish_gather:
        queries(group)
    expand(CACHE, lat_out[:, :, QR:LAT].reshape(TOK, KEY))
    new_keys()
    for group, ref in (
        ("t", buf.at[pl.ds(0, 31)]),
        ("o", lat_out.at[pl.ds(0, 31)]),
        ("m", all_blocks),
        ("l", all_rows),
        ("p", pre_out.at[0, pl.ds(0, 15)]),
        ("all", pre_out.at[0]),
        ("next", arr_s),
        ("wq", wqs.at[0]),
        ("wk", wks.at[0]),
        ("wd", wdt.at[:, :, half]),
        ("hid", hid.at[:, half]),
    ):
        net.sent(group, ref)
    assert (len(net.ids), len(net.groups)) == (COPIES, SENDS)


SHARP = float((NOPE + ROPE) ** (-0.5) * np.log2(np.e))


def trig_table():
    half = ROPE // 2
    frequency = 10000.0 ** (-np.arange(half) / half)
    angles = (CACHE + np.arange(TOK))[:, None] * frequency[None, :].astype(np.float32)
    angles = angles.astype(np.float32).astype(np.float64)
    both = np.concatenate([np.cos(angles), np.sin(angles)], axis=1)
    return both.astype(np.float32)


def per_device(
    sections, tokens, expert_ids, gate_values, w_gate, w_up, w_down, norm_gain, w_dq, w_dkv, q_gain, kv_gain, w_uq, w_uk,
    w_uv, prefix_cache,
):
    vm = pl.BlockSpec(memory_space=pltpu.VMEM)
    anyw = pl.BlockSpec(memory_space=pl.ANY)
    V = pltpu.VMEM
    out = pl.pallas_call(
        functools.partial(relay_kernel, sections),
        name="relay",
        out_shape=jax.ShapeDtypeStruct((TOK, 256), BF),
        in_specs=[anyw, vm, vm, anyw, anyw, anyw, vm, anyw, anyw, vm, vm, vm, anyw, anyw, anyw, anyw],
        out_specs=vm,
        scratch_shapes=[
            V((32, ROWS, WIDE), BF),
            V((D, 2 * HID), BF),
            V((HID, D), BF),
            V((32, FB, HID), BF),
            V((16, FB, 2 * HID), BF),
            V((TOK, 2 * HID), BF),
            V((2 * HID, TOK), BF),
            V((384, TOK), BF),
            V((16, FB, TOK), BF),
            V((16, FB, TOK), BF),
            V((8, FB, TOK), BF),
            V((8, FB, TOK), BF),
            V((2, FB, TOK // 2), BF),
            V((FB, TOK), BF),
            V((2, FB, QR), BF),
            V((2, FB, KEY), BF),
            V((TOK // 2, LATW), F32),
            V((16, ROWS, LATW), BF),
            V((16, ROWS, LATW), BF),
            V((8, ROWS, LATW), BF),
            V((8, ROWS, LATW), BF),
            V((32, ROWS, LATW), BF),
            V((2, 16, PRE, KEY), BF),
            V((2, 384, 128), F32),
            V((QR, 384), BF),
            V((2, NOPE, KVR), BF),
            V((2, KVR, 128), BF),
            V((KVR, 256), BF),
            V((2, NOPE + ROPE, CACHE + TOK), BF),
            V((2, CACHE + TOK, 128), BF),
            V((2, TOK, NOPE + ROPE), BF),
            V((2, TOK, 128), F32),
            V((2, TOK, 128), F32),
            V((2, TOK, 128), F32),
            pltpu.SemaphoreType.DMA((SENDS,)),
            pltpu.SemaphoreType.DMA((COPIES,)),
            pltpu.SemaphoreType.DMA((11,)),
        ],
        compiler_params=pltpu.CompilerParams(collective_id=0, has_side_effects=True, vmem_limit_bytes=60 << 20),
        cost_estimate=pl.CostEstimate(flops=12 * 10**9, bytes_accessed=12 * 10**6, transcendentals=4 * 10**6),
    )(
        tokens[0], expert_ids[0].T, gate_values[0].T, w_gate[0], w_up[0], w_down[0], norm_gain, w_dq[0], w_dkv[0],
        q_gain, kv_gain, jnp.asarray(trig_table().reshape(32, ROWS, ROPE)), prefix_cache[0], w_uq[0], w_uk[0], w_uv[0],
    )
    return out[None]


def solution(mesh):
    placed = (
        P("section", "expert", None),
        P("section", "expert", None),
        P("section", "expert", None),
        P("section", None, "expert"),
        P("section", None, "expert"),
        P("section", "expert", None),
        P("section", None),
        P("section", "expert", None),
        P("section", "expert", None),
        P("section", None),
        P("section", None),
        P("section", None, "expert"),
        P("section", "expert", None, None),
        P("section", "expert", None, None),
        P("section", "expert", None),
    )
    return jax.shard_map(
        functools.partial(per_device, mesh.shape["section"]),
        mesh=mesh,
        in_specs=placed,
        out_specs=P("section", None, "expert"),
        check_vma=False,
    )
```

```python
import functools

import jax
import jax.numpy as jnp
import numpy as np
from jax import lax
from jax.experimental import pallas as pl
from jax.experimental.pallas import tpu as pltpu
from jax.sharding import PartitionSpec as P

MESH = pl.DeviceIdType.MESH
COPIES = 107
SENDS = 11
REUSED = {"o": "t", "l": "m"}
BF = jnp.bfloat16
F32 = jnp.float32
EPSILON = 1e-06
D = 7168
ROWS = 16
SIDE = 128
WIDE = D + SIDE
HID = 128
QR = 1536
KVR = 512
ROPE = 64
NOPE = 128
KEY = KVR + ROPE
LAT = QR + KEY
LATW = 2176
FB = 224
TOK = 512
CACHE = 2048
PRE = 64
KT = (((1,), (0,)), ((), ()))
NT = (((1,), (1,)), ((), ()))
TN = (((0,), (0,)), ((), ()))


def mm(a, b, dims=KT):
    return lax.dot_general(a, b, dims, preferred_element_type=F32)


class Net:
    def __init__(self, send_sems, recv_sems, places):
        self.send_sems, self.recv_sems, self.places = send_sems, recv_sems, places
        self.ids, self.groups = {}, {}

    def copy(self, key, src, dst, place, group="t"):
        same = (REUSED.get(key[0], key[0]),) + key[1:]
        index = self.ids.setdefault(same, len(self.ids))
        return pltpu.make_async_remote_copy(
            src_ref=src,
            dst_ref=dst,
            send_sem=self.send_sems.at[self.groups.setdefault(group, len(self.groups))],
            recv_sem=self.recv_sems.at[index],
            device_id=self.places[place],
            device_id_type=MESH,
        )

    def send(self, key, src, dst, place):
        self.copy(key, src, dst, place, key[0]).start()

    def wait(self, key, ref):
        self.copy(key, ref, ref, "sib").wait_recv()

    def sent(self, group, ref):
        self.copy(("t", "xA"), ref, ref, "sib", group).wait_send()


class Hops:
    def __init__(self, ref):
        self.ref, self.at = ref, self

    def __getitem__(self, index):
        first = index[0] * 8 + index[1] * 2
        return self.ref.at[first + index[2]] if len(index) == 3 else self.ref.at[pl.ds(first, 2)]


DIRS = (("R", -1), ("L", 1))


def all_gather(n, net, slot, part):
    def pass_on(key, s, what, place):
        net.send(key, part(s, what), part(s, what), place)

    me, mate = slot(0, 0, 0), slot(1, 0, 0)
    pass_on((n, "xA"), me, "A", "xp")
    for what in "BA":
        for way, _ in DIRS:
            pass_on((n, what, way, 1), me, what, way)
    pass_on((n, "xB", "", 0), me, "B", "xp")
    pass_on((n, "s0", "", 0), me, "F", "sib")
    yield []

    net.wait((n, "xA"), part(mate, "A"))
    for way, _ in DIRS:
        pass_on((n, "A1", way, 1), mate, "A", way)
    net.wait((n, "xB", "", 0), part(mate, "B"))
    pass_on((n, "s1", "", 0), mate, "F", "sib")

    def finish(h):
        if h < 4:
            for way, sign in DIRS:
                s = slot(1, sign * h, 0)
                net.wait((n, "xB", way, h), part(s, "B"))
                pass_on((n, "s1", way, h), s, "F", "sib")
        else:
            s = slot(1, 4, 0)
            net.wait((n, "xB", "R", 4), part(s, "B1"))
            net.wait((n, "xB", "L", 4), part(s, "B2"))
            pass_on((n, "s1", "R", 4), s, "F", "sib")

    def second(h):
        for way, sign in DIRS:
            if h < 4 or way == "L":
                s = slot(1, sign * h, 0)
                net.wait((n, "A1", way, h), part(s, "A"))
                if h < 3 or (h == 3 and way == "L"):
                    pass_on((n, "A1", way, h + 1), s, "A", way)

    for h in range(1, 5):
        for way, sign in DIRS:
            s = slot(0, sign * h, 0)
            half = "B1" if way == "R" else "B2"
            if h < 4:
                net.wait((n, "B", way, h), part(s, "B"))
                pass_on((n, "B", way, h + 1), s, "B" if h < 3 else half, way)
                pass_on((n, "xB", way, h), s, "B", "xp")
            else:
                net.wait((n, "B", way, 4), part(s, half))
                pass_on((n, "xB", way, 4), s, half, "xp")
        if h > 1:
            finish(h - 1)
        for way, sign in DIRS:
            if h < 4 or way == "R":
                s = slot(0, sign * h, 0)
                net.wait((n, "A", way, h), part(s, "A"))
                if h < 3 or (h == 3 and way == "R"):
                    pass_on((n, "A", way, h + 1), s, "A", way)
                pass_on((n, "s0", way, h), s, "F", "sib")
        yield [(0, h - 1)] + ([(1, h - 2)] if h > 1 else [])
        if h < 4:
            second(h)
    second(4)
    yield [(0, 4), (1, 3)]
    finish(4)
    yield [(1, 4)]


def gather_far(n, net, slot, part):
    def pass_on(key, s, what, place):
        net.send(key, part(s, what), part(s, what), place)

    def both_ways(name, h, s, what):
        for way, _ in DIRS:
            pass_on((n, name, way, h), s, what, way + "2" if h == 2 else way)

    me, mate = slot(0, 0, 0), slot(1, 0, 0)
    pass_on((n, "xA"), me, "A", "xp")
    for what in "BA":
        both_ways(what, 2, me, what)
        both_ways(what, 1, me, what)
    pass_on((n, "xB", "", 0), me, "B", "xp")
    pass_on((n, "s0", "", 0), me, "F", "sib")
    yield []
    net.wait((n, "xA"), part(mate, "A"))
    both_ways("A1", 2, mate, "A")
    both_ways("A1", 1, mate, "A")
    net.wait((n, "xB", "", 0), part(mate, "B"))
    pass_on((n, "s1", "", 0), mate, "F", "sib")

    def ring_b(h):
        for way, sign in DIRS:
            s = slot(0, sign * h, 0)
            half = "B1" if way == "R" else "B2"
            what = "B" if h < 4 else half
            net.wait((n, "B", way, h), part(s, what))
            if h == 2:
                pass_on((n, "B", way, 3), s, "B", way)
                pass_on((n, "B", way, 4), s, half, way + "2")
            pass_on((n, "xB", way, h), s, what, "xp")

    def ring_a(name, h, d):
        for way, sign in DIRS:
            last = (way == "R") == (d == 0)
            if h < 4 or last:
                s = slot(d, sign * h, 0)
                net.wait((n, name, way, h), part(s, "A"))
                if h == 2:
                    pass_on((n, name, way, 3), s, "A", way)
                    if last:
                        pass_on((n, name, way, 4), s, "A", way + "2")
                if d == 0:
                    pass_on((n, "s0", way, h), s, "F", "sib")

    def finish(h):
        if h < 4:
            for way, sign in DIRS:
                s = slot(1, sign * h, 0)
                net.wait((n, "xB", way, h), part(s, "B"))
                pass_on((n, "s1", way, h), s, "F", "sib")
        else:
            s = slot(1, 4, 0)
            net.wait((n, "xB", "R", 4), part(s, "B1"))
            net.wait((n, "xB", "L", 4), part(s, "B2"))
            pass_on((n, "s1", "R", 4), s, "F", "sib")

    ring_b(1)
    ring_b(2)
    ring_a("A", 1, 0)
    ring_a("A", 2, 0)
    yield [(0, 0)]
    ring_a("A1", 1, 1)
    ring_a("A1", 2, 1)
    finish(1)
    finish(2)
    yield [(1, 0), (0, 1), (0, 2)]
    ring_b(3)
    ring_b(4)
    ring_a("A", 3, 0)
    ring_a("A", 4, 0)
    yield [(1, 1), (1, 2)]
    yield [(0, 3), (0, 4)]
    ring_a("A1", 3, 1)
    ring_a("A1", 4, 1)
    finish(3)
    finish(4)
    yield [(1, 3), (1, 4)]


def sib_rows(n, net, slot, part, group):
    slots = []
    for dx, h in group:
        for way, sign in DIRS if 0 < h < 4 else (("" if h == 0 else "R", 1),):
            net.wait((n, f"s{dx}", way, h), part(slot(dx, sign * h, 1), "F"))
            slots += [slot(dx, sign * h, 0), slot(dx, sign * h, 1)]
    return slots


def reduce_scatter(n, net, value, cut, ms, mr, xs, xr):
    order = [4, 3, -3, 2, -2, 1, -1, 0]

    def put(key, buf, there, what, val, place):
        cut(buf, what)[...] = val.astype(BF)
        net.send(key, cut(buf, what), cut(there, what), place)

    def got(key, buf, what):
        net.wait(key, cut(buf, what))
        return cut(buf, what)[...].astype(F32)

    last = ("B1", "B2")
    trips = [(k, 1) for k in range(8)]

    def over_x(j):
        if j < len(trips):
            k, count = trips[j]
            for i in range(k, k + count):
                cut(xs.at[i], "B")[...] = value(1, order[i], "B").astype(BF)
            there = pl.ds(k, count)
            if count == 1:
                there = k
            net.send((n, "x", k), cut(xs.at[there], "B"), cut(xr.at[there], "B"), "xp")

    def from_x(i):
        for j, (k, count) in enumerate(trips):
            if k == i:
                net.wait((n, "x", k), cut(xr.at[pl.ds(k, count) if count > 1 else k], "B"))
                over_x(j + 3)

    def hop_a(h, apart=False):
        for d in (1, 0):
            for w, way in enumerate("RL"):
                if (h == 1 and w != d) or (h == 2 and (w != d) != apart):
                    continue
                val = value(d, (5 - h) * (1 if way == "R" else -1), "A")
                if h > 2 or (h == 2 and w == d):
                    val = val + got((n, "A", way, h - 1, d), mr.at[w, h - 2, d], "A")
                put((n, "A", way, h, d), ms.at[w, h - 1, d], mr.at[w, h - 1, d], "A", val, way)

    def hop_b(h):
        for w, (way, half, rest) in enumerate((("R", "B1", "B2"), ("L", "B2", "B1"))):
            dz = (5 - h) * (1 if way == "R" else -1)
            k = order.index(dz if h > 1 else 4)
            if h > 1 or w == 0:
                from_x(k)
            buf, there = ms.at[w, h - 1, 0], mr.at[w, h - 1, 0]
            if h == 1:
                val = value(0, 4, half) + cut(xr.at[k], half)[...].astype(F32)
                put((n, "B", way, 1), buf, there, half, val, way)
            elif h == 2:
                val = value(0, dz, rest) + cut(xr.at[k], rest)[...].astype(F32)
                cut(buf, rest)[...] = val.astype(BF)
                val = value(0, dz, half) + cut(xr.at[k], half)[...].astype(F32)
                val = val + got((n, "B", way, 1), mr.at[w, 0, 0], half)
                cut(buf, half)[...] = val.astype(BF)
                net.send((n, "B", way, h), cut(buf, "B"), cut(there, "B"), way)
            else:
                net.wait((n, "B", way, h - 1), cut(mr.at[w, h - 2, 0], "B"))
                for what in last if h == 4 else ("B",):
                    val = value(0, dz, what) + cut(xr.at[k], what)[...].astype(F32)
                    val = val + cut(mr.at[w, h - 2, 0], what)[...].astype(F32)
                    put((n, "B2" if what == "B2" else "B", way, h), buf, there, what, val, way)

    over_x(0)
    hop_a(1)
    hop_a(2, True)
    over_x(1)
    over_x(2)
    yield 1
    for h in range(2, 5):
        hop_a(h)
        hop_b(h - 1)
        yield h
    val = value(1, 0, "A")
    for w, way in enumerate("RL"):
        val = val + got((n, "A", way, 4, 1), mr.at[w, 3, 1], "A")
    put((n, "xA"), xs.at[7], xr.at[7], "A", val, "xp")
    hop_b(4)
    yield 5
    own = value(0, 0, "A")
    for w, way in enumerate("RL"):
        own = own + got((n, "A", way, 4, 0), mr.at[w, 3, 0], "A")
    yield "A", own + got((n, "xA"), xr.at[7], "A")
    from_x(7)
    for what in last:
        val = value(0, 0, what) + cut(xr.at[7], what)[...].astype(F32)
        for w, way in enumerate("RL"):
            val = val + got((n, "B2" if what == "B2" else "B", way, 4), mr.at[w, 3, 0], what)
        yield what, val


def scatter_far(n, net, value, cut, ms, mr, xs, xr):
    order = [4, 3, -3, 2, -2, 1, -1, 0]
    trips = [(0, 1), (1, 2), (3, 2), (5, 2), (7, 1)]

    def put(key, buf, there, what, val, place):
        cut(buf, what)[...] = val.astype(BF)
        net.send(key, cut(buf, what), cut(there, what), place)

    def got(key, buf, what):
        net.wait(key, cut(buf, what))
        return cut(buf, what)[...].astype(F32)

    def over_x(j):
        if j < len(trips):
            k, count = trips[j]
            for i in range(k, k + count):
                cut(xs.at[i], "B")[...] = value(1, order[i], "B").astype(BF)
            there = pl.ds(k, count) if count > 1 else k
            net.send((n, "x", k), cut(xs.at[there], "B"), cut(xr.at[there], "B"), "xp")

    def from_x(j):
        k, count = trips[j]
        net.wait((n, "x", k), cut(xr.at[pl.ds(k, count) if count > 1 else k], "B"))
        over_x(j + 3)

    def place(way, h):
        return way + "2" if h in (1, 3) else way

    def send_a(h):
        for d in (1, 0):
            for w, way in enumerate("RL"):
                if h == 1 and w != d:
                    continue
                val = value(d, (5 - h) * (1 if way == "R" else -1), "A")
                if h == 3:
                    val = val + got((n, "A", way, 2, d), mr.at[w, 1, d], "A")
                    if w == d:
                        val = val + got((n, "A", way, 1, d), mr.at[w, 0, d], "A")
                put((n, "A", way, h, d), ms.at[w, h - 1, d], mr.at[w, h - 1, d], "A", val, place(way, h))

    def send_b(h):
        for w, (way, half, rest) in enumerate((("R", "B1", "B2"), ("L", "B2", "B1"))):
            dz = (5 - h) * (1 if way == "R" else -1)
            k = order.index(dz if h > 1 else 4)
            buf, there = ms.at[w, h - 1, 0], mr.at[w, h - 1, 0]

            def mine(what):
                return value(0, dz, what) + cut(xr.at[k], what)[...].astype(F32)

            if h == 3:
                net.wait((n, "B", way, 2), cut(mr.at[w, 1, 0], "B"))
                val = mine(rest) + cut(mr.at[w, 1, 0], rest)[...].astype(F32)
                cut(buf, rest)[...] = val.astype(BF)
                val = mine(half) + cut(mr.at[w, 1, 0], half)[...].astype(F32)
                val = val + got((n, "B", way, 1), mr.at[w, 0, 0], half)
                cut(buf, half)[...] = val.astype(BF)
                net.send((n, "B", way, h), cut(buf, "B"), cut(there, "B"), place(way, h))
            else:
                what = half if h == 1 else "B"
                put((n, "B", way, h), buf, there, what, mine(what), place(way, h))

    over_x(0)
    send_a(1)
    send_a(2)
    over_x(1)
    over_x(2)
    yield 1
    from_x(0)
    send_b(1)
    from_x(1)
    send_b(2)
    send_a(4)
    yield 2
    send_a(3)
    yield 3
    from_x(2)
    send_b(3)
    from_x(3)
    send_b(4)
    yield 4
    val = value(1, 0, "A")
    for w, way in enumerate("RL"):
        for h in (4, 3):
            val = val + got((n, "A", way, h, 1), mr.at[w, h - 1, 1], "A")
    put((n, "xA"), xs.at[7], xr.at[7], "A", val, "xp")
    yield 5
    own = value(0, 0, "A")
    for w, way in enumerate("RL"):
        for h in (4, 3):
            own = own + got((n, "A", way, h, 0), mr.at[w, h - 1, 0], "A")
    from_x(4)
    val = value(0, 0, "B") + cut(xr.at[7], "B")[...].astype(F32)
    for w, way in enumerate("RL"):
        for h in (4, 3):
            val = val + got((n, "B", way, h), mr.at[w, h - 1, 0], "B")
    yield "B", val
    yield "A", own + got((n, "xA"), xr.at[7], "A")


def last_cut(ref, a, b):
    return ref.at[..., pl.ds(a, b - a)]


TOK_CUTS = {"A": (0, 3456), "B": (3456, WIDE), "B1": (3456, 5376), "B2": (5376, WIDE), "F": (0, WIDE)}
LAT_CUTS = {"A": (0, 1024), "B": (1024, LATW), "B1": (1024, 1664), "B2": (1664, LATW), "F": (0, LATW)}
MIX_CUTS = {"A": (0, 112), "B": (112, 224), "B1": (112, 176), "B2": (176, 224), "F": (0, 224)}


def relay_kernel(
    sections,
    tok_ref, ids_ref, gates_ref, wg_ref, wu_ref, wd_ref, gain_ref, wq_ref, wk_ref, qg_ref, kg_ref, trig_ref, pre_ref,
    wuq_ref, wuk_ref, wuv_ref,
    out_ref,
    buf, wgu, wdn, wt, wdt, hid, hidt, toks_t, ms, mr, xs, xr, arr, arr_s, wqs, wks, lat,
    ms2, mr2, xs2, xr2, lat_out, pre_out, gcol, wuq, wuk, wuv, wx, kx, vx, qs, acc_s, max_s, sum_s, send_sems, recv_sems, local_sems,
):
    sec, e = lax.axis_index("section"), lax.axis_index("expert")
    xh, z, c = e // 16, (e // 2) % 8, e % 2

    turn = 1 - 2 * c

    def column(dz, dc=0):
        return (z + turn * (-dz if dc else dz) + 8) % 8

    def at(dx, dz, dc):
        return (xh + dx) % 2 * 16 + column(dz, dc) * 2 + (c + dc) % 2

    places = {
        "R": (sec, at(0, 1, 0)),
        "L": (sec, at(0, -1, 0)),
        "R2": (sec, at(0, 2, 0)),
        "L2": (sec, at(0, -2, 0)),
        "xp": (sec, at(1, 0, 0)),
        "sib": (sec, at(0, 0, 1)),
        "next": ((sec + 1) % sections, e),
        "next sib": ((sec + 1) % sections, at(0, 0, 1)),
        "prev": ((sec + sections - 1) % sections, e),
        "prev sib": ((sec + sections - 1) % sections, at(0, 0, 1)),
    }
    net = Net(send_sems, recv_sems, places)
    all_blocks, all_rows = ms.at[pl.ds(0, 15)], ms2.at[pl.ds(0, 15)]
    ms, mr, ms2, mr2 = (Hops(r) for r in (ms, mr, ms2, mr2))
    local = []

    def fetch(k, src, dst):
        cp = pltpu.make_async_copy(src, dst, local_sems.at[k])
        cp.start()
        local.append(cp)
        return cp

    def slot(dx, dz, dc):
        return (c + dc) % 2 * 16 + (xh + dx) % 2 * 8 + column(dz, dc)

    me = slot(0, 0, 0)
    own = fetch(0, tok_ref, buf.at[me, :, pl.ds(0, D)])
    load_g = fetch(1, wg_ref, wgu.at[:, pl.ds(0, HID)])
    load_u = fetch(2, wu_ref, wgu.at[:, pl.ds(HID, HID)])
    load_d = fetch(3, wd_ref, wdn)
    load_q = fetch(4, wq_ref, wqs.at[0])
    load_k = fetch(5, wk_ref, wks.at[0])
    load_p = fetch(6, pre_ref, pre_out.at[c, xh * 8 + z])
    load_uq = fetch(8, wuq_ref, wuq)
    load_uk = fetch(9, wuk_ref, wuk)
    load_uv = fetch(10, wuv_ref, wuv)

    barrier = pltpu.get_barrier_semaphore()
    for there in places.values():
        pl.semaphore_signal(barrier, inc=1, device_id=there, device_id_type=MESH)

    lane = lax.broadcasted_iota(jnp.int32, (ROWS, SIDE), 1)
    diag = lax.broadcasted_iota(jnp.int32, (ROWS, ROWS), 0) == lax.broadcasted_iota(jnp.int32, (ROWS, ROWS), 1)
    g = jnp.zeros((ROWS, SIDE), F32)
    for k in range(2):
        chosen = jnp.sum(jnp.where(diag, ids_ref[k : k + 1, :], 0), axis=1, keepdims=True)
        weight = jnp.sum(jnp.where(diag, gates_ref[k : k + 1, :], 0.0), axis=1, keepdims=True)
        g = g + jnp.where(chosen == lane % 4, weight, 0.0)
    high = g.astype(BF)
    low = (g - high.astype(F32)).astype(BF)
    side = jnp.where(lane < 4, high.astype(F32), jnp.where(lane < 8, low.astype(F32), 0.0)).astype(BF)
    buf[me, :, D:WIDE] = side

    pl.semaphore_wait(barrier, len(places))
    own.wait()

    def tok_part(s, what):
        return last_cut(buf.at[s], *TOK_CUTS[what])

    expert = e // 8
    gather = all_gather("t", net, slot, tok_part)
    next(gather)
    load_q.wait()
    net.send(("wq",), wqs.at[0], wqs.at[1], "sib")
    load_k.wait()
    net.send(("wk",), wks.at[0], wks.at[1], "sib")

    def window(owner):
        return jnp.minimum(FB * owner // 128 * 128, D - 384)

    for i in range(2):
        first = window(at(0, 0, i))
        piece = gain_ref[0:1, pl.ds(pl.multiple_of(first, 128), 384)]
        gcol[i] = jnp.broadcast_to(piece, (128, 384)).T
    load_d.wait()
    for k in range(8):
        wt[4 * k : 4 * k + 4] = wdn[:, 896 * k : 896 * (k + 1)].T.reshape(4, FB, HID)

    half = pl.ds(pl.multiple_of(c * HID, HID), HID)
    pairs = wt.reshape(16, 2, FB, HID)
    net.send(("wd",), pairs.at[:, (c + 1) % 2], wdt.at[:, :, half], "sib")
    keep_d = fetch(7, pairs.at[:, c], wdt.at[:, :, half])

    load_g.wait()
    load_u.wait()

    def experts(group):
        slots = sib_rows("t", net, slot, tok_part, group)
        m = len(slots) * ROWS
        acc = jnp.zeros((m, 2 * HID), F32)
        for k in range(7):
            rows = jnp.concatenate([buf[s, :, 1024 * k : 1024 * (k + 1)] for s in slots], axis=0)
            acc = acc + mm(rows, wgu[1024 * k : 1024 * (k + 1), :])
        side = jnp.concatenate([buf[s, :, D:WIDE] for s in slots], axis=0).astype(F32)
        lane = lax.broadcasted_iota(jnp.int32, (m, SIDE), 1)
        gate = jnp.sum(jnp.where((lane % 4 == expert) & (lane < 8), side, 0.0), axis=1, keepdims=True)
        gp, up = acc[:, :HID], acc[:, HID:]
        val = (gp / (1.0 + jnp.exp(-gp)) * up * gate).astype(BF)
        for i, s in enumerate(slots):
            hid[pl.ds(pl.multiple_of(s * ROWS, ROWS), ROWS), half] = val[ROWS * i : ROWS * (i + 1)]

    def gather_prefix():
        def chunk(dx, dz):
            return pre_out.at[c, (xh + dx) % 2 * 8 + column(dz)]

        def pass_on(key, ref, place):
            net.send(key, ref, ref, place)

        def hop(d, h):
            for way, sign in DIRS:
                if h < 4 or (way == "R") == (d == 0):
                    if h > 0:
                        net.wait(("p", d, way, h), chunk(d, sign * h))
                    if h < 3 or (h == 3 and (way == "R") == (d == 0)):
                        pass_on(("p", d, way, h + 1), chunk(d, sign * h), way)

        hop(0, 0)
        pass_on(("p", "x"), chunk(0, 0), "xp")
        yield
        hop(0, 1)
        yield
        net.wait(("p", "x"), chunk(1, 0))
        hop(1, 0)
        yield
        for d, h in ((0, 2), (1, 1), (0, 3), (1, 2), (0, 4), (1, 3), (1, 4)):
            hop(d, h)
            yield
        pass_on(("all", "sib"), pre_out.at[c], "sib")
        yield
        net.wait(("all", "sib"), pre_out.at[(c + 1) % 2])

    prefix = gather_prefix()

    def ticks(count):
        for _ in range(count):
            next(prefix, None)

    for group in gather:
        if group == [(0, 3), (1, 2)]:
            load_p.wait()
            ticks(1)
        if group == [(1, 4)]:
            ticks(1)
        experts(group)
        if group == [(0, 4), (1, 3)]:
            ticks(1)
    net.send(("hid",), hid.at[:, half], hid.at[:, half], "sib")

    start = window(e)
    toks_t[...] = buf[:, :, pl.ds(pl.multiple_of(start, 128), 384)].reshape(TOK, 384).T

    load_uk.wait()
    load_uv.wait()
    for k in range(2):
        wx[:, 128 * k : 128 * (k + 1)] = wuv[k]

    other = pl.ds(pl.multiple_of((c + 1) % 2 * HID, HID), HID)
    net.wait(("hid",), hid.at[:, other])
    net.wait(("wd",), wdt.at[:, :, other])
    keep_d.wait()
    hidt[...] = hid[...].T

    def mixed_term(dx, dz, what):
        a, b = MIX_CUTS[what]
        block = (xh + dx) % 2 * 8 + column(dz)
        return mm(wdt[block, a:b, :], hidt[...])

    def mix_cut(ref, what):
        a, b = MIX_CUTS[what]
        return ref.at[pl.ds(a, b - a)]

    off = FB * e - start
    for got in reduce_scatter("m", net, mixed_term, mix_cut, ms, mr, xs, xr):
        if not isinstance(got, tuple):
            ticks({5: 2}.get(got, 0))
            continue
        what, val = got
        a, b = MIX_CUTS[what]
        rows = toks_t[pl.ds(pl.multiple_of(off + a, 16), b - a), :].astype(F32)
        arr_s[a:b] = (val + rows).astype(BF)
        for i, place in enumerate(("next", "next sib")):
            tokens_of = pl.ds(pl.multiple_of((c + i) % 2 * 256, 256), 256)
            block = arr_s.at[pl.ds(a, b - a), tokens_of]
            net.send(("next", i, what), block, arr.at[i, pl.ds(a, b - a)], place)

    net.wait(("wq",), wqs.at[1])
    net.wait(("wk",), wks.at[1])
    squares = jnp.zeros((1, 256), F32)
    for i in range(2):
        if i == 1:
            ticks(2)
        for what in ("A", "B1", "B2"):
            net.wait(("next", i, what), mix_cut(arr.at[i], what))
        x = arr[i].astype(F32)
        squares = squares + jnp.sum(x * x, axis=0, keepdims=True)
        shift = FB * at(0, 0, i) - window(at(0, 0, i))
        scaled = (x * gcol[i, pl.ds(pl.multiple_of(shift, 32), FB), 0:1]).T.astype(BF)
        if i == 0:
            lat[:, 0:QR] = mm(scaled, wqs[0])
            lat[:, QR:LAT] = mm(scaled, wks[0])
        else:
            lat[:, 0:QR] += mm(scaled, wqs[1])
            lat[:, QR:LAT] += mm(scaled, wks[1])
    lat[:, LAT:LATW] = jnp.broadcast_to(squares, (128, 256)).T[:, 0 : LATW - LAT]

    def lat_term(dx, dz, what):
        a, b = LAT_CUTS[what]
        block = (xh + dx) % 2 * 8 + column(dz)
        return lat[pl.ds(pl.multiple_of(block * ROWS, ROWS), ROWS), a:b]

    def lat_cut(ref, what):
        return last_cut(ref, *LAT_CUTS[what])

    load_uq.wait()
    order = []

    def expand(first, rows):
        there = slice(first, first + 512)
        values = mm(rows[:, 0:KVR], wx[...]).astype(BF)
        for k in range(2):
            kx[k, 0:NOPE, there] = mm(wuk[k], rows[:, 0:KVR], NT).astype(BF)
            kx[k, NOPE:, there] = rows[:, KVR:KEY].T
            vx[k, there, :] = values[:, 128 * k : 128 * (k + 1)]

    def expand_prefix(i):
        expand(512 * i, pre_out[(c + i // 2) % 2, i % 2 * 8 : i % 2 * 8 + 8].reshape(512, KEY))

    sums = {}
    for got in scatter_far("l", net, lat_term, lat_cut, ms2, mr2, xs2, xr2):
        if isinstance(got, tuple):
            sums[got[0]] = got[1]
        elif got == 1:
            ticks(2)
        elif got == 3:
            ticks(2)
            expand_prefix(0)
        elif got == 4:
            expand_prefix(1)
        elif got == 5:
            ticks(1)
            expand_prefix(2)
            expand_prefix(3)
    total = jnp.concatenate([sums["A"], sums["B"]], axis=1)
    scale = lax.rsqrt(total[:, LAT : LAT + 1] * (1.0 / D) + EPSILON)

    def rms(v, gain):
        v = v * scale
        return (v * lax.rsqrt(jnp.mean(v * v, axis=1, keepdims=True) + EPSILON) * gain).astype(BF)

    lat_out[e, :, 0:QR] = rms(total[:, 0:QR], qg_ref[...])
    lat_out[e, :, QR : QR + KVR] = rms(total[:, QR : QR + KVR], kg_ref[...])
    tail = total[:, QR + KVR :] * scale
    first, second = tail[:, 0:32], tail[:, 32:64]
    cos, sin = trig_ref[e, :, 0:32], trig_ref[e, :, 32:64]
    turned = jnp.concatenate([first * cos - second * sin, first * sin + second * cos], axis=1)
    lat_out[e, :, QR + KVR : LAT] = turned.astype(BF)
    lat_out[e, :, LAT:LATW] = jnp.zeros((ROWS, LATW - LAT), BF)

    def lat_part(s, what):
        return last_cut(lat_out.at[s], *LAT_CUTS[what])

    def queries(group):
        slots = sib_rows("o", net, at, lat_part, group)
        m = len(slots) * ROWS
        base = len(order) * ROWS
        order.extend(slots)
        mine = slice(base, base + m)
        angle = jnp.concatenate([trig_ref[s] for s in slots], axis=0)
        cos, sin = angle[:, 0:32], angle[:, 32:64]
        q = mm(jnp.concatenate([lat_out[s, :, 0:QR] for s in slots], axis=0), wuq[...]) * SHARP
        for k in range(2):
            a = k * (NOPE + ROPE)
            first, second = q[:, a + NOPE : a + NOPE + 32], q[:, a + NOPE + 32 : a + NOPE + 64]
            turned = jnp.concatenate([first * cos - second * sin, first * sin + second * cos], axis=1)
            qs[k, mine, 0:NOPE] = q[:, a : a + NOPE].astype(BF)
            qs[k, mine, NOPE:] = turned.astype(BF)
        both = range(2)
        score = [[mm(qs[k, mine, :], kx[k, :, 512 * b : 512 * (b + 1)]) for b in range(4)] for k in both]
        top = [functools.reduce(jnp.maximum, [jnp.max(x, axis=1, keepdims=True) for x in score[k]]) for k in both]
        for k in both:
            total, mixed = 0.0, 0.0
            for b in range(4):
                p = jnp.exp2(score[k][b] - top[k])
                total = total + jnp.sum(p, axis=1, keepdims=True)
                mixed = mixed + mm(p.astype(BF), vx[k, 512 * b : 512 * (b + 1), :])
            acc_s[k, mine, :] = mixed
            max_s[k, mine, :] = jnp.broadcast_to(top[k], (m, 128))
            sum_s[k, mine, :] = jnp.broadcast_to(total, (m, 128))

    def new_keys():
        row = lax.broadcasted_iota(jnp.int32, (ROWS, 1), 0)
        when = jnp.concatenate([row + s * ROWS for s in order], axis=0)
        key_when = lax.broadcasted_iota(jnp.int32, (1, TOK), 1)
        pieces = [(k, slice(256 * i, 256 * (i + 1))) for i in range(2) for k in range(2)]
        score = [mm(qs[k, mine, :], kx[k, :, CACHE:]) for k, mine in pieces]
        score = [jnp.where(key_when <= when[mine], x, -jnp.inf) for x, (k, mine) in zip(score, pieces)]
        new = [jnp.maximum(max_s[k, mine, 0:1], jnp.max(x, axis=1, keepdims=True)) for x, (k, mine) in zip(score, pieces)]
        for (k, mine), x, top in zip(pieces, score, new):
            fade = jnp.exp2(max_s[k, mine, 0:1] - top)
            p = jnp.exp2(x - top)
            total = sum_s[k, mine, 0:1] * fade + jnp.sum(p, axis=1, keepdims=True)
            mixed = acc_s[k, mine, :] * fade + mm(p.astype(BF), vx[k, CACHE:, :])
            val = (mixed * (1.0 / total)).astype(BF)
            for j, s in enumerate(order[mine.start // ROWS : mine.stop // ROWS]):
                there = pl.ds(pl.multiple_of(s * ROWS, ROWS), ROWS)
                out_ref[there, 128 * k : 128 * (k + 1)] = val[ROWS * j : ROWS * (j + 1)]

    finish_gather = gather_far("o", net, at, lat_part)
    next(finish_gather)
    for group in finish_gather:
        queries(group)
    expand(CACHE, lat_out[:, :, QR:LAT].reshape(TOK, KEY))
    new_keys()
    for group, ref in (
        ("t", buf.at[pl.ds(0, 31)]),
        ("o", lat_out.at[pl.ds(0, 31)]),
        ("m", all_blocks),
        ("l", all_rows),
        ("p", pre_out.at[0, pl.ds(0, 15)]),
        ("all", pre_out.at[0]),
        ("next", arr_s),
        ("wq", wqs.at[0]),
        ("wk", wks.at[0]),
        ("wd", wdt.at[:, :, half]),
        ("hid", hid.at[:, half]),
    ):
        net.sent(group, ref)
    assert (len(net.ids), len(net.groups)) == (COPIES, SENDS)


SHARP = float((NOPE + ROPE) ** (-0.5) * np.log2(np.e))


def trig_table():
    half = ROPE // 2
    frequency = 10000.0 ** (-np.arange(half) / half)
    angles = (CACHE + np.arange(TOK))[:, None] * frequency[None, :].astype(np.float32)
    angles = angles.astype(np.float32).astype(np.float64)
    both = np.concatenate([np.cos(angles), np.sin(angles)], axis=1)
    return both.astype(np.float32)


def per_device(
    sections, tokens, expert_ids, gate_values, w_gate, w_up, w_down, norm_gain, w_dq, w_dkv, q_gain, kv_gain, w_uq, w_uk,
    w_uv, prefix_cache,
):
    vm = pl.BlockSpec(memory_space=pltpu.VMEM)
    anyw = pl.BlockSpec(memory_space=pl.ANY)
    V = pltpu.VMEM
    out = pl.pallas_call(
        functools.partial(relay_kernel, sections),
        name="relay",
        out_shape=jax.ShapeDtypeStruct((TOK, 256), BF),
        in_specs=[anyw, vm, vm, anyw, anyw, anyw, vm, anyw, anyw, vm, vm, vm, anyw, anyw, anyw, anyw],
        out_specs=vm,
        scratch_shapes=[
            V((32, ROWS, WIDE), BF),
            V((D, 2 * HID), BF),
            V((HID, D), BF),
            V((32, FB, HID), BF),
            V((16, FB, 2 * HID), BF),
            V((TOK, 2 * HID), BF),
            V((2 * HID, TOK), BF),
            V((384, TOK), BF),
            V((16, FB, TOK), BF),
            V((16, FB, TOK), BF),
            V((8, FB, TOK), BF),
            V((8, FB, TOK), BF),
            V((2, FB, TOK // 2), BF),
            V((FB, TOK), BF),
            V((2, FB, QR), BF),
            V((2, FB, KEY), BF),
            V((TOK // 2, LATW), F32),
            V((16, ROWS, LATW), BF),
            V((16, ROWS, LATW), BF),
            V((8, ROWS, LATW), BF),
            V((8, ROWS, LATW), BF),
            V((32, ROWS, LATW), BF),
            V((2, 16, PRE, KEY), BF),
            V((2, 384, 128), F32),
            V((QR, 384), BF),
            V((2, NOPE, KVR), BF),
            V((2, KVR, 128), BF),
            V((KVR, 256), BF),
            V((2, NOPE + ROPE, CACHE + TOK), BF),
            V((2, CACHE + TOK, 128), BF),
            V((2, TOK, NOPE + ROPE), BF),
            V((2, TOK, 128), F32),
            V((2, TOK, 128), F32),
            V((2, TOK, 128), F32),
            pltpu.SemaphoreType.DMA((SENDS,)),
            pltpu.SemaphoreType.DMA((COPIES,)),
            pltpu.SemaphoreType.DMA((11,)),
        ],
        compiler_params=pltpu.CompilerParams(collective_id=0, has_side_effects=True, vmem_limit_bytes=60 << 20),
        cost_estimate=pl.CostEstimate(flops=12 * 10**9, bytes_accessed=12 * 10**6, transcendentals=4 * 10**6),
    )(
        tokens[0], expert_ids[0].T, gate_values[0].T, w_gate[0], w_up[0], w_down[0], norm_gain, w_dq[0], w_dkv[0],
        q_gain, kv_gain, jnp.asarray(trig_table().reshape(32, ROWS, ROPE)), prefix_cache[0], w_uq[0], w_uk[0], w_uv[0],
    )
    return out[None]


def solution(mesh):
    placed = (
        P("section", "expert", None),
        P("section", "expert", None),
        P("section", "expert", None),
        P("section", None, "expert"),
        P("section", None, "expert"),
        P("section", "expert", None),
        P("section", None),
        P("section", "expert", None),
        P("section", "expert", None),
        P("section", None),
        P("section", None),
        P("section", None, "expert"),
        P("section", "expert", None, None),
        P("section", "expert", None, None),
        P("section", "expert", None),
    )
    return jax.shard_map(
        functools.partial(per_device, mesh.shape["section"]),
        mesh=mesh,
        in_specs=placed,
        out_specs=P("section", None, "expert"),
        check_vma=False,
    )
```
